32 devices in a mesh: dp: 16 (over z, x, core), tensor: 2 (over y).
Axes of the slice: x: 2, y: 2, z: 4, core: 2. Of those that a mesh axis runs over, the one named last changes fastest.
Arguments:
- hidden_in: bfloat16 [16384, 1024], P('dp'), may hold values from -6 to 6
- cotangent: bfloat16 [16384, 1024], P('dp'), may hold values from -6 to 6
- qkv_weight: float32 [2, 1024, 3, 1024], P(None, 'dp', None, 'tensor'), may hold values from -0.1875 to 0.1875
- out_weight: float32 [2, 1024, 1024], P(None, 'tensor', 'dp'), may hold values from -1 to 1
- in_weight: float32 [2, 1024, 2, 2624], P(None, 'dp', None, 'tensor'), may hold values from -0.1875 to 0.1875
- down_weight: float32 [2, 2624, 1024], P(None, 'tensor', 'dp'), may hold values from -0.125 to 0.125
- norm_gains: float32 [2, 2, 1024], P(None, None, 'dp'), may hold values from 0.5 to 1.5
- qkv_moment_in: float32 [2, 1024, 3, 1024], P(None, 'dp', None, 'tensor'), may hold values from -40 to 40
- qkv_square_in: float32 [2, 1024, 3, 1024], P(None, 'dp', None, 'tensor'), may hold values from 81.92 to 327.68
- out_moment_in: float32 [2, 1024, 1024], P(None, 'tensor', 'dp'), may hold values from -8 to 8
- out_square_in: float32 [2, 1024, 1024], P(None, 'tensor', 'dp'), may hold values from 3.2768 to 13.1072
- in_moment_in: float32 [2, 1024, 2, 2624], P(None, 'dp', None, 'tensor'), may hold values from -32 to 32
- in_square_in: float32 [2, 1024, 2, 2624], P(None, 'dp', None, 'tensor'), may hold values from 54.0672 to 212.992
- down_moment_in: float32 [2, 2624, 1024], P(None, 'tensor', 'dp'), may hold values from -48 to 48
- down_square_in: float32 [2, 2624, 1024], P(None, 'tensor', 'dp'), may hold values from 119.6032 to 475.136
- gain_moment_in: float32 [2, 2, 1024], P(None, None, 'dp'), may hold values from -80 to 80
- gain_square_in: float32 [2, 2, 1024], P(None, None, 'dp'), may hold values from 327.68 to 1310.72
Outputs:
- hidden_out: bfloat16 [16384, 1024], P('dp')
- grad_in: float32 [16384, 1024], P('dp')
- qkv_moment: float32 [2, 1024, 3, 1024], P(None, 'dp', None, 'tensor')
- qkv_square: float32 [2, 1024, 3, 1024], P(None, 'dp', None, 'tensor')
- qkv_updated: float32 [2, 1024, 3, 1024], P(None, 'dp', None, 'tensor')
- out_moment: float32 [2, 1024, 1024], P(None, 'tensor', 'dp')
- out_square: float32 [2, 1024, 1024], P(None, 'tensor', 'dp')
- out_updated: float32 [2, 1024, 1024], P(None, 'tensor', 'dp')
- in_moment: float32 [2, 1024, 2, 2624], P(None, 'dp', None, 'tensor')
- in_square: float32 [2, 1024, 2, 2624], P(None, 'dp', None, 'tensor')
- in_updated: float32 [2, 1024, 2, 2624], P(None, 'dp', None, 'tensor')
- down_moment: float32 [2, 2624, 1024], P(None, 'tensor', 'dp')
- down_square: float32 [2, 2624, 1024], P(None, 'tensor', 'dp')
- down_updated: float32 [2, 2624, 1024], P(None, 'tensor', 'dp')
- gain_moment: float32 [2, 2, 1024], P(None, None, 'dp')
- gain_square: float32 [2, 2, 1024], P(None, None, 'dp')
- gain_updated: float32 [2, 2, 1024], P(None, None, 'dp')
The draws below stay inside these ranges and needn't reach their ends.
All inputs are finite; a program needn't handle non-finite values.
Results may differ from the reference program's by a relative error of at most 0.034.
Values may be sent and summed in bfloat16 or wider, within the bound.
No kernel may reach another device: no remote copies, remote signals or barrier semaphores. Data moves between devices by JAX's collectives and lax.ppermute only.
A program may use at most 320 MiB of HBM per device.

```python
import math
import jax
import jax.numpy as jnp
from jax import lax

D = 1024
HEADS = 16
HEAD_DIM = 64
FF = 2624
HALF_WIN = 64
LAYERS = 2
STEP = 10
SEQ_LEN = 1024
TOKENS = 16384


def shard_levels(key, extent, cuts, least, largest):
    level, own = 1.0, jax.random.fold_in(key, 6)
    for dim, parts in cuts:
        draws = jnp.exp(jax.random.uniform(jax.random.fold_in(own, dim), (parts,), jnp.float32, least / len(cuts), largest / len(cuts)))
        level = level * jnp.repeat(draws, extent[dim] // parts).reshape([-1 if axis == dim else 1 for axis in range(len(extent))])
    return level


def gaussian(own_key, extent, scale, reach, cuts=(), kind=jnp.bfloat16):
    drawn = scale * jax.random.normal(own_key, extent, jnp.float32)
    if cuts:
        drawn = drawn * shard_levels(own_key, extent, cuts, -0.22, 0.18)
    return jnp.clip(drawn, -reach, reach).astype(kind)


def setup_inputs(seed: int = 0) -> dict:
    streams_of = jax.random.split(jax.random.key(seed), 18)
    hidden_in = gaussian(streams_of[0], (TOKENS, D), 1.0, 6.0, ((0, 16),))
    cotangent = gaussian(streams_of[1], (TOKENS, D), 1.0, 6.0, ((0, 16),))
    qkv_weight = gaussian(streams_of[2], (LAYERS, D, 3, D), D ** -0.5, 0.1875, ((1, 16), (3, 2)), jnp.float32)
    out_weight = gaussian(streams_of[3], (LAYERS, D, D), (D // 32) ** -0.5, 1.0, ((1, 2), (2, 16)), jnp.float32)
    in_weight = gaussian(streams_of[4], (LAYERS, D, 2, FF), D ** -0.5, 0.1875, ((1, 16), (3, 2)), jnp.float32)
    down_weight = gaussian(streams_of[5], (LAYERS, FF, D), FF ** -0.5, 0.125, ((1, 2), (2, 16)), jnp.float32)
    norm_gains = jnp.clip(1.0 + 0.1 * jax.random.normal(streams_of[6], (LAYERS, 2, D), jnp.float32), 0.5, 1.5)
    qkv_moment_in = gaussian(streams_of[7], (LAYERS, D, 3, D), (0.76 * (TOKENS / (HALF_WIN + SEQ_LEN // 8)) ** 0.5), 40.0, ((1, 16), (3, 2)), jnp.float32)
    qkv_square_in = jnp.clip(jnp.exp(math.log(327.68) - 1.3862944 * jax.random.uniform(streams_of[8], (LAYERS, D, 3, D), jnp.float32) ** shard_levels(streams_of[8], (LAYERS, D, 3, D), ((1, 16), (3, 2)), -0.2, 0.2)), 81.92, 327.68)
    out_moment_in = gaussian(streams_of[9], (LAYERS, D, D), (0.152 * (TOKENS / (HALF_WIN + SEQ_LEN // 8)) ** 0.5), 8.0, ((1, 2), (2, 16)), jnp.float32)
    out_square_in = jnp.clip(jnp.exp(math.log(13.1072) - 1.3862944 * jax.random.uniform(streams_of[10], (LAYERS, D, D), jnp.float32) ** shard_levels(streams_of[10], (LAYERS, D, D), ((1, 2), (2, 16)), -0.2, 0.2)), 3.2768, 13.1072)
    in_moment_in = gaussian(streams_of[11], (LAYERS, D, 2, FF), (0.044 * TOKENS ** 0.5), 32.0, ((1, 16), (3, 2)), jnp.float32)
    in_square_in = jnp.clip(jnp.exp(math.log(212.992) - 1.3710269 * jax.random.uniform(streams_of[12], (LAYERS, D, 2, FF), jnp.float32) ** shard_levels(streams_of[12], (LAYERS, D, 2, FF), ((1, 16), (3, 2)), -0.2, 0.2)), 54.0672, 212.992)
    down_moment_in = gaussian(streams_of[13], (LAYERS, FF, D), (0.067 * TOKENS ** 0.5), 48.0, ((1, 2), (2, 16)), jnp.float32)
    down_square_in = jnp.clip(jnp.exp(math.log(475.136) - 1.37942143 * jax.random.uniform(streams_of[14], (LAYERS, FF, D), jnp.float32) ** shard_levels(streams_of[14], (LAYERS, FF, D), ((1, 2), (2, 16)), -0.2, 0.2)), 119.6032, 475.136)
    gain_moment_in = gaussian(streams_of[15], (LAYERS, 2, D), (0.11 * TOKENS ** 0.5), 80.0, ((2, 16),), jnp.float32)
    gain_square_in = jnp.clip(jnp.exp(math.log(1310.72) - 1.3862944 * jax.random.uniform(streams_of[16], (LAYERS, 2, D), jnp.float32) ** shard_levels(streams_of[16], (LAYERS, 2, D), ((2, 16),), -0.2, 0.2)), 327.68, 1310.72)
    return dict(hidden_in=hidden_in, cotangent=cotangent, qkv_weight=qkv_weight, out_weight=out_weight, in_weight=in_weight, down_weight=down_weight, norm_gains=norm_gains, qkv_moment_in=qkv_moment_in, qkv_square_in=qkv_square_in, out_moment_in=out_moment_in, out_square_in=out_square_in, in_moment_in=in_moment_in, in_square_in=in_square_in, down_moment_in=down_moment_in, down_square_in=down_square_in, gain_moment_in=gain_moment_in, gain_square_in=gain_square_in)


norm_eps = 1e-05
theta_local = 10000.0
theta_global = 160000.0
masked_score = -1e+30
beta_one = 0.9
beta_two = 0.98
adam_eps = 1e-06
weight_decay = 1e-05
rate_qkv = 0.03
rate_out = 0.15
rate_inp = 0.03
rate_down = 0.02
rate_gain = 0.5
highest = lax.Precision.HIGHEST

@jax.custom_vjp
def low(v):
    return lax.optimization_barrier(v.astype(jnp.bfloat16)).astype(jnp.float32)

@jax.custom_vjp
def low_back(v):
    return v

def low_keep(v):
    return (low(v), None)

def low_pass(kept, grad):
    return (grad,)

def back_keep(v):
    return (v, None)

def back_low(kept, grad):
    return (low(grad),)
low.defvjp(low_keep, low_pass)
low_back.defvjp(back_keep, back_low)

def layer_norm(values, gain):
    centred = values - lax.optimization_barrier(jnp.mean(values, axis=-1, keepdims=True))
    spread = lax.optimization_barrier(jnp.mean(centred * centred, axis=-1, keepdims=True))
    return centred * lax.rsqrt(spread + norm_eps) * gain

def rotary_tables(positions, rotary_base):
    inverse = rotary_base ** (-jnp.arange(0, HEAD_DIM, 2, dtype=jnp.float32) / HEAD_DIM)
    angles = positions.astype(jnp.float32)[:, None] * inverse[None, :]
    cosine = jnp.concatenate([jnp.cos(angles), jnp.cos(angles)], axis=-1)[:, None, :]
    sine_table = jnp.concatenate([jnp.sin(angles), jnp.sin(angles)], axis=-1)[:, None, :]
    return (cosine, sine_table)

def rotate(values, cosine, sine_table):
    half_dim = values.shape[-1] // 2
    turned = jnp.concatenate([-values[..., half_dim:], values[..., :half_dim]], axis=-1)
    return values * cosine + turned * sine_table

def gelu_gate(inner, gate_part):
    return jax.nn.gelu(inner, approximate=False) * gate_part

def one_layer(values, w_qkv, w_out, w_inp, w_down, gain_pair, is_local):
    length = values.shape[0]
    positions = jnp.arange(length, dtype=jnp.int32)
    cosine, sine_table = rotary_tables(positions, theta_local if is_local else theta_global)
    normed = layer_norm(values, low(gain_pair[0]))
    lowered = low(normed)
    projected = jnp.einsum('td,dcn->tcn', lowered, low(w_qkv), precision=highest)
    queries = low(rotate(low_back(projected[:, 0]).reshape(length, HEADS, HEAD_DIM), cosine, sine_table))
    key_heads = low(rotate(low_back(projected[:, 1]).reshape(length, HEADS, HEAD_DIM), cosine, sine_table))
    value_heads = low(low_back(projected[:, 2])).reshape(length, HEADS, HEAD_DIM)
    scores = low_back(jnp.einsum('thd,shd->hts', queries, key_heads, precision=highest) * 0.125)
    if is_local:
        allowed = jnp.abs(positions[:, None] - positions[None, :]) <= HALF_WIN
        scores = jnp.where(allowed[None], scores, masked_score)
    row_max = lax.optimization_barrier(jnp.max(scores, axis=-1, keepdims=True))
    exponent = jnp.exp(scores - row_max)
    probability = exponent / lax.optimization_barrier(jnp.sum(exponent, axis=-1, keepdims=True))
    attended = jnp.einsum('hts,shd->thd', low(probability), value_heads, precision=highest).reshape(length, D)
    attended = low(low_back(attended))
    middle = values + low_back(jnp.dot(attended, low(w_out), precision=highest))
    lowered_two = low(layer_norm(middle, low(gain_pair[1])))
    hidden = low_back(jnp.einsum('td,dcf->tcf', lowered_two, low(w_inp), precision=highest))
    activated = low(gelu_gate(hidden[:, 0], hidden[:, 1]))
    return middle + low_back(jnp.dot(activated, low(w_down), precision=highest))

def adam_update(weight, moment, square, gradient, step_rate, decay_here):
    moment_new = beta_one * moment + (1.0 - beta_one) * gradient
    square_new = beta_two * square + (1.0 - beta_two) * gradient * gradient
    moment_hat = moment_new / (1.0 - beta_one ** STEP)
    square_hat = square_new / (1.0 - beta_two ** STEP)
    updated = weight - step_rate * (moment_hat / (jnp.sqrt(square_hat) + adam_eps) + decay_here * weight)
    return (moment_new, square_new, updated)

def reference(hidden_in, cotangent, qkv_weight, out_weight, in_weight, down_weight, norm_gains, qkv_moment_in, qkv_square_in, out_moment_in, out_square_in, in_moment_in, in_square_in, down_moment_in, down_square_in, gain_moment_in, gain_square_in):
    sequences = TOKENS // SEQ_LEN
    inputs = hidden_in.astype(jnp.float32).reshape(sequences, SEQ_LEN, D)
    cotangents = cotangent.astype(jnp.float32).reshape(sequences, SEQ_LEN, D)
    masters = (qkv_weight, out_weight, in_weight, down_weight, norm_gains)

    def forward(values, params):
        w_qkv, w_out, w_inp, w_down, gain_all = params
        middle = one_layer(values, w_qkv[0], w_out[0], w_inp[0], w_down[0], gain_all[0], True)
        return one_layer(middle, w_qkv[1], w_out[1], w_inp[1], w_down[1], gain_all[1], False)

    def per_sequence(running, pieces):
        values, upstream = pieces
        result, pullback = jax.vjp(forward, values, masters)
        d_values, d_params = pullback(upstream)
        return (jax.tree.map(jnp.add, running, d_params), (result, d_values))
    zero_grads = jax.tree.map(jnp.zeros_like, masters)
    gradients, (results, d_inputs) = lax.scan(per_sequence, zero_grads, (inputs, cotangents))
    g_qkv, g_out, g_inp, g_down, g_gain = gradients
    qkv_m, qkv_s, qkv_w = adam_update(qkv_weight, qkv_moment_in, qkv_square_in, g_qkv, rate_qkv, weight_decay)
    out_m, out_s, out_w = adam_update(out_weight, out_moment_in, out_square_in, g_out, rate_out, weight_decay)
    inp_m, inp_s, inp_w = adam_update(in_weight, in_moment_in, in_square_in, g_inp, rate_inp, weight_decay)
    down_m, down_s, down_w = adam_update(down_weight, down_moment_in, down_square_in, g_down, rate_down, weight_decay)
    gain_m, gain_s, gain_w = adam_update(norm_gains, gain_moment_in, gain_square_in, g_gain, rate_gain, 0.0)
    hidden_out = results.reshape(TOKENS, D).astype(jnp.bfloat16)
    grad_in = d_inputs.reshape(TOKENS, D)
    return (hidden_out, grad_in, qkv_m, qkv_s, qkv_w, out_m, out_s, out_w, inp_m, inp_s, inp_w, down_m, down_s, down_w, gain_m, gain_s, gain_w)
```

```python
import jax
import jax.numpy as jnp
from jax import lax
from jax.sharding import Mesh, PartitionSpec as P

HEAD_DIM = 64
HALF_WIN = 64
STEP = 10
SEQ_LEN = 1024


norm_eps = 1e-05
theta_local = 10000.0
theta_global = 160000.0
masked_score = -1e30
beta_one = 0.9
beta_two = 0.98
adam_eps = 1e-06
weight_decay = 1e-05
rate_qkv = 0.03
rate_out = 0.15
rate_inp = 0.03
rate_down = 0.02
rate_gain = 0.5

every_axis = ("chip", "core", "tensor")
chip_axes = ("chip", "tensor")


def swap_pairs(chips):
    pairs = []
    for chip in range(chips):
        for core in range(2):
            for row in range(2):
                pairs.append((chip * 4 + core * 2 + row, chip * 4 + row * 2 + core))
    return pairs


def result_pairs(chips):
    return [(chip * 4 + c * 3, chip * 4 + c * 2 + 1 - c) for chip in range(chips) for c in range(2)]


def role_swap(values, chips):
    return lax.ppermute(values, every_axis, swap_pairs(chips))


def core_swap(values):
    return lax.ppermute(values, "core", [(0, 1), (1, 0)])


def core_total(partial_sum):
    own = partial_sum.astype(jnp.bfloat16)
    return own.astype(jnp.float32) + core_swap(own).astype(jnp.float32)


def layer_norm(values, gain):
    centred = values - jnp.mean(values, axis=-1, keepdims=True)
    spread = jnp.mean(centred * centred, axis=-1, keepdims=True)
    return centred * lax.rsqrt(spread + norm_eps) * gain


def rotary_tables(positions, rotary_base):
    inverse = rotary_base ** (-jnp.arange(0, HEAD_DIM, 2, dtype=jnp.float32) / HEAD_DIM)
    angles = positions.astype(jnp.float32)[:, None] * inverse[None, :]
    cosine = jnp.concatenate([jnp.cos(angles), jnp.cos(angles)], axis=-1)[:, None, :]
    sine_table = jnp.concatenate([jnp.sin(angles), jnp.sin(angles)], axis=-1)[:, None, :]
    return (cosine, sine_table)


def rotate(values, cosine, sine_table):
    half_dim = values.shape[-1] // 2
    turned = jnp.concatenate([-values[..., half_dim:], values[..., :half_dim]], axis=-1)
    return values * cosine + turned * sine_table


def gelu_gate(inner, gate_part):
    return jax.nn.gelu(inner, approximate=False) * gate_part


def gather_rows(shard, chips):
    return lax.all_gather(role_swap(shard, chips), chip_axes, axis=0, tiled=True)


def scatter_rows(gradient, chips):
    shard = lax.psum_scatter(
        gradient.astype(jnp.bfloat16), chip_axes, scatter_dimension=0, tiled=True
    )
    return role_swap(shard, chips).astype(jnp.float32)


def gather_weights(masters, layer, chips):
    qkv, out, inp, down, gains = [m[layer] for m in masters]
    rows = qkv.shape[0]
    qkv_rows = jnp.concatenate(
        [qkv.reshape(rows, -1), jnp.pad(gains.T, ((0, 0), (0, 126)))], axis=1
    ).astype(jnp.bfloat16)
    qkv_all = gather_rows(qkv_rows, chips)
    width = qkv.shape[1] * qkv.shape[2]
    return (
        qkv_all[:, :width],
        gather_rows(out.T.astype(jnp.bfloat16), chips),
        gather_rows(inp[:, 0].astype(jnp.bfloat16), chips),
        gather_rows(inp[:, 1].astype(jnp.bfloat16), chips),
        gather_rows(down.T.astype(jnp.bfloat16), chips),
        qkv_all[:, width : width + 2].T.astype(jnp.float32),
    )


def band_view(heads, half_width):
    block = 2 * half_width
    seq_count, length = (heads.shape[0], heads.shape[1])
    count = length // block
    padded = jnp.pad(heads, ((0, 0), (half_width, half_width), (0, 0), (0, 0)))
    first = padded[:, :length].reshape(seq_count, count, block, heads.shape[2], heads.shape[3])
    second = padded[:, block:].reshape(seq_count, count, block, heads.shape[2], heads.shape[3])
    return jnp.concatenate([first, second], axis=2)


def band_fold(band, half_width, length):
    block = 2 * half_width
    seq_count = band.shape[0]
    first = band[:, :, :block].reshape(seq_count, length, band.shape[3], band.shape[4])
    second = band[:, :, block:].reshape(seq_count, length, band.shape[3], band.shape[4])
    padding = ((0, 0), (0, block), (0, 0), (0, 0))
    total = jnp.pad(first, padding) + jnp.pad(second, ((0, 0), (block, 0), (0, 0), (0, 0)))
    return total[:, half_width : half_width + length]


def band_mask(length, half_width):
    block = 2 * half_width
    count = length // block
    query_at = jnp.arange(block, dtype=jnp.int32)[None, :, None]
    key_at = jnp.arange(2 * block, dtype=jnp.int32)[None, None, :]
    start = jnp.arange(count, dtype=jnp.int32)[:, None, None] * block
    key_pos = start - half_width + key_at
    near = jnp.abs(query_at - key_at + half_width) <= half_width
    return near & (key_pos >= 0) & (key_pos < length)


def local_probability(queries, key_all):
    seq_count, length, heads_here, head_size = queries.shape
    block = 2 * HALF_WIN
    query_blocks = queries.reshape(seq_count, length // block, block, heads_here, head_size)
    key_band = band_view(key_all, HALF_WIN)
    scores = (
        jnp.einsum("sbqhd,sbkhd->sbhqk", query_blocks, key_band, preferred_element_type=jnp.float32)
        * 0.125
    )
    allowed = band_mask(length, HALF_WIN)[None, :, None]
    return (jnp.where(allowed, scores, masked_score), allowed, query_blocks, key_band)


def global_scores(queries, key_all):
    return (
        jnp.einsum("sqhd,skhd->shqk", queries, key_all, preferred_element_type=jnp.float32) * 0.125
    )


def attend_forward(queries, key_all, value_all, is_local):
    seq_count, length, heads_here, head_size = queries.shape
    if is_local:
        scores, allowed, query_blocks, key_band = local_probability(queries, key_all)
    else:
        scores = global_scores(queries, key_all)
    row_max = jnp.max(scores, axis=-1, keepdims=True)
    exponent = jnp.exp(scores - row_max)
    exp_total = jnp.sum(exponent, axis=-1, keepdims=True)
    probability = (exponent / exp_total).astype(jnp.bfloat16)
    if is_local:
        value_band = band_view(value_all, HALF_WIN)
        attended = jnp.einsum(
            "sbhqk,sbkhd->sbqhd", probability, value_band, preferred_element_type=jnp.float32
        )
    else:
        attended = jnp.einsum(
            "shqk,skhd->sqhd", probability, value_all, preferred_element_type=jnp.float32
        )
    return (
        attended.reshape(seq_count * length, heads_here * head_size),
        row_max + jnp.log(exp_total),
    )


def attend_backward(queries, key_all, value_all, log_total, d_attended, is_local):
    seq_count, length, heads_here, head_size = queries.shape
    if is_local:
        block = 2 * HALF_WIN
        scores, allowed, query_blocks, key_band = local_probability(queries, key_all)
        probability = jnp.where(allowed, jnp.exp(scores - log_total), 0.0)
        value_band = band_view(value_all, HALF_WIN)
        d_blocks = d_attended.reshape(seq_count, length // block, block, heads_here, head_size)
        d_value = band_fold(
            jnp.einsum(
                "sbhqk,sbqhd->sbkhd",
                probability.astype(jnp.bfloat16),
                d_blocks,
                preferred_element_type=jnp.float32,
            ),
            HALF_WIN,
            length,
        )
        d_probability = jnp.einsum(
            "sbqhd,sbkhd->sbhqk", d_blocks, value_band, preferred_element_type=jnp.float32
        )
        centre = jnp.sum(probability * d_probability, axis=-1, keepdims=True)
        d_scores = (probability * (d_probability - centre)).astype(jnp.bfloat16)
        d_queries = jnp.einsum(
            "sbhqk,sbkhd->sbqhd", d_scores, key_band, preferred_element_type=jnp.float32
        )
        d_queries = d_queries.reshape(seq_count, length, heads_here, head_size) * 0.125
        d_keys = (
            band_fold(
                jnp.einsum(
                    "sbhqk,sbqhd->sbkhd", d_scores, query_blocks, preferred_element_type=jnp.float32
                ),
                HALF_WIN,
                length,
            )
            * 0.125
        )
    else:
        d_heads = d_attended.reshape(seq_count, length, heads_here, head_size)
        probability = jnp.exp(global_scores(queries, key_all) - log_total)
        d_value = jnp.einsum(
            "shqk,sqhd->skhd",
            probability.astype(jnp.bfloat16),
            d_heads,
            preferred_element_type=jnp.float32,
        )
        d_probability = jnp.einsum(
            "sqhd,skhd->shqk", d_heads, value_all, preferred_element_type=jnp.float32
        )
        centre = jnp.sum(probability * d_probability, axis=-1, keepdims=True)
        d_scores = (probability * (d_probability - centre)).astype(jnp.bfloat16)
        d_queries = (
            jnp.einsum("shqk,skhd->sqhd", d_scores, key_all, preferred_element_type=jnp.float32)
            * 0.125
        )
        d_keys = (
            jnp.einsum("shqk,sqhd->skhd", d_scores, queries, preferred_element_type=jnp.float32)
            * 0.125
        )
    return (d_queries, d_keys, d_value)


def product(left, right, contract):
    return lax.dot_general(
        left, right, ((contract[:1], contract[1:]), ((), ())), preferred_element_type=jnp.float32
    )


def forward_layer(residual, weights, is_local):
    w_qkv, w_out, w_inner, w_gate, w_down, gain_pair = weights
    lowered = layer_norm(residual, gain_pair[0]).astype(jnp.bfloat16)
    row_count = lowered.shape[0]
    seq_count = row_count // SEQ_LEN
    local_width = w_qkv.shape[1] // 3
    heads_here = local_width // HEAD_DIM
    positions = jnp.arange(SEQ_LEN, dtype=jnp.int32)
    cosine, sine_table = rotary_tables(positions, theta_local if is_local else theta_global)
    projected = product(lowered, w_qkv, (1, 0))
    shape_four = (seq_count, SEQ_LEN, heads_here, HEAD_DIM)
    raw = [projected[:, i * local_width : (i + 1) * local_width] for i in range(3)]
    queries = rotate(raw[0].reshape(shape_four), cosine, sine_table).astype(jnp.bfloat16)
    key_all = rotate(raw[1].reshape(shape_four), cosine, sine_table).astype(jnp.bfloat16)
    value_all = raw[2].astype(jnp.bfloat16).reshape(shape_four)
    attended, log_total = attend_forward(queries, key_all, value_all, is_local)
    attended = attended.astype(jnp.bfloat16)
    middle = residual + core_total(product(attended, w_out, (1, 1)))
    lowered_two = layer_norm(middle, gain_pair[1]).astype(jnp.bfloat16)
    inner = product(lowered_two, w_inner, (1, 0))
    gate_part = product(lowered_two, w_gate, (1, 0))
    activated = gelu_gate(inner, gate_part).astype(jnp.bfloat16)
    output = middle + core_total(product(activated, w_down, (1, 1)))
    kept = (
        residual,
        middle,
        lowered,
        lowered_two,
        queries,
        key_all,
        value_all,
        log_total,
        attended,
        inner,
        gate_part,
        activated,
        cosine,
        sine_table,
    )
    return (output, kept)


def backward_layer(upstream, weights, kept, is_local, chips):
    w_qkv, w_out, w_inner, w_gate, w_down, gain_pair = weights
    (
        residual,
        middle,
        lowered,
        lowered_two,
        queries,
        key_all,
        value_all,
        log_total,
        attended,
        inner,
        gate_part,
        activated,
        cosine,
        sine_table,
    ) = kept
    row_count = lowered.shape[0]
    local_width = w_qkv.shape[1] // 3
    up_low = upstream.astype(jnp.bfloat16)
    d_activated = product(up_low, w_down, (1, 0))
    grad_down = scatter_rows(product(up_low, activated, (0, 0)), chips)
    unused, pullback = jax.vjp(gelu_gate, inner, gate_part)
    d_inner, d_gate = [v.astype(jnp.bfloat16) for v in pullback(d_activated)]
    grad_inner = scatter_rows(product(lowered_two, d_inner, (0, 0)), chips)
    grad_gate = scatter_rows(product(lowered_two, d_gate, (0, 0)), chips)
    d_normed_two = core_total(
        product(d_inner, w_inner, (1, 1)) + product(d_gate, w_gate, (1, 1))
    )
    unused, pullback = jax.vjp(layer_norm, middle, gain_pair[1])
    d_mid_norm, d_gain_two = pullback(d_normed_two)
    d_middle = upstream + d_mid_norm
    d_branch = d_middle.astype(jnp.bfloat16)
    d_attended = product(d_branch, w_out, (1, 0)).astype(jnp.bfloat16)
    grad_out = scatter_rows(product(d_branch, attended, (0, 0)), chips)
    d_queries, d_keys, d_value = attend_backward(
        queries, key_all, value_all, log_total, d_attended, is_local
    )

    def turn(heads_in):
        return rotate(heads_in, cosine, sine_table)

    unused, pullback = jax.vjp(turn, d_queries)
    d_query_raw = pullback(d_queries)[0].reshape(row_count, local_width)
    d_key_raw = pullback(d_keys)[0].reshape(row_count, local_width)
    d_projected = jnp.concatenate(
        [d_query_raw, d_key_raw, d_value.reshape(row_count, local_width)], axis=1
    ).astype(jnp.bfloat16)
    d_normed = core_total(product(d_projected, w_qkv, (1, 1)))
    unused, pullback = jax.vjp(layer_norm, residual, gain_pair[0])
    d_in_norm, d_gain_one = pullback(d_normed)
    gains = jnp.pad(jnp.stack([d_gain_one, d_gain_two], axis=1), ((0, 0), (0, 126)))
    grad_qkv = scatter_rows(
        jnp.concatenate([product(lowered, d_projected, (0, 0)), gains], axis=1), chips
    )
    rows = grad_qkv.shape[0]
    width = 3 * local_width
    gradients = (
        grad_qkv[:, :width].reshape(rows, 3, local_width),
        grad_out.T,
        jnp.stack([grad_inner, grad_gate], axis=1),
        grad_down.T,
        grad_qkv[:, width : width + 2].T,
    )
    return (d_middle + d_in_norm, gradients)


def adam_update(weight, moment, square, gradient, step_rate, decay_here):
    moment_new = beta_one * moment + (1.0 - beta_one) * gradient
    square_new = beta_two * square + (1.0 - beta_two) * gradient * gradient
    moment_hat = moment_new / (1.0 - beta_one**STEP)
    square_hat = square_new / (1.0 - beta_two**STEP)
    updated = weight - step_rate * (
        moment_hat / (jnp.sqrt(square_hat) + adam_eps) + decay_here * weight
    )
    return (moment_new, square_new, updated)


def per_device(chips, hidden_in, cotangent, *state):
    masters = state[:5]
    moments = state[5:]
    same = lax.axis_index("core") == lax.axis_index("tensor")

    def chip_sequence(values):
        return jnp.where(same, values, core_swap(values)).astype(jnp.float32)

    def own_sequence(values):
        return jnp.where(same, values, lax.ppermute(values, every_axis, result_pairs(chips)))

    inputs = chip_sequence(hidden_in)
    upstream = chip_sequence(cotangent)
    first_weights = gather_weights(masters, 0, chips)
    second_weights = gather_weights(masters, 1, chips)
    middle, kept_first = forward_layer(inputs, first_weights, True)
    output, kept_second = forward_layer(middle, second_weights, False)
    final_out = own_sequence(output.astype(jnp.bfloat16))
    d_middle, grads_second = backward_layer(upstream, second_weights, kept_second, False, chips)
    d_values, grads_first = backward_layer(d_middle, first_weights, kept_first, True, chips)
    final_grad = own_sequence(d_values.astype(jnp.bfloat16)).astype(jnp.float32)
    rates = (rate_qkv, rate_out, rate_inp, rate_down, rate_gain)
    results = [final_out, final_grad]
    for i, rate in enumerate(rates):
        gradient = jnp.stack([grads_first[i], grads_second[i]])
        decay = 0.0 if i == 4 else weight_decay
        results += adam_update(
            masters[i], moments[2 * i], moments[2 * i + 1], gradient, rate, decay
        )
    return tuple(results)


def solution(mesh):
    chips = mesh.shape["dp"] // 2
    fine = Mesh(mesh.devices.reshape(chips, 2, mesh.shape["tensor"]), every_axis)
    dp = ("chip", "core")
    tokens = P(dp, None)
    first = P(None, dp, None, "tensor")
    second = P(None, "tensor", dp)
    gain = P(None, None, dp)
    weights = (first, second, first, second, gain)
    pairs = tuple(s for s in weights for unused in range(2))
    triples = tuple(s for s in weights for unused in range(3))

    def body(*arguments):
        return per_device(chips, *arguments)

    return jax.shard_map(
        body,
        mesh=fine,
        in_specs=(tokens, tokens) + weights + pairs,
        out_specs=(tokens, tokens) + triples,
        check_vma=False,
    )
```

```python
import jax
import jax.numpy as jnp
from jax import lax
from jax.sharding import Mesh, PartitionSpec as P

HEAD_DIM = 64
HALF_WIN = 64
STEP = 10
SEQ_LEN = 1024


norm_eps = 1e-05
theta_local = 10000.0
theta_global = 160000.0
masked_score = -1e30
beta_one = 0.9
beta_two = 0.98
adam_eps = 1e-06
weight_decay = 1e-05
rate_qkv = 0.03
rate_out = 0.15
rate_inp = 0.03
rate_down = 0.02
rate_gain = 0.5

every_axis = ("chip", "core", "tensor")
chip_axes = ("chip", "tensor")


def swap_pairs(chips):
    pairs = []
    for chip in range(chips):
        for core in range(2):
            for row in range(2):
                pairs.append((chip * 4 + core * 2 + row, chip * 4 + row * 2 + core))
    return pairs


def result_pairs(chips):
    return [(chip * 4 + c * 3, chip * 4 + c * 2 + 1 - c) for chip in range(chips) for c in range(2)]


def role_swap(values, chips):
    return lax.ppermute(values, every_axis, swap_pairs(chips))


def core_swap(values):
    return lax.ppermute(values, "core", [(0, 1), (1, 0)])


def core_total(partial_sum):
    own = partial_sum.astype(jnp.bfloat16)
    return own.astype(jnp.float32) + core_swap(own).astype(jnp.float32)


def layer_norm(values, gain):
    centred = values - jnp.mean(values, axis=-1, keepdims=True)
    spread = jnp.mean(centred * centred, axis=-1, keepdims=True)
    return centred * lax.rsqrt(spread + norm_eps) * gain


def rotary_tables(positions, rotary_base):
    inverse = rotary_base ** (-jnp.arange(0, HEAD_DIM, 2, dtype=jnp.float32) / HEAD_DIM)
    angles = positions.astype(jnp.float32)[:, None] * inverse[None, :]
    cosine = jnp.concatenate([jnp.cos(angles), jnp.cos(angles)], axis=-1)[:, None, :]
    sine_table = jnp.concatenate([jnp.sin(angles), jnp.sin(angles)], axis=-1)[:, None, :]
    return (cosine, sine_table)


def rotate(values, cosine, sine_table):
    half_dim = values.shape[-1] // 2
    turned = jnp.concatenate([-values[..., half_dim:], values[..., :half_dim]], axis=-1)
    return values * cosine + turned * sine_table


def gelu_gate(inner, gate_part):
    return jax.nn.gelu(inner, approximate=False) * gate_part


def group_bits(chips):
    return chips.bit_length() - 1


def bit_swap(values, bit, chips):
    if bit < 0:
        return lax.ppermute(values, "tensor", [(0, 1), (1, 0)])
    return lax.ppermute(values, "chip", [(chip, chip ^ (1 << bit)) for chip in range(chips)])


def own_bit(bit):
    if bit < 0:
        return lax.axis_index("tensor")
    return (lax.axis_index("chip") >> bit) & 1


def gather_bit(values, held, bit, chips):
    place = len([b for b in held if b > bit])
    other = bit_swap(values, bit, chips)
    is_low = own_bit(bit) == 0
    joined = jnp.stack(
        [jnp.where(is_low, values, other), jnp.where(is_low, other, values)], axis=place
    )
    return joined, sorted(held + [bit], reverse=True)


def reduce_bit(values, held, bit, chips):
    place = held.index(bit)
    mine = own_bit(bit)
    kept = lax.dynamic_index_in_dim(values, mine, place, keepdims=False)
    sent = lax.dynamic_index_in_dim(values, 1 - mine, place, keepdims=False)
    other = bit_swap(sent, bit, chips)
    total = (kept.astype(jnp.float32) + other.astype(jnp.float32)).astype(jnp.bfloat16)
    return total, [b for b in held if b != bit]


def gather_quick(shard, cut, chips):
    values, held = shard, []
    for bit in range(group_bits(chips) - 1, 0, -1):
        values, held = gather_bit(values, held, bit, chips)
    halves = []
    for order, part in (((0, -1), values[..., :cut]), ((-1, 0), values[..., cut:])):
        part_held = held
        for bit in order:
            part, part_held = gather_bit(part, part_held, bit, chips)
        halves.append(part.reshape(-1, part.shape[-1]))
    return halves


def scatter_quick(halves, chips):
    count = group_bits(chips)
    parts = []
    for order, part in (((-1, 0), halves[0]), ((0, -1), halves[1])):
        held = list(range(count - 1, -2, -1))
        values = part.astype(jnp.bfloat16).reshape([2] * len(held) + [-1, part.shape[-1]])
        for bit in order:
            values, held = reduce_bit(values, held, bit, chips)
        parts.append(values)
    values = jnp.concatenate(parts, axis=-1)
    for bit in range(1, count):
        values, held = reduce_bit(values, held, bit, chips)
    return role_swap(values, chips).astype(jnp.float32)


def gather_rows(shard, chips):
    return lax.all_gather(shard, chip_axes, axis=0, tiled=True)


def scatter_rows(gradient, chips):
    shard = lax.psum_scatter(
        gradient.astype(jnp.bfloat16), chip_axes, scatter_dimension=0, tiled=True
    )
    return role_swap(shard, chips).astype(jnp.float32)


def padded_width(width):
    return -(-width // 128) * 128


def widen(values):
    width = values.shape[1]
    return jnp.pad(values, ((0, 0), (0, padded_width(width) - width)))


def pack_shards(masters, layer):
    qkv, out, inp, down, gains = [m[layer] for m in masters]
    quick = jnp.concatenate([qkv.reshape(qkv.shape[0], -1), widen(gains.T)], axis=1)
    bulk = jnp.concatenate([out.T, widen(inp[:, 0]), widen(inp[:, 1]), down.T], axis=1)
    return quick.astype(jnp.bfloat16), bulk.astype(jnp.bfloat16)


def gather_weights(masters, quick, bulk, chips):
    qkv, out, inp, down, gains = masters
    width = qkv.shape[2] * qkv.shape[3]
    cut = width // 2
    first, second = gather_quick(quick, cut, chips)
    bulk = gather_rows(bulk, chips)
    heads, hidden = out.shape[1], down.shape[1]
    step = padded_width(hidden)
    start = heads
    w_inner = bulk[:, start : start + hidden]
    w_gate = bulk[:, start + step : start + step + hidden]
    w_down = bulk[:, start + 2 * step :]
    return (
        jnp.concatenate([first, second[:, :cut]], axis=1),
        bulk[:, :heads],
        w_inner,
        w_gate,
        w_down,
        second[:, cut : cut + 2].T.astype(jnp.float32),
    )


def band_view(heads, half_width):
    block = 2 * half_width
    seq_count, length = (heads.shape[0], heads.shape[1])
    count = length // block
    padded = jnp.pad(heads, ((0, 0), (half_width, half_width), (0, 0), (0, 0)))
    first = padded[:, :length].reshape(seq_count, count, block, heads.shape[2], heads.shape[3])
    second = padded[:, block:].reshape(seq_count, count, block, heads.shape[2], heads.shape[3])
    return jnp.concatenate([first, second], axis=2)


def band_fold(band, half_width, length):
    block = 2 * half_width
    seq_count = band.shape[0]
    first = band[:, :, :block].reshape(seq_count, length, band.shape[3], band.shape[4])
    second = band[:, :, block:].reshape(seq_count, length, band.shape[3], band.shape[4])
    padding = ((0, 0), (0, block), (0, 0), (0, 0))
    total = jnp.pad(first, padding) + jnp.pad(second, ((0, 0), (block, 0), (0, 0), (0, 0)))
    return total[:, half_width : half_width + length]


def band_mask(length, half_width):
    block = 2 * half_width
    count = length // block
    query_at = jnp.arange(block, dtype=jnp.int32)[None, :, None]
    key_at = jnp.arange(2 * block, dtype=jnp.int32)[None, None, :]
    start = jnp.arange(count, dtype=jnp.int32)[:, None, None] * block
    key_pos = start - half_width + key_at
    near = jnp.abs(query_at - key_at + half_width) <= half_width
    return near & (key_pos >= 0) & (key_pos < length)


def local_probability(queries, key_all):
    seq_count, length, heads_here, head_size = queries.shape
    block = 2 * HALF_WIN
    query_blocks = queries.reshape(seq_count, length // block, block, heads_here, head_size)
    key_band = band_view(key_all, HALF_WIN)
    scores = (
        jnp.einsum("sbqhd,sbkhd->sbhqk", query_blocks, key_band, preferred_element_type=jnp.float32)
        * 0.125
    )
    allowed = band_mask(length, HALF_WIN)[None, :, None]
    return (jnp.where(allowed, scores, masked_score), allowed, query_blocks, key_band)


def global_scores(queries, key_all):
    return (
        jnp.einsum("sqhd,skhd->shqk", queries, key_all, preferred_element_type=jnp.float32) * 0.125
    )


def attend_forward(queries, key_all, value_all, is_local):
    seq_count, length, heads_here, head_size = queries.shape
    if is_local:
        scores, allowed, query_blocks, key_band = local_probability(queries, key_all)
    else:
        scores = global_scores(queries, key_all)
    row_max = jnp.max(scores, axis=-1, keepdims=True)
    exponent = jnp.exp(scores - row_max)
    exp_total = jnp.sum(exponent, axis=-1, keepdims=True)
    probability = (exponent / exp_total).astype(jnp.bfloat16)
    if is_local:
        value_band = band_view(value_all, HALF_WIN)
        attended = jnp.einsum(
            "sbhqk,sbkhd->sbqhd", probability, value_band, preferred_element_type=jnp.float32
        )
    else:
        attended = jnp.einsum(
            "shqk,skhd->sqhd", probability, value_all, preferred_element_type=jnp.float32
        )
    return (
        attended.reshape(seq_count * length, heads_here * head_size),
        row_max + jnp.log(exp_total),
    )


def attend_backward(queries, key_all, value_all, log_total, d_attended, is_local):
    seq_count, length, heads_here, head_size = queries.shape
    if is_local:
        block = 2 * HALF_WIN
        scores, allowed, query_blocks, key_band = local_probability(queries, key_all)
        probability = jnp.where(allowed, jnp.exp(scores - log_total), 0.0)
        value_band = band_view(value_all, HALF_WIN)
        d_blocks = d_attended.reshape(seq_count, length // block, block, heads_here, head_size)
        d_value = band_fold(
            jnp.einsum(
                "sbhqk,sbqhd->sbkhd",
                probability.astype(jnp.bfloat16),
                d_blocks,
                preferred_element_type=jnp.float32,
            ),
            HALF_WIN,
            length,
        )
        d_probability = jnp.einsum(
            "sbqhd,sbkhd->sbhqk", d_blocks, value_band, preferred_element_type=jnp.float32
        )
        centre = jnp.sum(probability * d_probability, axis=-1, keepdims=True)
        d_scores = (probability * (d_probability - centre)).astype(jnp.bfloat16)
        d_queries = jnp.einsum(
            "sbhqk,sbkhd->sbqhd", d_scores, key_band, preferred_element_type=jnp.float32
        )
        d_queries = d_queries.reshape(seq_count, length, heads_here, head_size) * 0.125
        d_keys = (
            band_fold(
                jnp.einsum(
                    "sbhqk,sbqhd->sbkhd", d_scores, query_blocks, preferred_element_type=jnp.float32
                ),
                HALF_WIN,
                length,
            )
            * 0.125
        )
    else:
        d_heads = d_attended.reshape(seq_count, length, heads_here, head_size)
        probability = jnp.exp(global_scores(queries, key_all) - log_total)
        d_value = jnp.einsum(
            "shqk,sqhd->skhd",
            probability.astype(jnp.bfloat16),
            d_heads,
            preferred_element_type=jnp.float32,
        )
        d_probability = jnp.einsum(
            "sqhd,skhd->shqk", d_heads, value_all, preferred_element_type=jnp.float32
        )
        centre = jnp.sum(probability * d_probability, axis=-1, keepdims=True)
        d_scores = (probability * (d_probability - centre)).astype(jnp.bfloat16)
        d_queries = (
            jnp.einsum("shqk,skhd->sqhd", d_scores, key_all, preferred_element_type=jnp.float32)
            * 0.125
        )
        d_keys = (
            jnp.einsum("shqk,sqhd->skhd", d_scores, queries, preferred_element_type=jnp.float32)
            * 0.125
        )
    return (d_queries, d_keys, d_value)


def product(left, right, contract):
    return lax.dot_general(
        left, right, ((contract[:1], contract[1:]), ((), ())), preferred_element_type=jnp.float32
    )


def forward_layer(residual, weights, is_local):
    w_qkv, w_out, w_inner, w_gate, w_down, gain_pair = weights
    lowered = layer_norm(residual, gain_pair[0]).astype(jnp.bfloat16)
    row_count = lowered.shape[0]
    seq_count = row_count // SEQ_LEN
    local_width = w_qkv.shape[1] // 3
    heads_here = local_width // HEAD_DIM
    positions = jnp.arange(SEQ_LEN, dtype=jnp.int32)
    cosine, sine_table = rotary_tables(positions, theta_local if is_local else theta_global)
    projected = product(lowered, w_qkv, (1, 0))
    shape_four = (seq_count, SEQ_LEN, heads_here, HEAD_DIM)
    raw = [projected[:, i * local_width : (i + 1) * local_width] for i in range(3)]
    queries = rotate(raw[0].reshape(shape_four), cosine, sine_table).astype(jnp.bfloat16)
    key_all = rotate(raw[1].reshape(shape_four), cosine, sine_table).astype(jnp.bfloat16)
    value_all = raw[2].astype(jnp.bfloat16).reshape(shape_four)
    attended, log_total = attend_forward(queries, key_all, value_all, is_local)
    attended = attended.astype(jnp.bfloat16)
    middle = residual + core_total(product(attended, w_out, (1, 1)))
    lowered_two = layer_norm(middle, gain_pair[1]).astype(jnp.bfloat16)
    inner = product(lowered_two, w_inner, (1, 0))
    gate_part = product(lowered_two, w_gate, (1, 0))
    activated = gelu_gate(inner, gate_part).astype(jnp.bfloat16)
    output = middle + core_total(product(activated, w_down, (1, 1)))
    kept = (
        residual,
        middle,
        lowered,
        lowered_two,
        queries,
        key_all,
        value_all,
        log_total,
        attended,
        inner,
        gate_part,
        activated,
        cosine,
        sine_table,
    )
    return (output, kept)


def backward_layer(upstream, weights, kept, is_local, chips):
    w_qkv, w_out, w_inner, w_gate, w_down, gain_pair = weights
    (
        residual,
        middle,
        lowered,
        lowered_two,
        queries,
        key_all,
        value_all,
        log_total,
        attended,
        inner,
        gate_part,
        activated,
        cosine,
        sine_table,
    ) = kept
    row_count = lowered.shape[0]
    local_width = w_qkv.shape[1] // 3
    up_low = upstream.astype(jnp.bfloat16)
    d_activated = product(up_low, w_down, (1, 0))
    grad_down = product(up_low, activated, (0, 0)).astype(jnp.bfloat16)
    unused, pullback = jax.vjp(gelu_gate, inner, gate_part)
    d_inner, d_gate = [v.astype(jnp.bfloat16) for v in pullback(d_activated)]
    grad_inner = product(lowered_two, d_inner, (0, 0)).astype(jnp.bfloat16)
    grad_gate = product(lowered_two, d_gate, (0, 0)).astype(jnp.bfloat16)
    d_normed_two = core_total(
        product(d_inner, w_inner, (1, 1)) + product(d_gate, w_gate, (1, 1))
    )
    unused, pullback = jax.vjp(layer_norm, middle, gain_pair[1])
    d_mid_norm, d_gain_two = pullback(d_normed_two)
    d_middle = upstream + d_mid_norm
    d_branch = d_middle.astype(jnp.bfloat16)
    d_attended = product(d_branch, w_out, (1, 0)).astype(jnp.bfloat16)
    grad_out = product(d_branch, attended, (0, 0)).astype(jnp.bfloat16)
    heads, hidden = grad_out.shape[1], grad_down.shape[1]
    step = padded_width(hidden)
    bulk = jnp.concatenate([grad_out, widen(grad_inner), widen(grad_gate), grad_down], axis=1)
    d_attended, bulk = lax.optimization_barrier((d_attended, bulk))
    bulk = scatter_rows(bulk, chips)
    grad_inp = jnp.stack(
        [bulk[:, heads : heads + hidden], bulk[:, heads + step : heads + step + hidden]], axis=1
    )
    d_queries, d_keys, d_value = attend_backward(
        queries, key_all, value_all, log_total, d_attended, is_local
    )

    def turn(heads_in):
        return rotate(heads_in, cosine, sine_table)

    unused, pullback = jax.vjp(turn, d_queries)
    d_query_raw = pullback(d_queries)[0].reshape(row_count, local_width)
    d_key_raw = pullback(d_keys)[0].reshape(row_count, local_width)
    d_projected = jnp.concatenate(
        [d_query_raw, d_key_raw, d_value.reshape(row_count, local_width)], axis=1
    ).astype(jnp.bfloat16)
    d_normed = core_total(product(d_projected, w_qkv, (1, 1)))
    unused, pullback = jax.vjp(layer_norm, residual, gain_pair[0])
    d_in_norm, d_gain_one = pullback(d_normed)
    gains = widen(jnp.stack([d_gain_one, d_gain_two], axis=1)).astype(jnp.bfloat16)
    width = 3 * local_width
    cut = width // 2
    grad_qkv = product(lowered, d_projected, (0, 0)).astype(jnp.bfloat16)
    quick = scatter_quick(
        (grad_qkv[:, :cut], jnp.concatenate([grad_qkv[:, cut:], gains], axis=1)), chips
    )
    gradients = (
        quick[:, :width].reshape(-1, 3, local_width),
        bulk[:, :heads].T,
        grad_inp,
        bulk[:, heads + 2 * step :].T,
        quick[:, width : width + 2].T,
    )
    return (d_middle + d_in_norm, gradients)


def adam_update(weight, moment, square, gradient, step_rate, decay_here):
    moment_new = beta_one * moment + (1.0 - beta_one) * gradient
    square_new = beta_two * square + (1.0 - beta_two) * gradient * gradient
    moment_hat = moment_new / (1.0 - beta_one**STEP)
    square_hat = square_new / (1.0 - beta_two**STEP)
    updated = weight - step_rate * (
        moment_hat / (jnp.sqrt(square_hat) + adam_eps) + decay_here * weight
    )
    return (moment_new, square_new, updated)


def per_device(chips, hidden_in, cotangent, *state):
    masters = state[:5]
    moments = state[5:]
    same = lax.axis_index("core") == lax.axis_index("tensor")

    def chip_sequence(values):
        return jnp.where(same, values, core_swap(values)).astype(jnp.float32)

    def own_sequence(values):
        return jnp.where(same, values, lax.ppermute(values, every_axis, result_pairs(chips)))

    quick_first, bulk_first = pack_shards(masters, 0)
    quick_second, bulk_second = pack_shards(masters, 1)
    quick_first = role_swap(quick_first, chips)
    rest = role_swap(jnp.concatenate([bulk_first, bulk_second, quick_second], axis=1), chips)
    cut = bulk_first.shape[1]
    hidden_in, quick_first, rest = lax.optimization_barrier((hidden_in, quick_first, rest))
    inputs = chip_sequence(hidden_in)
    upstream = chip_sequence(cotangent)
    first_weights = gather_weights(masters, quick_first, rest[:, :cut], chips)
    second_weights = gather_weights(masters, rest[:, 2 * cut :], rest[:, cut : 2 * cut], chips)
    middle, kept_first = forward_layer(inputs, first_weights, True)
    output, kept_second = forward_layer(middle, second_weights, False)
    final_out = own_sequence(output.astype(jnp.bfloat16))
    d_middle, grads_second = backward_layer(upstream, second_weights, kept_second, False, chips)
    d_values, grads_first = backward_layer(d_middle, first_weights, kept_first, True, chips)
    final_grad = own_sequence(d_values.astype(jnp.bfloat16)).astype(jnp.float32)
    rates = (rate_qkv, rate_out, rate_inp, rate_down, rate_gain)
    results = [final_out, final_grad]
    for i, rate in enumerate(rates):
        gradient = jnp.stack([grads_first[i], grads_second[i]])
        decay = 0.0 if i == 4 else weight_decay
        results += adam_update(
            masters[i], moments[2 * i], moments[2 * i + 1], gradient, rate, decay
        )
    return tuple(results)


def solution(mesh):
    chips = mesh.shape["dp"] // 2
    fine = Mesh(mesh.devices.reshape(chips, 2, mesh.shape["tensor"]), every_axis)
    dp = ("chip", "core")
    tokens = P(dp, None)
    first = P(None, dp, None, "tensor")
    second = P(None, "tensor", dp)
    gain = P(None, None, dp)
    weights = (first, second, first, second, gain)
    pairs = tuple(s for s in weights for unused in range(2))
    triples = tuple(s for s in weights for unused in range(3))

    def body(*arguments):
        return per_device(chips, *arguments)

    return jax.shard_map(
        body,
        mesh=fine,
        in_specs=(tokens, tokens) + weights + pairs,
        out_specs=(tokens, tokens) + triples,
        check_vma=False,
    )
```

```python
import functools

import jax
import jax.numpy as jnp
from jax import lax
from jax.experimental import pallas as pl
from jax.experimental.pallas import tpu as pltpu
from jax.sharding import Mesh, PartitionSpec as P

HEAD_DIM = 64
HALF_WIN = 64
STEP = 10
SEQ_LEN = 1024


norm_eps = 1e-05
theta_local = 10000.0
theta_global = 160000.0
masked_score = -1e30
beta_one = 0.9
beta_two = 0.98
adam_eps = 1e-06
weight_decay = 1e-05
rate_qkv = 0.03
rate_out = 0.15
rate_inp = 0.03
rate_down = 0.02
rate_gain = 0.5

kernel_vmem = 48 * 1024 * 1024
every_axis = ("chip", "core", "tensor")
chip_axes = ("chip", "tensor")


def swap_pairs(chips):
    pairs = []
    for chip in range(chips):
        for core in range(2):
            for row in range(2):
                pairs.append((chip * 4 + core * 2 + row, chip * 4 + row * 2 + core))
    return pairs


def result_pairs(chips):
    return [(chip * 4 + c * 3, chip * 4 + c * 2 + 1 - c) for chip in range(chips) for c in range(2)]


def role_swap(values, chips):
    return lax.ppermute(values, every_axis, swap_pairs(chips))


def core_swap(values):
    return lax.ppermute(values, "core", [(0, 1), (1, 0)])


def core_total(partial_sum):
    own = partial_sum.astype(jnp.bfloat16)
    return own.astype(jnp.float32) + core_swap(own).astype(jnp.float32)


def layer_norm(values, gain):
    centred = values - jnp.mean(values, axis=-1, keepdims=True)
    spread = jnp.mean(centred * centred, axis=-1, keepdims=True)
    return centred * lax.rsqrt(spread + norm_eps) * gain


def rotary_tables(rotary_base):
    positions = jnp.arange(SEQ_LEN, dtype=jnp.int32)
    inverse = rotary_base ** (-jnp.arange(0, HEAD_DIM, 2, dtype=jnp.float32) / HEAD_DIM)
    angles = positions.astype(jnp.float32)[:, None] * inverse[None, :]
    cosine, sine = jnp.cos(angles), jnp.sin(angles)
    return (
        jnp.concatenate([cosine] * 4, axis=-1),
        jnp.concatenate([-sine, sine, -sine, sine], axis=-1),
    )


def gelu_gate(inner, gate_part):
    return jax.nn.gelu(inner, approximate=False) * gate_part


def gather_rows(shard, chips):
    return lax.all_gather(shard, chip_axes, axis=0, tiled=True)


def scatter_rows(gradient, chips):
    shard = lax.psum_scatter(
        gradient.astype(jnp.bfloat16), chip_axes, scatter_dimension=0, tiled=True
    )
    return role_swap(shard, chips).astype(jnp.float32)


def padded_width(width):
    return -(-width // 128) * 128


def widen(values):
    width = values.shape[1]
    return jnp.pad(values, ((0, 0), (0, padded_width(width) - width)))


def layer_starts(masters):
    heads = masters[0].shape[3]
    step = padded_width(masters[2].shape[3])
    return (0, 3 * heads, 4 * heads, 4 * heads + 128, 4 * heads + 128 + step, 4 * heads + 128 + 2 * step)


def pair_major(values):
    rows, kinds, width = values.shape
    wide = 2 * HEAD_DIM
    return values.reshape(rows, kinds, width // wide, wide).swapaxes(1, 2).reshape(rows, -1)


def kind_major(values):
    rows, wide = values.shape[0], 2 * HEAD_DIM
    return values.reshape(rows, -1, 3, wide).swapaxes(1, 2).reshape(rows, 3, -1)


def pack_shards(masters, layer):
    qkv, out, inp, down, gains = [m[layer].astype(jnp.bfloat16) for m in masters]
    return jnp.concatenate(
        [pair_major(qkv), out.T, widen(gains.T), widen(inp[:, 0]), widen(inp[:, 1]), down.T], axis=1
    )


def unpack_weights(packed, starts, hidden):
    return (
        packed[:, : starts[1]],
        packed[:, starts[1] : starts[2]],
        packed[:, starts[3] : starts[3] + hidden],
        packed[:, starts[4] : starts[4] + hidden],
        packed[:, starts[5] :],
        packed[:, starts[2] : starts[2] + 2].T.astype(jnp.float32),
    )


def unpack_grads(packed, starts, hidden):
    inner = packed[:, starts[3] : starts[3] + hidden]
    gate = packed[:, starts[4] : starts[4] + hidden]
    return (
        kind_major(packed[:, : starts[1]]),
        packed[:, starts[1] : starts[2]].T,
        jnp.stack([inner, gate], axis=1),
        packed[:, starts[5] :].T,
        packed[:, starts[2] : starts[2] + 2].T,
    )


def rolled(values):
    lane = lax.broadcasted_iota(jnp.int32, values.shape, 1) % HEAD_DIM
    half = HEAD_DIM // 2
    width = values.shape[1]
    return jnp.where(
        lane < half, pltpu.roll(values, width - half, 1), pltpu.roll(values, half, 1)
    )


def pair_stack(values):
    lane = lax.broadcasted_iota(jnp.int32, values.shape, 1)
    nothing = jnp.zeros_like(values)
    return jnp.concatenate(
        [jnp.where(lane < HEAD_DIM, values, nothing), jnp.where(lane < HEAD_DIM, nothing, values)],
        axis=0,
    )


def pair_unstack(values):
    rows = values.shape[1] // 2
    return jnp.concatenate(
        [values[:HEAD_DIM, :rows], values[HEAD_DIM:, rows:]], axis=0
    ).T


def probability_block(keys_here, stacked, start, is_local, length):
    scores = (
        lax.dot_general(
            keys_here, stacked, (((1,), (1,)), ((), ())), preferred_element_type=jnp.float32
        )
        * 0.125
    )
    if is_local:
        rows = stacked.shape[0] // 2
        key_at = start - HALF_WIN + lax.broadcasted_iota(jnp.int32, scores.shape, 0)
        query_at = start + lax.broadcasted_iota(jnp.int32, scores.shape, 1) % rows
        allowed = (jnp.abs(query_at - key_at) <= HALF_WIN) & (key_at >= 0) & (key_at < length)
        scores = jnp.where(allowed, scores, masked_score)
    exponent = jnp.exp(scores - jnp.max(scores, axis=0, keepdims=True))
    return exponent * (1.0 / jnp.sum(exponent, axis=0, keepdims=True))


def attend_kernel(is_local, block, raw_ref, cos_ref, sin_ref, out_ref, keys, values_t):
    length = raw_ref.shape[0]
    pad = HALF_WIN if is_local else 0
    reach = block + 2 * HALF_WIN if is_local else length
    wide = 2 * HEAD_DIM
    raw_keys = raw_ref[:, wide : 2 * wide]
    rotated = (raw_keys * cos_ref[...] + rolled(raw_keys) * sin_ref[...]).astype(jnp.bfloat16)
    if is_local:
        keys[...] = jnp.zeros_like(keys)
        values_t[...] = jnp.zeros_like(values_t)
    keys[pl.ds(pad, length), :] = rotated
    values_t[:, pl.ds(pad, length)] = raw_ref[:, 2 * wide :].astype(jnp.bfloat16).T

    def step(i):
        start = pl.multiple_of(i * block, block)
        at = start if is_local else 0
        part = raw_ref[pl.ds(start, block), :wide]
        here = pl.ds(start, block)
        query = (part * cos_ref[here, :] + rolled(part) * sin_ref[here, :]).astype(jnp.bfloat16)
        probability = probability_block(
            keys[pl.ds(at, reach), :], pair_stack(query), start, is_local, length
        )
        mixed = jnp.dot(
            values_t[:, pl.ds(at, reach)],
            probability.astype(jnp.bfloat16),
            preferred_element_type=jnp.float32,
        )
        out_ref[here, :] = pair_unstack(mixed).astype(jnp.bfloat16)

    pl.loop(0, length // block, unroll=2)(step)


def attend_back_kernel(
    is_local, block, raw_ref, cos_ref, sin_ref, up_ref, out_ref, keys, keys_t, values, d_keys, d_values
):
    length = raw_ref.shape[0]
    pad = HALF_WIN if is_local else 0
    reach = block + 2 * HALF_WIN if is_local else length
    wide = 2 * HEAD_DIM
    raw_keys = raw_ref[:, wide : 2 * wide]
    rotated = (raw_keys * cos_ref[...] + rolled(raw_keys) * sin_ref[...]).astype(jnp.bfloat16)
    if is_local:
        keys[...] = jnp.zeros_like(keys)
        keys_t[...] = jnp.zeros_like(keys_t)
        values[...] = jnp.zeros_like(values)
    keys[pl.ds(pad, length), :] = rotated
    keys_t[:, pl.ds(pad, length)] = rotated.T
    values[pl.ds(pad, length), :] = raw_ref[:, 2 * wide :].astype(jnp.bfloat16)
    d_keys[...] = jnp.zeros_like(d_keys)
    d_values[...] = jnp.zeros_like(d_values)

    def step(i):
        start = pl.multiple_of(i * block, block)
        at = start if is_local else 0
        here = pl.ds(start, block)
        band = pl.ds(at, reach)
        part = raw_ref[here, :wide]
        query = (part * cos_ref[here, :] + rolled(part) * sin_ref[here, :]).astype(jnp.bfloat16)
        stacked = pair_stack(query)
        upstream = pair_stack(up_ref[here, :])
        probability = probability_block(keys[band, :], stacked, start, is_local, length)
        d_values[band, :] += jnp.dot(
            probability.astype(jnp.bfloat16), upstream, preferred_element_type=jnp.float32
        )
        d_probability = lax.dot_general(
            values[band, :], upstream, (((1,), (1,)), ((), ())), preferred_element_type=jnp.float32
        )
        centre = jnp.sum(probability * d_probability, axis=0, keepdims=True)
        d_scores = (probability * (d_probability - centre)).astype(jnp.bfloat16)
        d_keys[band, :] += jnp.dot(d_scores, stacked, preferred_element_type=jnp.float32)
        d_query = (
            pair_unstack(
                jnp.dot(keys_t[:, band], d_scores, preferred_element_type=jnp.float32)
            )
            * 0.125
        )
        out_ref[here, :wide] = (
            d_query * cos_ref[here, :] - rolled(d_query) * sin_ref[here, :]
        ).astype(jnp.bfloat16)

    pl.loop(0, length // block, unroll=2)(step)
    d_key = d_keys[pl.ds(pad, length), :] * 0.125
    out_ref[:, wide : 2 * wide] = (d_key * cos_ref[...] - rolled(d_key) * sin_ref[...]).astype(
        jnp.bfloat16
    )
    out_ref[:, 2 * wide :] = d_values[pl.ds(pad, length), :].astype(jnp.bfloat16)


def attend_specs(projected):
    rows, columns = projected.shape
    wide = 2 * HEAD_DIM
    raw = pl.BlockSpec((SEQ_LEN, 3 * wide), lambda s, j: (s, j))
    table = pl.BlockSpec((SEQ_LEN, wide), lambda s, j: (0, 0))
    narrow = pl.BlockSpec((SEQ_LEN, wide), lambda s, j: (s, j))
    grid = (rows // SEQ_LEN, columns // (3 * wide))
    return grid, raw, table, narrow


def attend_cost(projected, is_local, products):
    rows, columns = projected.shape
    reach = 4 * HALF_WIN if is_local else SEQ_LEN
    pairs = columns // (6 * HEAD_DIM)
    cells = rows * reach * pairs * 2
    return pl.CostEstimate(
        flops=cells * 8 * HEAD_DIM * products,
        bytes_accessed=projected.size * 8,
        transcendentals=cells,
    )


def attend_forward(projected, tables, is_local):
    rows, columns = projected.shape
    wide = 2 * HEAD_DIM
    grid, raw, table, narrow = attend_specs(projected)
    span = SEQ_LEN + 2 * HALF_WIN if is_local else SEQ_LEN
    return pl.pallas_call(
        functools.partial(attend_kernel, is_local, 128),
        out_shape=jax.ShapeDtypeStruct((rows, columns // 3), jnp.bfloat16),
        grid=grid,
        in_specs=[raw, table, table],
        out_specs=narrow,
        scratch_shapes=[
            pltpu.VMEM((span, wide), jnp.bfloat16),
            pltpu.VMEM((wide, span), jnp.bfloat16),
        ],
        compiler_params=pltpu.CompilerParams(vmem_limit_bytes=kernel_vmem),
        cost_estimate=attend_cost(projected, is_local, 2),
    )(projected, *tables)


def attend_backward(projected, tables, d_attended, is_local):
    rows, columns = projected.shape
    wide = 2 * HEAD_DIM
    grid, raw, table, narrow = attend_specs(projected)
    span = SEQ_LEN + 2 * HALF_WIN if is_local else SEQ_LEN
    return pl.pallas_call(
        functools.partial(attend_back_kernel, is_local, 128),
        out_shape=jax.ShapeDtypeStruct((rows, columns), jnp.bfloat16),
        grid=grid,
        in_specs=[raw, table, table, narrow],
        out_specs=raw,
        scratch_shapes=[
            pltpu.VMEM((span, wide), jnp.bfloat16),
            pltpu.VMEM((wide, span), jnp.bfloat16),
            pltpu.VMEM((span, wide), jnp.bfloat16),
            pltpu.VMEM((span, wide), jnp.float32),
            pltpu.VMEM((span, wide), jnp.float32),
        ],
        compiler_params=pltpu.CompilerParams(vmem_limit_bytes=kernel_vmem),
        cost_estimate=attend_cost(projected, is_local, 5),
    )(projected, *tables, d_attended)


def weight_grad_kernel(
    starts, lowered, branch, lowered_two, up, d_projected, attended, gains, d_inner, d_gate,
    activated, out_ref
):
    def put(left, right, start):
        width = right.shape[1]
        out_ref[:, start : start + width] = lax.dot_general(
            left, right[...], (((0,), (0,)), ((), ())), preferred_element_type=jnp.float32
        ).astype(jnp.bfloat16)

    put(lowered[...], d_projected, starts[0])
    put(branch[...], attended, starts[1])
    out_ref[:, starts[2] : starts[3]] = gains[...]
    normed = lowered_two[...]
    for right, start, stop in ((d_inner, starts[3], starts[4]), (d_gate, starts[4], starts[5])):
        put(normed, right, start)
        filled = start + right.shape[1]
        if filled < stop:
            out_ref[:, filled:stop] = jnp.zeros((out_ref.shape[0], stop - filled), jnp.bfloat16)
    put(up[...], activated, starts[5])


def weight_grads(starts, lefts, rights, gains):
    tokens, features = lefts[0].shape
    block = 256
    left = pl.BlockSpec((tokens, block), lambda i: (0, i))

    def whole(values):
        return pl.BlockSpec(values.shape, lambda i: (0, 0), pipeline_mode=pl.Buffered(1))

    total = starts[5] + rights[4].shape[1]
    d_projected, attended, d_inner, d_gate, activated = rights
    return pl.pallas_call(
        functools.partial(weight_grad_kernel, starts),
        out_shape=jax.ShapeDtypeStruct((features, total), jnp.bfloat16),
        grid=(features // block,),
        in_specs=[left] * 4
        + [
            whole(d_projected),
            whole(attended),
            pl.BlockSpec((block, gains.shape[1]), lambda i: (i, 0)),
            whole(d_inner),
            whole(d_gate),
            whole(activated),
        ],
        out_specs=pl.BlockSpec((block, total), lambda i: (i, 0)),
        compiler_params=pltpu.CompilerParams(vmem_limit_bytes=kernel_vmem),
        cost_estimate=pl.CostEstimate(
            flops=2 * tokens * features * total,
            bytes_accessed=2 * (4 * tokens * features + (tokens + features) * total),
            transcendentals=0,
        ),
    )(*lefts, d_projected, attended, gains, d_inner, d_gate, activated)


def product(left, right, contract):
    return lax.dot_general(
        left, right, ((contract[:1], contract[1:]), ((), ())), preferred_element_type=jnp.float32
    )


def forward_layer(residual, weights, tables, is_local):
    w_qkv, w_out, w_inner, w_gate, w_down, gain_pair = weights
    lowered = layer_norm(residual, gain_pair[0]).astype(jnp.bfloat16)
    projected = product(lowered, w_qkv, (1, 0))
    attended = attend_forward(projected, tables, is_local)
    middle = residual + core_total(product(attended, w_out, (1, 1)))
    lowered_two = layer_norm(middle, gain_pair[1]).astype(jnp.bfloat16)
    inner = product(lowered_two, w_inner, (1, 0))
    gate_part = product(lowered_two, w_gate, (1, 0))
    activated = gelu_gate(inner, gate_part).astype(jnp.bfloat16)
    output = middle + core_total(product(activated, w_down, (1, 1)))
    kept = (residual, middle, lowered, lowered_two, projected, attended, inner, gate_part, activated)
    return (output, kept)


def backward_layer(upstream, weights, tables, kept, is_local, starts):
    w_qkv, w_out, w_inner, w_gate, w_down, gain_pair = weights
    residual, middle, lowered, lowered_two, projected, attended, inner, gate_part, activated = kept
    up_low = upstream.astype(jnp.bfloat16)
    d_activated = product(up_low, w_down, (1, 0))
    unused, pullback = jax.vjp(gelu_gate, inner, gate_part)
    d_inner, d_gate = [v.astype(jnp.bfloat16) for v in pullback(d_activated)]
    d_normed_two = core_total(
        product(d_inner, w_inner, (1, 1)) + product(d_gate, w_gate, (1, 1))
    )
    unused, pullback = jax.vjp(layer_norm, middle, gain_pair[1])
    d_mid_norm, d_gain_two = pullback(d_normed_two)
    d_middle = upstream + d_mid_norm
    d_branch = d_middle.astype(jnp.bfloat16)
    d_attended = product(d_branch, w_out, (1, 0)).astype(jnp.bfloat16)
    d_projected = attend_backward(projected, tables, d_attended, is_local)
    d_normed = core_total(product(d_projected, w_qkv, (1, 1)))
    unused, pullback = jax.vjp(layer_norm, residual, gain_pair[0])
    d_in_norm, d_gain_one = pullback(d_normed)
    gains = widen(jnp.stack([d_gain_one, d_gain_two], axis=1)).astype(jnp.bfloat16)
    packed = weight_grads(
        starts,
        (lowered, d_branch, lowered_two, up_low),
        (d_projected, attended, d_inner, d_gate, activated),
        gains,
    )
    return (d_middle + d_in_norm, packed)


def adam_update(weight, moment, square, gradient, step_rate, decay_here):
    moment_new = beta_one * moment + (1.0 - beta_one) * gradient
    square_new = beta_two * square + (1.0 - beta_two) * gradient * gradient
    moment_hat = moment_new / (1.0 - beta_one**STEP)
    square_hat = square_new / (1.0 - beta_two**STEP)
    updated = weight - step_rate * (
        moment_hat / (jnp.sqrt(square_hat) + adam_eps) + decay_here * weight
    )
    return (moment_new, square_new, updated)


def per_device(chips, hidden_in, cotangent, *state):
    masters = state[:5]
    moments = state[5:]
    same = lax.axis_index("core") == lax.axis_index("tensor")

    def chip_sequence(values):
        return jnp.where(same, values, core_swap(values)).astype(jnp.float32)

    def own_sequence(values):
        return jnp.where(same, values, lax.ppermute(values, every_axis, result_pairs(chips)))

    starts = layer_starts(masters)
    hidden = masters[2].shape[3]
    local_tables = rotary_tables(theta_local)
    global_tables = rotary_tables(theta_global)
    shards = [role_swap(pack_shards(masters, layer), chips) for layer in range(2)]
    hidden_in, shards = lax.optimization_barrier((hidden_in, shards))
    weights = [unpack_weights(gather_rows(s, chips), starts, hidden) for s in shards]
    inputs = chip_sequence(hidden_in)
    upstream = chip_sequence(cotangent)
    middle, kept_first = forward_layer(inputs, weights[0], local_tables, True)
    output, kept_second = forward_layer(middle, weights[1], global_tables, False)
    final_out = own_sequence(output.astype(jnp.bfloat16))
    d_middle, packed = backward_layer(
        upstream, weights[1], global_tables, kept_second, False, starts
    )
    grads_second = unpack_grads(scatter_rows(packed, chips), starts, hidden)
    d_values, packed = backward_layer(d_middle, weights[0], local_tables, kept_first, True, starts)
    grads_first = unpack_grads(scatter_rows(packed, chips), starts, hidden)
    final_grad = own_sequence(d_values.astype(jnp.bfloat16)).astype(jnp.float32)
    rates = (rate_qkv, rate_out, rate_inp, rate_down, rate_gain)
    results = [final_out, final_grad]
    for i, rate in enumerate(rates):
        gradient = jnp.stack([grads_first[i], grads_second[i]])
        decay = 0.0 if i == 4 else weight_decay
        results += adam_update(
            masters[i], moments[2 * i], moments[2 * i + 1], gradient, rate, decay
        )
    return tuple(results)


def solution(mesh):
    chips = mesh.shape["dp"] // 2
    fine = Mesh(mesh.devices.reshape(chips, 2, mesh.shape["tensor"]), every_axis)
    dp = ("chip", "core")
    tokens = P(dp, None)
    first = P(None, dp, None, "tensor")
    second = P(None, "tensor", dp)
    gain = P(None, None, dp)
    weights = (first, second, first, second, gain)
    pairs = tuple(s for s in weights for unused in range(2))
    triples = tuple(s for s in weights for unused in range(3))

    def body(*arguments):
        return per_device(chips, *arguments)

    return jax.shard_map(
        body,
        mesh=fine,
        in_specs=(tokens, tokens) + weights + pairs,
        out_specs=(tokens, tokens) + triples,
        check_vma=False,
    )
```

```python
import functools

import jax
import jax.numpy as jnp
from jax import lax
from jax.experimental import pallas as pl
from jax.experimental.pallas import tpu as pltpu
from jax.sharding import Mesh, PartitionSpec as P

HEAD_DIM = 64
HALF_WIN = 64
STEP = 10
SEQ_LEN = 1024


norm_eps = 1e-05
theta_local = 10000.0
theta_global = 160000.0
masked_score = -1e30
beta_one = 0.9
beta_two = 0.98
adam_eps = 1e-06
weight_decay = 1e-05
rate_qkv = 0.03
rate_out = 0.15
rate_inp = 0.03
rate_down = 0.02
rate_gain = 0.5

kernel_vmem = 48 * 1024 * 1024
every_axis = ("chip", "core", "tensor")
chip_axes = ("chip", "tensor")


def swap_pairs(chips):
    pairs = []
    for chip in range(chips):
        for core in range(2):
            for row in range(2):
                pairs.append((chip * 4 + core * 2 + row, chip * 4 + row * 2 + core))
    return pairs


def result_pairs(chips):
    return [(chip * 4 + c * 3, chip * 4 + c * 2 + 1 - c) for chip in range(chips) for c in range(2)]


def role_swap(values, chips):
    return lax.ppermute(values, every_axis, swap_pairs(chips))


def core_swap(values):
    return lax.ppermute(values, "core", [(0, 1), (1, 0)])


def core_total(partial_sum):
    own = partial_sum.astype(jnp.bfloat16)
    return own.astype(jnp.float32) + core_swap(own).astype(jnp.float32)


def layer_norm(values, gain):
    centred = values - jnp.mean(values, axis=-1, keepdims=True)
    spread = jnp.mean(centred * centred, axis=-1, keepdims=True)
    return centred * lax.rsqrt(spread + norm_eps) * gain


def rotary_tables(rotary_base):
    positions = jnp.arange(SEQ_LEN, dtype=jnp.int32)
    inverse = rotary_base ** (-jnp.arange(0, HEAD_DIM, 2, dtype=jnp.float32) / HEAD_DIM)
    angles = positions.astype(jnp.float32)[:, None] * inverse[None, :]
    cosine, sine = jnp.cos(angles), jnp.sin(angles)
    return (
        jnp.concatenate([cosine] * 4, axis=-1),
        jnp.concatenate([-sine, sine, -sine, sine], axis=-1),
    )


def gelu_gate(inner, gate_part):
    return jax.nn.gelu(inner, approximate=False) * gate_part


def group_bits(chips):
    return chips.bit_length() - 1


def bit_swap(values, bit, chips):
    if bit < 0:
        return lax.ppermute(values, "tensor", [(0, 1), (1, 0)])
    return lax.ppermute(values, "chip", [(chip, chip ^ (1 << bit)) for chip in range(chips)])


def own_bit(bit):
    if bit < 0:
        return lax.axis_index("tensor")
    return (lax.axis_index("chip") >> bit) & 1


def gather_bit(values, held, bit, chips):
    place = len([b for b in held if b > bit])
    other = bit_swap(values, bit, chips)
    is_low = own_bit(bit) == 0
    joined = jnp.stack(
        [jnp.where(is_low, values, other), jnp.where(is_low, other, values)], axis=place
    )
    return joined, sorted(held + [bit], reverse=True)


def reduce_bit(values, held, bit, chips):
    place = held.index(bit)
    mine = own_bit(bit)
    kept = lax.dynamic_index_in_dim(values, mine, place, keepdims=False)
    sent = lax.dynamic_index_in_dim(values, 1 - mine, place, keepdims=False)
    other = bit_swap(sent, bit, chips)
    total = (kept.astype(jnp.float32) + other.astype(jnp.float32)).astype(jnp.bfloat16)
    return total, [b for b in held if b != bit]


def half_columns(values):
    return values.shape[1] // 256 * 128


def gather_quick(shard, chips):
    values, held = shard, []
    cut = half_columns(shard)
    for bit in range(group_bits(chips) - 1, 0, -1):
        values, held = gather_bit(values, held, bit, chips)
    halves = []
    for order, part in (((0, -1), values[..., :cut]), ((-1, 0), values[..., cut:])):
        part_held = held
        for bit in order:
            part, part_held = gather_bit(part, part_held, bit, chips)
        halves.append(part.reshape(-1, part.shape[-1]))
    return jnp.concatenate(halves, axis=1)


def scatter_quick(gradient, chips):
    count = group_bits(chips)
    cut = half_columns(gradient)
    parts = []
    for order, part in (((-1, 0), gradient[:, :cut]), ((0, -1), gradient[:, cut:])):
        held = list(range(count - 1, -2, -1))
        values = part.reshape([2] * len(held) + [-1, part.shape[-1]])
        for bit in order:
            values, held = reduce_bit(values, held, bit, chips)
        parts.append(values)
    values = jnp.concatenate(parts, axis=-1)
    for bit in range(1, count):
        values, held = reduce_bit(values, held, bit, chips)
    return values


def gather_rows(shard, chips):
    return lax.all_gather(shard, chip_axes, axis=0, tiled=True)


def scatter_rows(gradient, chips):
    return lax.psum_scatter(gradient, chip_axes, scatter_dimension=0, tiled=True)


def padded_width(width):
    return -(-width // 128) * 128


def widen(values):
    width = values.shape[1]
    return jnp.pad(values, ((0, 0), (0, padded_width(width) - width)))


def layer_starts(masters):
    heads = masters[0].shape[3]
    step = padded_width(masters[2].shape[3])
    return (0, 3 * heads, 4 * heads, 4 * heads + 128, 4 * heads + 128 + step, 4 * heads + 128 + 2 * step)


def pair_major(values):
    rows, kinds, width = values.shape
    wide = 2 * HEAD_DIM
    return values.reshape(rows, kinds, width // wide, wide).swapaxes(1, 2).reshape(rows, -1)


def kind_major(values):
    rows, wide = values.shape[0], 2 * HEAD_DIM
    return values.reshape(rows, -1, 3, wide).swapaxes(1, 2).reshape(rows, 3, -1)


def pack_shards(masters, layer):
    qkv, out, inp, down, gains = [m[layer].astype(jnp.bfloat16) for m in masters]
    return jnp.concatenate(
        [pair_major(qkv), out.T, widen(gains.T), widen(inp[:, 0]), widen(inp[:, 1]), down.T], axis=1
    )


def split_packed(packed, starts):
    return packed[:, : starts[3]], packed[:, starts[3] :]


def unpack_weights(heads_part, hidden_part, starts, hidden):
    step = starts[4] - starts[3]
    return (
        heads_part[:, : starts[1]],
        heads_part[:, starts[1] : starts[2]],
        hidden_part[:, :hidden],
        hidden_part[:, step : step + hidden],
        hidden_part[:, 2 * step :],
        heads_part[:, starts[2] : starts[2] + 2].T.astype(jnp.float32),
    )


def unpack_grads(packed, starts, hidden):
    inner = packed[:, starts[3] : starts[3] + hidden]
    gate = packed[:, starts[4] : starts[4] + hidden]
    return (
        kind_major(packed[:, : starts[1]]),
        packed[:, starts[1] : starts[2]].T,
        jnp.stack([inner, gate], axis=1),
        packed[:, starts[5] :].T,
        packed[:, starts[2] : starts[2] + 2].T,
    )


def rolled(values):
    lane = lax.broadcasted_iota(jnp.int32, values.shape, 1) % HEAD_DIM
    half = HEAD_DIM // 2
    width = values.shape[1]
    return jnp.where(
        lane < half, pltpu.roll(values, width - half, 1), pltpu.roll(values, half, 1)
    )


def pair_stack(values):
    lane = lax.broadcasted_iota(jnp.int32, values.shape, 1)
    nothing = jnp.zeros_like(values)
    return jnp.concatenate(
        [jnp.where(lane < HEAD_DIM, values, nothing), jnp.where(lane < HEAD_DIM, nothing, values)],
        axis=0,
    )


def pair_unstack(values):
    rows = values.shape[1] // 2
    return jnp.concatenate(
        [values[:HEAD_DIM, :rows], values[HEAD_DIM:, rows:]], axis=0
    ).T


def probability_block(keys_here, stacked, start, is_local, length):
    scores = (
        lax.dot_general(
            keys_here, stacked, (((1,), (1,)), ((), ())), preferred_element_type=jnp.float32
        )
        * 0.125
    )
    if is_local:
        rows = stacked.shape[0] // 2
        key_at = start - HALF_WIN + lax.broadcasted_iota(jnp.int32, scores.shape, 0)
        query_at = start + lax.broadcasted_iota(jnp.int32, scores.shape, 1) % rows
        allowed = (jnp.abs(query_at - key_at) <= HALF_WIN) & (key_at >= 0) & (key_at < length)
        scores = jnp.where(allowed, scores, masked_score)
    exponent = jnp.exp(scores - jnp.max(scores, axis=0, keepdims=True))
    return exponent * (1.0 / jnp.sum(exponent, axis=0, keepdims=True))


def attend_kernel(is_local, block, raw_ref, cos_ref, sin_ref, out_ref, keys, values_t):
    length = raw_ref.shape[0]
    pad = HALF_WIN if is_local else 0
    reach = block + 2 * HALF_WIN if is_local else length
    wide = 2 * HEAD_DIM
    raw_keys = raw_ref[:, wide : 2 * wide]
    rotated = (raw_keys * cos_ref[...] + rolled(raw_keys) * sin_ref[...]).astype(jnp.bfloat16)
    if is_local:
        keys[...] = jnp.zeros_like(keys)
        values_t[...] = jnp.zeros_like(values_t)
    keys[pl.ds(pad, length), :] = rotated
    values_t[:, pl.ds(pad, length)] = raw_ref[:, 2 * wide :].astype(jnp.bfloat16).T

    def step(i):
        start = pl.multiple_of(i * block, block)
        at = start if is_local else 0
        part = raw_ref[pl.ds(start, block), :wide]
        here = pl.ds(start, block)
        query = (part * cos_ref[here, :] + rolled(part) * sin_ref[here, :]).astype(jnp.bfloat16)
        probability = probability_block(
            keys[pl.ds(at, reach), :], pair_stack(query), start, is_local, length
        )
        mixed = jnp.dot(
            values_t[:, pl.ds(at, reach)],
            probability.astype(jnp.bfloat16),
            preferred_element_type=jnp.float32,
        )
        out_ref[here, :] = pair_unstack(mixed).astype(jnp.bfloat16)

    pl.loop(0, length // block, unroll=2)(step)


def attend_back_kernel(
    is_local, block, raw_ref, cos_ref, sin_ref, up_ref, out_ref, keys, keys_t, values, d_keys, d_values
):
    length = raw_ref.shape[0]
    pad = HALF_WIN if is_local else 0
    reach = block + 2 * HALF_WIN if is_local else length
    wide = 2 * HEAD_DIM
    raw_keys = raw_ref[:, wide : 2 * wide]
    rotated = (raw_keys * cos_ref[...] + rolled(raw_keys) * sin_ref[...]).astype(jnp.bfloat16)
    if is_local:
        keys[...] = jnp.zeros_like(keys)
        keys_t[...] = jnp.zeros_like(keys_t)
        values[...] = jnp.zeros_like(values)
    keys[pl.ds(pad, length), :] = rotated
    keys_t[:, pl.ds(pad, length)] = rotated.T
    values[pl.ds(pad, length), :] = raw_ref[:, 2 * wide :].astype(jnp.bfloat16)
    d_keys[...] = jnp.zeros_like(d_keys)
    d_values[...] = jnp.zeros_like(d_values)

    def step(i):
        start = pl.multiple_of(i * block, block)
        at = start if is_local else 0
        here = pl.ds(start, block)
        band = pl.ds(at, reach)
        part = raw_ref[here, :wide]
        query = (part * cos_ref[here, :] + rolled(part) * sin_ref[here, :]).astype(jnp.bfloat16)
        stacked = pair_stack(query)
        upstream = pair_stack(up_ref[here, :])
        probability = probability_block(keys[band, :], stacked, start, is_local, length)
        d_values[band, :] += jnp.dot(
            probability.astype(jnp.bfloat16), upstream, preferred_element_type=jnp.float32
        )
        d_probability = lax.dot_general(
            values[band, :], upstream, (((1,), (1,)), ((), ())), preferred_element_type=jnp.float32
        )
        centre = jnp.sum(probability * d_probability, axis=0, keepdims=True)
        d_scores = (probability * (d_probability - centre)).astype(jnp.bfloat16)
        d_keys[band, :] += jnp.dot(d_scores, stacked, preferred_element_type=jnp.float32)
        d_query = (
            pair_unstack(
                jnp.dot(keys_t[:, band], d_scores, preferred_element_type=jnp.float32)
            )
            * 0.125
        )
        out_ref[here, :wide] = (
            d_query * cos_ref[here, :] - rolled(d_query) * sin_ref[here, :]
        ).astype(jnp.bfloat16)

    pl.loop(0, length // block, unroll=2)(step)
    d_key = d_keys[pl.ds(pad, length), :] * 0.125
    out_ref[:, wide : 2 * wide] = (d_key * cos_ref[...] - rolled(d_key) * sin_ref[...]).astype(
        jnp.bfloat16
    )
    out_ref[:, 2 * wide :] = d_values[pl.ds(pad, length), :].astype(jnp.bfloat16)


def attend_specs(projected):
    rows, columns = projected.shape
    wide = 2 * HEAD_DIM
    raw = pl.BlockSpec((SEQ_LEN, 3 * wide), lambda s, j: (s, j))
    table = pl.BlockSpec((SEQ_LEN, wide), lambda s, j: (0, 0))
    narrow = pl.BlockSpec((SEQ_LEN, wide), lambda s, j: (s, j))
    grid = (rows // SEQ_LEN, columns // (3 * wide))
    return grid, raw, table, narrow


def attend_cost(projected, is_local, products):
    rows, columns = projected.shape
    reach = 4 * HALF_WIN if is_local else SEQ_LEN
    pairs = columns // (6 * HEAD_DIM)
    cells = rows * reach * pairs * 2
    return pl.CostEstimate(
        flops=cells * 8 * HEAD_DIM * products,
        bytes_accessed=projected.size * 8,
        transcendentals=cells,
    )


def attend_forward(projected, tables, is_local):
    rows, columns = projected.shape
    wide = 2 * HEAD_DIM
    grid, raw, table, narrow = attend_specs(projected)
    span = SEQ_LEN + 2 * HALF_WIN if is_local else SEQ_LEN
    return pl.pallas_call(
        functools.partial(attend_kernel, is_local, 128),
        out_shape=jax.ShapeDtypeStruct((rows, columns // 3), jnp.bfloat16),
        grid=grid,
        in_specs=[raw, table, table],
        out_specs=narrow,
        scratch_shapes=[
            pltpu.VMEM((span, wide), jnp.bfloat16),
            pltpu.VMEM((wide, span), jnp.bfloat16),
        ],
        compiler_params=pltpu.CompilerParams(vmem_limit_bytes=kernel_vmem),
        cost_estimate=attend_cost(projected, is_local, 2),
    )(projected, *tables)


def attend_backward(projected, tables, d_attended, is_local):
    rows, columns = projected.shape
    wide = 2 * HEAD_DIM
    grid, raw, table, narrow = attend_specs(projected)
    span = SEQ_LEN + 2 * HALF_WIN if is_local else SEQ_LEN
    return pl.pallas_call(
        functools.partial(attend_back_kernel, is_local, 128),
        out_shape=jax.ShapeDtypeStruct((rows, columns), jnp.bfloat16),
        grid=grid,
        in_specs=[raw, table, table, narrow],
        out_specs=raw,
        scratch_shapes=[
            pltpu.VMEM((span, wide), jnp.bfloat16),
            pltpu.VMEM((wide, span), jnp.bfloat16),
            pltpu.VMEM((span, wide), jnp.bfloat16),
            pltpu.VMEM((span, wide), jnp.float32),
            pltpu.VMEM((span, wide), jnp.float32),
        ],
        compiler_params=pltpu.CompilerParams(vmem_limit_bytes=kernel_vmem),
        cost_estimate=attend_cost(projected, is_local, 5),
    )(projected, *tables, d_attended)


def weight_grad_kernel(choice, starts, total, left_count, *refs):
    lefts = [ref[...] for ref in refs[:left_count]]
    rights, out_ref = refs[left_count:-1], refs[-1]
    for right, which, start, stop in zip(rights, choice, starts, list(starts[1:]) + [total]):
        filled = start + right.shape[1]
        if which is None:
            out_ref[:, start:filled] = right[...]
        else:
            out_ref[:, start:filled] = lax.dot_general(
                lefts[which],
                right[...],
                (((0,), (0,)), ((), ())),
                preferred_element_type=jnp.float32,
            ).astype(jnp.bfloat16)
        if filled < stop:
            out_ref[:, filled:stop] = jnp.zeros((out_ref.shape[0], stop - filled), jnp.bfloat16)


def weight_grads(lefts, rights, choice):
    tokens, features = lefts[0].shape
    block = 256
    starts, total = [], 0
    for right in rights:
        total = padded_width(total)
        starts.append(total)
        total += right.shape[1]
    specs = [pl.BlockSpec((tokens, block), lambda i: (0, i))] * len(lefts)
    for right, which in zip(rights, choice):
        if which is None:
            specs.append(pl.BlockSpec((block, right.shape[1]), lambda i: (i, 0)))
        else:
            specs.append(
                pl.BlockSpec(right.shape, lambda i: (0, 0), pipeline_mode=pl.Buffered(1))
            )
    return pl.pallas_call(
        functools.partial(weight_grad_kernel, choice, tuple(starts), total, len(lefts)),
        out_shape=jax.ShapeDtypeStruct((features, total), jnp.bfloat16),
        grid=(features // block,),
        in_specs=specs,
        out_specs=pl.BlockSpec((block, total), lambda i: (i, 0)),
        compiler_params=pltpu.CompilerParams(vmem_limit_bytes=kernel_vmem),
        cost_estimate=pl.CostEstimate(
            flops=2 * tokens * features * total,
            bytes_accessed=2 * (len(lefts) * tokens * features + (tokens + features) * total),
            transcendentals=0,
        ),
    )(*lefts, *rights)


def product(left, right, contract):
    return lax.dot_general(
        left, right, ((contract[:1], contract[1:]), ((), ())), preferred_element_type=jnp.float32
    )


def forward_layer(residual, weights, tables, is_local):
    w_qkv, w_out, w_inner, w_gate, w_down, gain_pair = weights
    lowered = layer_norm(residual, gain_pair[0]).astype(jnp.bfloat16)
    projected = product(lowered, w_qkv, (1, 0))
    attended = attend_forward(projected, tables, is_local)
    middle = residual + core_total(product(attended, w_out, (1, 1)))
    lowered_two = layer_norm(middle, gain_pair[1]).astype(jnp.bfloat16)
    inner = product(lowered_two, w_inner, (1, 0))
    gate_part = product(lowered_two, w_gate, (1, 0))
    activated = gelu_gate(inner, gate_part).astype(jnp.bfloat16)
    output = middle + core_total(product(activated, w_down, (1, 1)))
    kept = (residual, middle, lowered, lowered_two, projected, attended, inner, gate_part, activated)
    return (output, kept)


def backward_layer(upstream, weights, tables, kept, is_local, scatter):
    w_qkv, w_out, w_inner, w_gate, w_down, gain_pair = weights
    residual, middle, lowered, lowered_two, projected, attended, inner, gate_part, activated = kept
    up_low = upstream.astype(jnp.bfloat16)
    d_activated = product(up_low, w_down, (1, 0))
    unused, pullback = jax.vjp(gelu_gate, inner, gate_part)
    d_inner, d_gate = [v.astype(jnp.bfloat16) for v in pullback(d_activated)]
    hidden_grads = weight_grads((lowered_two, up_low), (d_inner, d_gate, activated), (0, 0, 1))
    d_normed_two = core_total(
        product(d_inner, w_inner, (1, 1)) + product(d_gate, w_gate, (1, 1))
    )
    unused, pullback = jax.vjp(layer_norm, middle, gain_pair[1])
    d_mid_norm, d_gain_two = pullback(d_normed_two)
    d_middle = upstream + d_mid_norm
    d_branch = d_middle.astype(jnp.bfloat16)
    d_attended = product(d_branch, w_out, (1, 0)).astype(jnp.bfloat16)
    d_attended, hidden_grads = lax.optimization_barrier((d_attended, hidden_grads))
    hidden_grads = scatter(hidden_grads)
    d_projected = attend_backward(projected, tables, d_attended, is_local)
    d_normed = core_total(product(d_projected, w_qkv, (1, 1)))
    unused, pullback = jax.vjp(layer_norm, residual, gain_pair[0])
    d_in_norm, d_gain_one = pullback(d_normed)
    gains = widen(jnp.stack([d_gain_one, d_gain_two], axis=1)).astype(jnp.bfloat16)
    head_grads = scatter(
        weight_grads((lowered, d_branch), (d_projected, attended, gains), (0, 1, None))
    )
    return (d_middle + d_in_norm, (head_grads, hidden_grads))


def adam_update(weight, moment, square, gradient, step_rate, decay_here):
    moment_new = beta_one * moment + (1.0 - beta_one) * gradient
    square_new = beta_two * square + (1.0 - beta_two) * gradient * gradient
    moment_hat = moment_new / (1.0 - beta_one**STEP)
    square_hat = square_new / (1.0 - beta_two**STEP)
    updated = weight - step_rate * (
        moment_hat / (jnp.sqrt(square_hat) + adam_eps) + decay_here * weight
    )
    return (moment_new, square_new, updated)


def per_device(chips, hidden_in, cotangent, *state):
    masters = state[:5]
    moments = state[5:]
    same = lax.axis_index("core") == lax.axis_index("tensor")

    def chip_sequence(values):
        return jnp.where(same, values, core_swap(values)).astype(jnp.float32)

    def own_sequence(values):
        return jnp.where(same, values, lax.ppermute(values, every_axis, result_pairs(chips)))

    starts = layer_starts(masters)
    hidden = masters[2].shape[3]
    local_tables = rotary_tables(theta_local)
    global_tables = rotary_tables(theta_global)
    packed = [pack_shards(masters, layer) for layer in range(2)]
    heads_part = role_swap(packed[0][:, : starts[3]], chips)
    hidden_part = role_swap(packed[0][:, starts[3] :], chips)
    second = role_swap(packed[1], chips)
    hidden_in, heads_part, hidden_part, second = lax.optimization_barrier(
        (hidden_in, heads_part, hidden_part, second)
    )
    first = [gather_quick(part, chips) for part in (heads_part, hidden_part)]
    weights = [
        unpack_weights(first[0], first[1], starts, hidden),
        unpack_weights(*split_packed(gather_rows(second, chips), starts), starts, hidden),
    ]
    inputs = chip_sequence(hidden_in)
    upstream = chip_sequence(cotangent)
    middle, kept_first = forward_layer(inputs, weights[0], local_tables, True)
    output, kept_second = forward_layer(middle, weights[1], global_tables, False)
    final_out = own_sequence(output.astype(jnp.bfloat16))
    by_call = functools.partial(scatter_rows, chips=chips)
    by_steps = functools.partial(scatter_quick, chips=chips)
    d_middle, shards_second = backward_layer(
        upstream, weights[1], global_tables, kept_second, False, by_call
    )
    d_values, shards_first = backward_layer(
        d_middle, weights[0], local_tables, kept_first, True, by_steps
    )
    shards_first = role_swap(jnp.concatenate(shards_first, axis=1), chips)
    shards_first, shards_second = lax.optimization_barrier((shards_first, shards_second))
    shards_second = role_swap(jnp.concatenate(shards_second, axis=1), chips)
    grads_first, grads_second = [
        unpack_grads(packed.astype(jnp.float32), starts, hidden)
        for packed in (shards_first, shards_second)
    ]
    final_grad = own_sequence(d_values.astype(jnp.bfloat16)).astype(jnp.float32)
    rates = (rate_qkv, rate_out, rate_inp, rate_down, rate_gain)
    results = [final_out, final_grad]
    for i, rate in enumerate(rates):
        gradient = jnp.stack([grads_first[i], grads_second[i]])
        decay = 0.0 if i == 4 else weight_decay
        results += adam_update(
            masters[i], moments[2 * i], moments[2 * i + 1], gradient, rate, decay
        )
    return tuple(results)


def solution(mesh):
    chips = mesh.shape["dp"] // 2
    fine = Mesh(mesh.devices.reshape(chips, 2, mesh.shape["tensor"]), every_axis)
    dp = ("chip", "core")
    tokens = P(dp, None)
    first = P(None, dp, None, "tensor")
    second = P(None, "tensor", dp)
    gain = P(None, None, dp)
    weights = (first, second, first, second, gain)
    pairs = tuple(s for s in weights for unused in range(2))
    triples = tuple(s for s in weights for unused in range(3))

    def body(*arguments):
        return per_device(chips, *arguments)

    return jax.shard_map(
        body,
        mesh=fine,
        in_specs=(tokens, tokens) + weights + pairs,
        out_specs=(tokens, tokens) + triples,
        check_vma=False,
    )
```

```python
import functools

import jax
import jax.numpy as jnp
from jax import lax
from jax.experimental import pallas as pl
from jax.experimental.pallas import tpu as pltpu
from jax.sharding import Mesh, PartitionSpec as P

HEAD_DIM = 64
HALF_WIN = 64
STEP = 10
SEQ_LEN = 1024


norm_eps = 1e-05
theta_local = 10000.0
theta_global = 160000.0
masked_score = -1e30
beta_one = 0.9
beta_two = 0.98
adam_eps = 1e-06
weight_decay = 1e-05
rate_qkv = 0.03
rate_out = 0.15
rate_inp = 0.03
rate_down = 0.02
rate_gain = 0.5

kernel_vmem = 48 * 1024 * 1024
every_axis = ("chip", "core", "tensor")
chip_axes = ("chip", "tensor")


def swap_pairs(chips):
    pairs = []
    for chip in range(chips):
        for core in range(2):
            for row in range(2):
                pairs.append((chip * 4 + core * 2 + row, chip * 4 + row * 2 + core))
    return pairs


def result_pairs(chips):
    return [(chip * 4 + c * 3, chip * 4 + c * 2 + 1 - c) for chip in range(chips) for c in range(2)]


def role_swap(values, chips):
    return lax.ppermute(values, every_axis, swap_pairs(chips))


def swap_after(values, earlier, chips):
    width = values.shape[1]
    return role_swap(jnp.concatenate([values, earlier[:, :128]], axis=1), chips)[:, :width]


def core_swap(values):
    return lax.ppermute(values, "core", [(0, 1), (1, 0)])


def core_total(partial_sum):
    own = partial_sum.astype(jnp.bfloat16)
    return own.astype(jnp.float32) + core_swap(own).astype(jnp.float32)


def layer_norm(values, gain):
    centred = values - jnp.mean(values, axis=-1, keepdims=True)
    spread = jnp.mean(centred * centred, axis=-1, keepdims=True)
    return centred * lax.rsqrt(spread + norm_eps) * gain


def rotary_tables(rotary_base):
    positions = jnp.arange(SEQ_LEN, dtype=jnp.int32)
    inverse = rotary_base ** (-jnp.arange(0, HEAD_DIM, 2, dtype=jnp.float32) / HEAD_DIM)
    angles = positions.astype(jnp.float32)[:, None] * inverse[None, :]
    cosine, sine = jnp.cos(angles), jnp.sin(angles)
    return (
        jnp.concatenate([cosine] * 4, axis=-1),
        jnp.concatenate([-sine, sine, -sine, sine], axis=-1),
    )


def gelu_gate(inner, gate_part):
    return jax.nn.gelu(inner, approximate=False) * gate_part


def group_bits(chips):
    return chips.bit_length() - 1


def bit_swap(values, bit, chips):
    if bit < 0:
        return lax.ppermute(values, "tensor", [(0, 1), (1, 0)])
    return lax.ppermute(values, "chip", [(chip, chip ^ (1 << bit)) for chip in range(chips)])


def own_bit(bit):
    if bit < 0:
        return lax.axis_index("tensor")
    return (lax.axis_index("chip") >> bit) & 1


def gather_bit(values, held, bit, chips):
    place = len([b for b in held if b > bit])
    other = bit_swap(values, bit, chips)
    is_low = own_bit(bit) == 0
    joined = jnp.stack(
        [jnp.where(is_low, values, other), jnp.where(is_low, other, values)], axis=place
    )
    return joined, sorted(held + [bit], reverse=True)


def exchange_bit(values, held, bit, chips):
    place = held.index(bit)
    mine = own_bit(bit)
    kept = lax.dynamic_index_in_dim(values, mine, place, keepdims=False)
    sent = lax.dynamic_index_in_dim(values, 1 - mine, place, keepdims=False)
    return kept, bit_swap(sent, bit, chips), [b for b in held if b != bit]


def add_halves(kept, other):
    return (kept.astype(jnp.float32) + other.astype(jnp.float32)).astype(jnp.bfloat16)


def reduce_bit(values, held, bit, chips):
    kept, other, held = exchange_bit(values, held, bit, chips)
    return add_halves(kept, other), held


def half_columns(values):
    return values.shape[1] // 256 * 128


def gather_quick(shard, chips):
    values, held = shard, []
    cut = half_columns(shard)
    for bit in range(group_bits(chips) - 1, 0, -1):
        values, held = gather_bit(values, held, bit, chips)
    halves = []
    for order, part in (((0, -1), values[..., :cut]), ((-1, 0), values[..., cut:])):
        part_held = held
        for bit in order:
            part, part_held = gather_bit(part, part_held, bit, chips)
        halves.append(part.reshape(-1, part.shape[-1]))
    return jnp.concatenate(halves, axis=1)


def quick_begin(gradient, chips):
    held = list(range(group_bits(chips) - 1, -2, -1))
    cut = half_columns(gradient)
    begun = []
    for bit, part in ((-1, gradient[:, :cut]), (0, gradient[:, cut:])):
        values = part.reshape([2] * len(held) + [-1, part.shape[-1]])
        begun.append(exchange_bit(values, held, bit, chips))
    return begun


def quick_finish(begun, chips):
    parts = []
    for bit, (kept, other, held) in zip((0, -1), begun):
        values, held = reduce_bit(add_halves(kept, other), held, bit, chips)
        parts.append(values)
    values = jnp.concatenate(parts, axis=-1)
    for bit in range(1, group_bits(chips)):
        values, held = reduce_bit(values, held, bit, chips)
    return values


def gather_rows(shard, chips):
    return lax.all_gather(shard, chip_axes, axis=0, tiled=True)


def scatter_rows(gradient, chips):
    return lax.psum_scatter(gradient, chip_axes, scatter_dimension=0, tiled=True)


def padded_width(width):
    return -(-width // 128) * 128


def widen(values):
    width = values.shape[1]
    return jnp.pad(values, ((0, 0), (0, padded_width(width) - width)))


def layer_starts(masters):
    heads = masters[0].shape[3]
    step = padded_width(masters[2].shape[3])
    return (0, 3 * heads, 4 * heads, 4 * heads + 128, 4 * heads + 128 + step, 4 * heads + 128 + 2 * step)


def pair_major(values):
    rows, kinds, width = values.shape
    wide = 2 * HEAD_DIM
    return values.reshape(rows, kinds, width // wide, wide).swapaxes(1, 2).reshape(rows, -1)


def kind_major(values):
    rows, wide = values.shape[0], 2 * HEAD_DIM
    return values.reshape(rows, -1, 3, wide).swapaxes(1, 2).reshape(rows, 3, -1)


def pack_shards(masters, layer):
    qkv, out, inp, down, gains = [m[layer].astype(jnp.bfloat16) for m in masters]
    return jnp.concatenate(
        [pair_major(qkv), out.T, widen(gains.T), widen(inp[:, 0]), widen(inp[:, 1]), down.T], axis=1
    )


def split_packed(packed, starts):
    return packed[:, : starts[3]], packed[:, starts[3] :]


def unpack_weights(heads_part, hidden_part, starts, hidden):
    step = starts[4] - starts[3]
    return (
        heads_part[:, : starts[1]],
        heads_part[:, starts[1] : starts[2]],
        hidden_part[:, :hidden],
        hidden_part[:, step : step + hidden],
        hidden_part[:, 2 * step :],
        heads_part[:, starts[2] : starts[2] + 2].T.astype(jnp.float32),
    )


def unpack_grads(packed, starts, hidden):
    inner = packed[:, starts[3] : starts[3] + hidden]
    gate = packed[:, starts[4] : starts[4] + hidden]
    return (
        kind_major(packed[:, : starts[1]]),
        packed[:, starts[1] : starts[2]].T,
        jnp.stack([inner, gate], axis=1),
        packed[:, starts[5] :].T,
        packed[:, starts[2] : starts[2] + 2].T,
    )


def rolled(values):
    lane = lax.broadcasted_iota(jnp.int32, values.shape, 1) % HEAD_DIM
    half = HEAD_DIM // 2
    width = values.shape[1]
    return jnp.where(
        lane < half, pltpu.roll(values, width - half, 1), pltpu.roll(values, half, 1)
    )


def pair_stack(values):
    lane = lax.broadcasted_iota(jnp.int32, values.shape, 1)
    nothing = jnp.zeros_like(values)
    return jnp.concatenate(
        [jnp.where(lane < HEAD_DIM, values, nothing), jnp.where(lane < HEAD_DIM, nothing, values)],
        axis=0,
    )


def pair_unstack(values):
    rows = values.shape[1] // 2
    return jnp.concatenate(
        [values[:HEAD_DIM, :rows], values[HEAD_DIM:, rows:]], axis=0
    ).T


def probability_block(keys_here, stacked, start, is_local, length):
    scores = lax.dot_general(
        keys_here, stacked, (((1,), (1,)), ((), ())), preferred_element_type=jnp.float32
    )
    if is_local:
        rows = stacked.shape[0] // 2
        key_at = start - HALF_WIN + lax.broadcasted_iota(jnp.int32, scores.shape, 0)
        query_at = start + lax.broadcasted_iota(jnp.int32, scores.shape, 1) % rows
        allowed = (jnp.abs(query_at - key_at) <= HALF_WIN) & (key_at >= 0) & (key_at < length)
        scores = jnp.where(allowed, scores, masked_score)
    exponent = jnp.exp(scores - jnp.max(scores, axis=0, keepdims=True))
    return exponent * (1.0 / jnp.sum(exponent, axis=0, keepdims=True))


def attend_kernel(is_local, block, raw_ref, cos_ref, sin_ref, out_ref, keys, values_t):
    length = raw_ref.shape[0]
    pad = HALF_WIN if is_local else 0
    reach = block + 2 * HALF_WIN if is_local else length
    wide = 2 * HEAD_DIM
    raw_keys = raw_ref[:, wide : 2 * wide]
    rotated = (raw_keys * cos_ref[...] + rolled(raw_keys) * sin_ref[...]).astype(jnp.bfloat16)
    if is_local:
        keys[...] = jnp.zeros_like(keys)
        values_t[...] = jnp.zeros_like(values_t)
    keys[pl.ds(pad, length), :] = rotated
    values_t[:, pl.ds(pad, length)] = raw_ref[:, 2 * wide :].astype(jnp.bfloat16).T

    def step(i):
        start = pl.multiple_of(i * block, block)
        at = start if is_local else 0
        part = raw_ref[pl.ds(start, block), :wide]
        here = pl.ds(start, block)
        query = (part * cos_ref[here, :] + rolled(part) * sin_ref[here, :]).astype(
            jnp.bfloat16
        ) * jnp.bfloat16(0.125)
        probability = probability_block(
            keys[pl.ds(at, reach), :], pair_stack(query), start, is_local, length
        )
        mixed = jnp.dot(
            values_t[:, pl.ds(at, reach)],
            probability.astype(jnp.bfloat16),
            preferred_element_type=jnp.float32,
        )
        out_ref[here, :] = pair_unstack(mixed).astype(jnp.bfloat16)

    pl.loop(0, length // block, unroll=2)(step)


def attend_back_kernel(is_local, block, raw_ref, cos_ref, sin_ref, up_ref, *refs):
    out_ref, keys, keys_t, values, d_keys, d_values = refs[-6:]
    length = raw_ref.shape[0]
    pad = HALF_WIN if is_local else 0
    reach = block + 2 * HALF_WIN if is_local else length
    wide = 2 * HEAD_DIM
    raw_keys = raw_ref[:, wide : 2 * wide]
    rotated = (raw_keys * cos_ref[...] + rolled(raw_keys) * sin_ref[...]).astype(jnp.bfloat16)
    if is_local:
        keys[...] = jnp.zeros_like(keys)
        keys_t[...] = jnp.zeros_like(keys_t)
        values[...] = jnp.zeros_like(values)
    keys[pl.ds(pad, length), :] = rotated
    keys_t[:, pl.ds(pad, length)] = (rotated * jnp.bfloat16(0.125)).T
    values[pl.ds(pad, length), :] = raw_ref[:, 2 * wide :].astype(jnp.bfloat16)
    d_keys[...] = jnp.zeros_like(d_keys)
    d_values[...] = jnp.zeros_like(d_values)

    def step(i):
        start = pl.multiple_of(i * block, block)
        at = start if is_local else 0
        here = pl.ds(start, block)
        band = pl.ds(at, reach)
        part = raw_ref[here, :wide]
        query = (part * cos_ref[here, :] + rolled(part) * sin_ref[here, :]).astype(
            jnp.bfloat16
        ) * jnp.bfloat16(0.125)
        stacked = pair_stack(query)
        upstream = pair_stack(up_ref[here, :])
        probability = probability_block(keys[band, :], stacked, start, is_local, length)
        d_values[band, :] += jnp.dot(
            probability.astype(jnp.bfloat16), upstream, preferred_element_type=jnp.float32
        )
        d_probability = lax.dot_general(
            values[band, :], upstream, (((1,), (1,)), ((), ())), preferred_element_type=jnp.float32
        )
        centre = jnp.sum(probability * d_probability, axis=0, keepdims=True)
        d_scores = (probability * (d_probability - centre)).astype(jnp.bfloat16)
        d_keys[band, :] += jnp.dot(d_scores, stacked, preferred_element_type=jnp.float32)
        d_query = pair_unstack(
            jnp.dot(keys_t[:, band], d_scores, preferred_element_type=jnp.float32)
        )
        out_ref[here, :wide] = (
            d_query * cos_ref[here, :] - rolled(d_query) * sin_ref[here, :]
        ).astype(jnp.bfloat16)

    pl.loop(0, length // block, unroll=2)(step)
    d_key = d_keys[pl.ds(pad, length), :]
    out_ref[:, wide : 2 * wide] = (d_key * cos_ref[...] - rolled(d_key) * sin_ref[...]).astype(
        jnp.bfloat16
    )
    out_ref[:, 2 * wide :] = d_values[pl.ds(pad, length), :].astype(jnp.bfloat16)


def attend_specs(projected, part=0, parts=1):
    rows, columns = projected.shape
    wide = 2 * HEAD_DIM
    pairs = columns // (3 * wide) // parts
    skipped = part * pairs
    raw = pl.BlockSpec((SEQ_LEN, 3 * wide), lambda s, j: (s, j + skipped))
    table = pl.BlockSpec((SEQ_LEN, wide), lambda s, j: (0, 0))
    narrow = pl.BlockSpec((SEQ_LEN, wide), lambda s, j: (s, j + skipped))
    return (rows // SEQ_LEN, pairs), raw, table, narrow


def attend_cost(projected, is_local, products):
    rows, columns = projected.shape
    reach = 4 * HALF_WIN if is_local else SEQ_LEN
    pairs = columns // (6 * HEAD_DIM)
    cells = rows * reach * pairs * 2
    return pl.CostEstimate(
        flops=cells * 8 * HEAD_DIM * products,
        bytes_accessed=projected.size * 8,
        transcendentals=cells,
    )


def attend_forward(projected, tables, is_local):
    rows, columns = projected.shape
    wide = 2 * HEAD_DIM
    grid, raw, table, narrow = attend_specs(projected)
    span = SEQ_LEN + 2 * HALF_WIN if is_local else SEQ_LEN
    return pl.pallas_call(
        functools.partial(attend_kernel, is_local, 128),
        out_shape=jax.ShapeDtypeStruct((rows, columns // 3), jnp.bfloat16),
        grid=grid,
        in_specs=[raw, table, table],
        out_specs=narrow,
        scratch_shapes=[
            pltpu.VMEM((span, wide), jnp.bfloat16),
            pltpu.VMEM((wide, span), jnp.bfloat16),
        ],
        compiler_params=pltpu.CompilerParams(vmem_limit_bytes=kernel_vmem),
        cost_estimate=attend_cost(projected, is_local, 2),
    )(projected, *tables)


def attend_backward(projected, tables, d_attended, is_local, part, after=()):
    rows, columns = projected.shape
    wide = 2 * HEAD_DIM
    grid, raw, table, narrow = attend_specs(projected, part, 2)
    span = SEQ_LEN + 2 * HALF_WIN if is_local else SEQ_LEN
    return pl.pallas_call(
        functools.partial(attend_back_kernel, is_local, 128),
        out_shape=jax.ShapeDtypeStruct((rows, columns // 2), jnp.bfloat16),
        grid=grid,
        in_specs=[raw, table, table, narrow] + [pl.BlockSpec(memory_space=pl.ANY)] * len(after),
        out_specs=pl.BlockSpec((SEQ_LEN, 3 * wide), lambda s, j: (s, j)),
        scratch_shapes=[
            pltpu.VMEM((span, wide), jnp.bfloat16),
            pltpu.VMEM((wide, span), jnp.bfloat16),
            pltpu.VMEM((span, wide), jnp.bfloat16),
            pltpu.VMEM((span, wide), jnp.float32),
            pltpu.VMEM((span, wide), jnp.float32),
        ],
        compiler_params=pltpu.CompilerParams(vmem_limit_bytes=kernel_vmem),
        cost_estimate=attend_cost(projected, is_local, 2),
    )(projected, *tables, d_attended, *after)


def weight_grad_kernel(choice, starts, total, left_count, *refs):
    lefts = [ref[...] for ref in refs[:left_count]]
    rights, out_ref = refs[left_count:-1], refs[-1]
    for right, which, start, stop in zip(rights, choice, starts, list(starts[1:]) + [total]):
        filled = start + right.shape[1]
        if which is None:
            out_ref[:, start:filled] = right[...]
        else:
            out_ref[:, start:filled] = lax.dot_general(
                lefts[which],
                right[...],
                (((0,), (0,)), ((), ())),
                preferred_element_type=jnp.float32,
            ).astype(jnp.bfloat16)
        if filled < stop:
            out_ref[:, filled:stop] = jnp.zeros((out_ref.shape[0], stop - filled), jnp.bfloat16)


def weight_grads(lefts, rights, choice):
    tokens, features = lefts[0].shape
    block = 256
    starts, total = [], 0
    for right in rights:
        total = padded_width(total)
        starts.append(total)
        total += right.shape[1]
    specs = [pl.BlockSpec((tokens, block), lambda i: (0, i))] * len(lefts)
    for right, which in zip(rights, choice):
        if which is None:
            specs.append(pl.BlockSpec((block, right.shape[1]), lambda i: (i, 0)))
        else:
            specs.append(
                pl.BlockSpec(right.shape, lambda i: (0, 0), pipeline_mode=pl.Buffered(1))
            )
    return pl.pallas_call(
        functools.partial(weight_grad_kernel, choice, tuple(starts), total, len(lefts)),
        out_shape=jax.ShapeDtypeStruct((features, total), jnp.bfloat16),
        grid=(features // block,),
        in_specs=specs,
        out_specs=pl.BlockSpec((block, total), lambda i: (i, 0)),
        compiler_params=pltpu.CompilerParams(vmem_limit_bytes=kernel_vmem),
        cost_estimate=pl.CostEstimate(
            flops=2 * tokens * features * total,
            bytes_accessed=2 * (len(lefts) * tokens * features + (tokens + features) * total),
            transcendentals=0,
        ),
    )(*lefts, *rights)


def product(left, right, contract):
    return lax.dot_general(
        left, right, ((contract[:1], contract[1:]), ((), ())), preferred_element_type=jnp.float32
    )


def forward_layer(residual, weights, tables, is_local):
    w_qkv, w_out, w_inner, w_gate, w_down, gain_pair = weights
    lowered = layer_norm(residual, gain_pair[0]).astype(jnp.bfloat16)
    projected = product(lowered, w_qkv, (1, 0))
    attended = attend_forward(projected, tables, is_local)
    middle = residual + core_total(product(attended, w_out, (1, 1)))
    lowered_two = layer_norm(middle, gain_pair[1]).astype(jnp.bfloat16)
    inner = product(lowered_two, w_inner, (1, 0))
    gate_part = product(lowered_two, w_gate, (1, 0))
    activated = gelu_gate(inner, gate_part).astype(jnp.bfloat16)
    output = middle + core_total(product(activated, w_down, (1, 1)))
    kept = (residual, middle, lowered, lowered_two, projected, attended, inner, gate_part, activated)
    return (output, kept)


def backward_layer(upstream, weights, tables, kept, is_local, begin, after):
    w_qkv, w_out, w_inner, w_gate, w_down, gain_pair = weights
    residual, middle, lowered, lowered_two, projected, attended, inner, gate_part, activated = kept
    up_low = upstream.astype(jnp.bfloat16)
    d_activated = product(up_low, w_down, (1, 0))
    unused, pullback = jax.vjp(gelu_gate, inner, gate_part)
    d_inner, d_gate = [v.astype(jnp.bfloat16) for v in pullback(d_activated)]
    hidden_grads = weight_grads((lowered_two, up_low), (d_inner, d_gate, activated), (0, 0, 1))
    d_normed_two = core_total(
        product(d_inner, w_inner, (1, 1)) + product(d_gate, w_gate, (1, 1))
    )
    unused, pullback = jax.vjp(layer_norm, middle, gain_pair[1])
    d_mid_norm, d_gain_two = pullback(d_normed_two)
    d_middle = upstream + d_mid_norm
    d_branch = d_middle.astype(jnp.bfloat16)
    d_attended = product(d_branch, w_out, (1, 0)).astype(jnp.bfloat16)
    d_attended, hidden_grads = lax.optimization_barrier((d_attended, hidden_grads))
    hidden_begun = begin(hidden_grads)
    d_first = attend_backward(projected, tables, d_attended, is_local, 0)
    d_second = attend_backward(
        projected, tables, d_attended, is_local, 1, after(hidden_begun)
    )
    cut = d_first.shape[1]
    d_normed = core_total(
        product(d_first, w_qkv[:, :cut], (1, 1)) + product(d_second, w_qkv[:, cut:], (1, 1))
    )
    unused, pullback = jax.vjp(layer_norm, residual, gain_pair[0])
    d_in_norm, d_gain_one = pullback(d_normed)
    gains = widen(jnp.stack([d_gain_one, d_gain_two], axis=1)).astype(jnp.bfloat16)
    head_grads = weight_grads(
        (lowered, d_branch), (d_first, d_second, attended, gains), (0, 0, 1, None)
    )
    return (d_middle + d_in_norm, (begin(head_grads), hidden_begun))


def adam_update(weight, moment, square, gradient, step_rate, decay_here):
    moment_new = beta_one * moment + (1.0 - beta_one) * gradient
    square_new = beta_two * square + (1.0 - beta_two) * gradient * gradient
    moment_hat = moment_new / (1.0 - beta_one**STEP)
    square_hat = square_new / (1.0 - beta_two**STEP)
    updated = weight - step_rate * (
        moment_hat / (jnp.sqrt(square_hat) + adam_eps) + decay_here * weight
    )
    return (moment_new, square_new, updated)


def per_device(chips, hidden_in, cotangent, *state):
    masters = state[:5]
    moments = state[5:]
    same = lax.axis_index("core") == lax.axis_index("tensor")

    def chip_sequence(values):
        return jnp.where(same, values, core_swap(values)).astype(jnp.float32)

    def arriving_sequence(values):
        return lax.ppermute(values, every_axis, result_pairs(chips))

    starts = layer_starts(masters)
    hidden = masters[2].shape[3]
    local_tables = rotary_tables(theta_local)
    global_tables = rotary_tables(theta_global)
    packed = [split_packed(pack_shards(masters, layer), starts) for layer in range(2)]
    heads_first = role_swap(packed[0][0], chips)
    hidden_first = swap_after(packed[0][1], heads_first, chips)
    hidden_second = swap_after(packed[1][1], hidden_first, chips)
    heads_second = swap_after(packed[1][0], hidden_second, chips)
    heads_all = gather_quick(heads_first, chips)
    weights = [
        unpack_weights(heads_all, gather_rows(hidden_first, chips), starts, hidden),
        unpack_weights(
            gather_quick(heads_second, chips), gather_rows(hidden_second, chips), starts, hidden
        ),
    ]
    inputs = chip_sequence(hidden_in)
    upstream = chip_sequence(cotangent)
    middle, kept_first = forward_layer(inputs, weights[0], local_tables, True)
    output, kept_second = forward_layer(middle, weights[1], global_tables, False)
    out_arrived = arriving_sequence(output.astype(jnp.bfloat16))
    d_middle, (heads_second, hidden_second) = backward_layer(
        upstream,
        weights[1],
        global_tables,
        kept_second,
        False,
        functools.partial(scatter_rows, chips=chips),
        lambda begun: (out_arrived,),
    )
    final_out = jnp.where(same, output.astype(jnp.bfloat16), out_arrived)
    d_values, begun_first = backward_layer(
        d_middle,
        weights[0],
        local_tables,
        kept_first,
        True,
        functools.partial(quick_begin, chips=chips),
        lambda begun: tuple(other for kept, other, held in begun),
    )
    heads_first, hidden_first = [quick_finish(begun, chips) for begun in begun_first]
    shards_first = role_swap(jnp.concatenate([heads_first, hidden_first], axis=1), chips)
    hidden_second = swap_after(hidden_second, shards_first, chips)
    heads_second = swap_after(heads_second, hidden_second, chips)
    shards_second = jnp.concatenate([heads_second, hidden_second], axis=1)
    grads_first, grads_second = [
        unpack_grads(packed.astype(jnp.float32), starts, hidden)
        for packed in (shards_first, shards_second)
    ]
    d_low = d_values.astype(jnp.bfloat16)
    final_grad = jnp.where(same, d_low, arriving_sequence(d_low)).astype(jnp.float32)
    rates = (rate_qkv, rate_out, rate_inp, rate_down, rate_gain)
    results = [final_out, final_grad]
    for i, rate in enumerate(rates):
        gradient = jnp.stack([grads_first[i], grads_second[i]])
        decay = 0.0 if i == 4 else weight_decay
        results += adam_update(
            masters[i], moments[2 * i], moments[2 * i + 1], gradient, rate, decay
        )
    return tuple(results)


def solution(mesh):
    chips = mesh.shape["dp"] // 2
    fine = Mesh(mesh.devices.reshape(chips, 2, mesh.shape["tensor"]), every_axis)
    dp = ("chip", "core")
    tokens = P(dp, None)
    first = P(None, dp, None, "tensor")
    second = P(None, "tensor", dp)
    gain = P(None, None, dp)
    weights = (first, second, first, second, gain)
    pairs = tuple(s for s in weights for unused in range(2))
    triples = tuple(s for s in weights for unused in range(3))

    def body(*arguments):
        return per_device(chips, *arguments)

    return jax.shard_map(
        body,
        mesh=fine,
        in_specs=(tokens, tokens) + weights + pairs,
        out_specs=(tokens, tokens) + triples,
        check_vma=False,
    )
```

```python
import functools

import jax
import jax.numpy as jnp
from jax import lax
from jax.experimental import pallas as pl
from jax.experimental.pallas import tpu as pltpu
from jax.sharding import Mesh, PartitionSpec as P

HEAD_DIM = 64
HALF_WIN = 64
STEP = 10
SEQ_LEN = 1024


norm_eps = 1e-05
theta_local = 10000.0
theta_global = 160000.0
masked_score = -1e30
beta_one = 0.9
beta_two = 0.98
adam_eps = 1e-06
weight_decay = 1e-05
rate_qkv = 0.03
rate_out = 0.15
rate_inp = 0.03
rate_down = 0.02
rate_gain = 0.5

kernel_vmem = 48 * 1024 * 1024
every_axis = ("chip", "core", "tensor")
chip_axes = ("chip", "tensor")


def swap_pairs(chips):
    pairs = []
    for chip in range(chips):
        for core in range(2):
            for row in range(2):
                pairs.append((chip * 4 + core * 2 + row, chip * 4 + row * 2 + core))
    return pairs


def result_pairs(chips):
    return [(chip * 4 + c * 3, chip * 4 + c * 2 + 1 - c) for chip in range(chips) for c in range(2)]


def role_swap(values, chips):
    return lax.ppermute(values, every_axis, swap_pairs(chips))


def swap_after(values, earlier, chips):
    rows, width = values.shape
    rider = jnp.broadcast_to(earlier[:1, :128], (rows, 128))
    return role_swap(jnp.concatenate([values, rider], axis=1), chips)[:, :width]


def core_swap(values):
    return lax.ppermute(values, "core", [(0, 1), (1, 0)])


def core_total(partial_sum):
    own = partial_sum.astype(jnp.bfloat16)
    return own.astype(jnp.float32) + core_swap(own).astype(jnp.float32)


def layer_norm(values, gain):
    centred = values - jnp.mean(values, axis=-1, keepdims=True)
    spread = jnp.mean(centred * centred, axis=-1, keepdims=True)
    return centred * lax.rsqrt(spread + norm_eps) * gain


def rotary_tables(rotary_base):
    positions = jnp.arange(SEQ_LEN, dtype=jnp.int32)
    inverse = rotary_base ** (-jnp.arange(0, HEAD_DIM, 2, dtype=jnp.float32) / HEAD_DIM)
    angles = positions.astype(jnp.float32)[:, None] * inverse[None, :]
    cosine, sine = jnp.cos(angles), jnp.sin(angles)
    return (
        jnp.concatenate([cosine] * 4, axis=-1),
        jnp.concatenate([-sine, sine, -sine, sine], axis=-1),
    )


def gelu_gate(inner, gate_part):
    return jax.nn.gelu(inner, approximate=False) * gate_part


def group_bits(chips):
    return chips.bit_length() - 1


def bit_swap(values, bit, chips):
    if bit < 0:
        return lax.ppermute(values, "tensor", [(0, 1), (1, 0)])
    return lax.ppermute(values, "chip", [(chip, chip ^ (1 << bit)) for chip in range(chips)])


def own_bit(bit):
    if bit < 0:
        return lax.axis_index("tensor")
    return (lax.axis_index("chip") >> bit) & 1


def gather_bit(values, held, bit, chips):
    place = len([b for b in held if b > bit])
    other = bit_swap(values, bit, chips)
    is_low = own_bit(bit) == 0
    joined = jnp.stack(
        [jnp.where(is_low, values, other), jnp.where(is_low, other, values)], axis=place
    )
    return joined, sorted(held + [bit], reverse=True)


def exchange_bit(values, held, bit, chips):
    place = held.index(bit)
    mine = own_bit(bit)
    kept = lax.dynamic_index_in_dim(values, mine, place, keepdims=False)
    sent = lax.dynamic_index_in_dim(values, 1 - mine, place, keepdims=False)
    return kept, bit_swap(sent, bit, chips), [b for b in held if b != bit]


def add_halves(kept, other):
    return (kept.astype(jnp.float32) + other.astype(jnp.float32)).astype(jnp.bfloat16)


def reduce_bit(values, held, bit, chips):
    kept, other, held = exchange_bit(values, held, bit, chips)
    return add_halves(kept, other), held


def half_columns(values):
    return values.shape[1] // 256 * 128


def gather_quick(shard, chips):
    values, held = shard, []
    cut = half_columns(shard)
    for bit in range(group_bits(chips) - 1, 0, -1):
        values, held = gather_bit(values, held, bit, chips)
    token = corner(values)
    halves = []
    for order, part in (((0, -1), values[..., :cut]), ((-1, 0), values[..., cut:])):
        part_held = held
        for bit in order:
            part, part_held = gather_bit(part, part_held, bit, chips)
        halves.append(part.reshape(-1, part.shape[-1]))
    return jnp.concatenate(halves, axis=1), token


def corner(values):
    return values[(0,) * (values.ndim - 2)][:16, :128]


def quick_scatter(gradient, chips, results):
    held = list(range(group_bits(chips) - 1, -2, -1))
    cut = half_columns(gradient)
    begun = []
    for bit, part in ((-1, gradient[:, :cut]), (0, gradient[:, cut:])):
        values = part.reshape([2] * len(held) + [-1, part.shape[-1]])
        begun.append(exchange_bit(values, held, bit, chips))
    yield tuple(corner(other) for kept, other, held in begun)
    begun = [
        exchange_bit(add_halves(kept, other), held, bit, chips)
        for bit, (kept, other, held) in zip((0, -1), begun)
    ]
    yield tuple(corner(other) for kept, other, held in begun)
    held = begun[0][2]
    values = jnp.concatenate([add_halves(kept, other) for kept, other, unused in begun], axis=-1)
    for bit in range(1, group_bits(chips)):
        kept, other, held = exchange_bit(values, held, bit, chips)
        yield (corner(other),)
        values = add_halves(kept, other)
    results.append(values)


def gather_rows(shard, chips):
    return lax.all_gather(shard, chip_axes, axis=0, tiled=True)


def padded_width(width):
    return -(-width // 128) * 128


def widen(values):
    width = values.shape[1]
    return jnp.pad(values, ((0, 0), (0, padded_width(width) - width)))


def layer_starts(masters):
    heads = masters[0].shape[3]
    step = padded_width(masters[2].shape[3])
    return (0, 3 * heads, 4 * heads, 4 * heads + 128, 4 * heads + 128 + step, 4 * heads + 128 + 2 * step)


def pair_major(values):
    rows, kinds, width = values.shape
    wide = 2 * HEAD_DIM
    return values.reshape(rows, kinds, width // wide, wide).swapaxes(1, 2).reshape(rows, -1)


def kind_major(values):
    rows, wide = values.shape[0], 2 * HEAD_DIM
    return values.reshape(rows, -1, 3, wide).swapaxes(1, 2).reshape(rows, 3, -1)


def pack_shards(masters, layer):
    qkv, out, inp, down, gains = [m[layer].astype(jnp.bfloat16) for m in masters]
    return jnp.concatenate(
        [pair_major(qkv), out.T, widen(gains.T), widen(inp[:, 0]), widen(inp[:, 1]), down.T], axis=1
    )


def split_packed(packed, starts):
    return packed[:, : starts[3]], packed[:, starts[3] :]


def unpack_hidden(packed, starts, hidden):
    step = starts[4] - starts[3]
    last = 2 * step
    return packed[:, :hidden], packed[:, step : step + hidden], packed[:, last : last + hidden]


def unpack_heads(packed, starts):
    return (
        packed[:, : starts[1]],
        packed[:, starts[1] : starts[2]],
        packed[:, starts[2] : starts[2] + 2].T.astype(jnp.float32),
    )


def unpack_grads(packed, starts, hidden):
    inner = packed[:, starts[3] : starts[3] + hidden]
    gate = packed[:, starts[4] : starts[4] + hidden]
    return (
        kind_major(packed[:, : starts[1]]),
        packed[:, starts[1] : starts[2]].T,
        jnp.stack([inner, gate], axis=1),
        packed[:, starts[5] :].T,
        packed[:, starts[2] : starts[2] + 2].T,
    )


def rolled(values):
    lane = lax.broadcasted_iota(jnp.int32, values.shape, 1) % HEAD_DIM
    half = HEAD_DIM // 2
    width = values.shape[1]
    return jnp.where(
        lane < half, pltpu.roll(values, width - half, 1), pltpu.roll(values, half, 1)
    )


def pair_stack(values):
    lane = lax.broadcasted_iota(jnp.int32, values.shape, 1)
    nothing = jnp.zeros_like(values)
    return jnp.concatenate(
        [jnp.where(lane < HEAD_DIM, values, nothing), jnp.where(lane < HEAD_DIM, nothing, values)],
        axis=0,
    )


def pair_unstack(values):
    rows = values.shape[1] // 2
    return jnp.concatenate(
        [values[:HEAD_DIM, :rows], values[HEAD_DIM:, rows:]], axis=0
    ).T


def probability_block(keys_here, stacked, start, is_local, length):
    scores = lax.dot_general(
        keys_here, stacked, (((1,), (1,)), ((), ())), preferred_element_type=jnp.float32
    )
    if is_local:
        rows = stacked.shape[0] // 2
        key_at = start - HALF_WIN + lax.broadcasted_iota(jnp.int32, scores.shape, 0)
        query_at = start + lax.broadcasted_iota(jnp.int32, scores.shape, 1) % rows
        allowed = (jnp.abs(query_at - key_at) <= HALF_WIN) & (key_at >= 0) & (key_at < length)
        scores = jnp.where(allowed, scores, masked_score)
    exponent = jnp.exp(scores - jnp.max(scores, axis=0, keepdims=True))
    return exponent * (1.0 / jnp.sum(exponent, axis=0, keepdims=True))


def attend_kernel(is_local, block, raw_ref, cos_ref, sin_ref, out_ref, keys, values_t):
    length = raw_ref.shape[0]
    pad = HALF_WIN if is_local else 0
    reach = block + 2 * HALF_WIN if is_local else length
    wide = 2 * HEAD_DIM
    raw_keys = raw_ref[:, wide : 2 * wide]
    rotated = (raw_keys * cos_ref[...] + rolled(raw_keys) * sin_ref[...]).astype(jnp.bfloat16)
    if is_local:
        keys[...] = jnp.zeros_like(keys)
        values_t[...] = jnp.zeros_like(values_t)
    keys[pl.ds(pad, length), :] = rotated
    values_t[:, pl.ds(pad, length)] = raw_ref[:, 2 * wide :].astype(jnp.bfloat16).T

    def step(i):
        start = pl.multiple_of(i * block, block)
        at = start if is_local else 0
        part = raw_ref[pl.ds(start, block), :wide]
        here = pl.ds(start, block)
        query = (part * cos_ref[here, :] + rolled(part) * sin_ref[here, :]).astype(
            jnp.bfloat16
        ) * jnp.bfloat16(0.125)
        probability = probability_block(
            keys[pl.ds(at, reach), :], pair_stack(query), start, is_local, length
        )
        mixed = jnp.dot(
            values_t[:, pl.ds(at, reach)],
            probability.astype(jnp.bfloat16),
            preferred_element_type=jnp.float32,
        )
        out_ref[here, :] = pair_unstack(mixed).astype(jnp.bfloat16)

    pl.loop(0, length // block, unroll=2)(step)


def attend_back_kernel(is_local, block, raw_ref, cos_ref, sin_ref, up_ref, *refs):
    out_ref, keys, keys_t, values, d_keys, d_values = refs[-6:]
    length = raw_ref.shape[0]
    pad = HALF_WIN if is_local else 0
    reach = block + 2 * HALF_WIN if is_local else length
    wide = 2 * HEAD_DIM
    raw_keys = raw_ref[:, wide : 2 * wide]
    rotated = (raw_keys * cos_ref[...] + rolled(raw_keys) * sin_ref[...]).astype(jnp.bfloat16)
    if is_local:
        keys[...] = jnp.zeros_like(keys)
        keys_t[...] = jnp.zeros_like(keys_t)
        values[...] = jnp.zeros_like(values)
    keys[pl.ds(pad, length), :] = rotated
    keys_t[:, pl.ds(pad, length)] = (rotated * jnp.bfloat16(0.125)).T
    values[pl.ds(pad, length), :] = raw_ref[:, 2 * wide :].astype(jnp.bfloat16)
    d_keys[...] = jnp.zeros_like(d_keys)
    d_values[...] = jnp.zeros_like(d_values)

    def step(i):
        start = pl.multiple_of(i * block, block)
        at = start if is_local else 0
        here = pl.ds(start, block)
        band = pl.ds(at, reach)
        part = raw_ref[here, :wide]
        query = (part * cos_ref[here, :] + rolled(part) * sin_ref[here, :]).astype(
            jnp.bfloat16
        ) * jnp.bfloat16(0.125)
        stacked = pair_stack(query)
        upstream = pair_stack(up_ref[here, :])
        probability = probability_block(keys[band, :], stacked, start, is_local, length)
        d_values[band, :] += jnp.dot(
            probability.astype(jnp.bfloat16), upstream, preferred_element_type=jnp.float32
        )
        d_probability = lax.dot_general(
            values[band, :], upstream, (((1,), (1,)), ((), ())), preferred_element_type=jnp.float32
        )
        centre = jnp.sum(probability * d_probability, axis=0, keepdims=True)
        d_scores = (probability * (d_probability - centre)).astype(jnp.bfloat16)
        d_keys[band, :] += jnp.dot(d_scores, stacked, preferred_element_type=jnp.float32)
        d_query = pair_unstack(
            jnp.dot(keys_t[:, band], d_scores, preferred_element_type=jnp.float32)
        )
        out_ref[here, :wide] = (
            d_query * cos_ref[here, :] - rolled(d_query) * sin_ref[here, :]
        ).astype(jnp.bfloat16)

    pl.loop(0, length // block, unroll=2)(step)
    d_key = d_keys[pl.ds(pad, length), :]
    out_ref[:, wide : 2 * wide] = (d_key * cos_ref[...] - rolled(d_key) * sin_ref[...]).astype(
        jnp.bfloat16
    )
    out_ref[:, 2 * wide :] = d_values[pl.ds(pad, length), :].astype(jnp.bfloat16)


def attend_specs(projected, part=0, parts=1):
    rows, columns = projected.shape
    wide = 2 * HEAD_DIM
    pairs = columns // (3 * wide) // parts
    skipped = part * pairs
    raw = pl.BlockSpec((SEQ_LEN, 3 * wide), lambda s, j: (s, j + skipped))
    table = pl.BlockSpec((SEQ_LEN, wide), lambda s, j: (0, 0))
    narrow = pl.BlockSpec((SEQ_LEN, wide), lambda s, j: (s, j + skipped))
    return (rows // SEQ_LEN, pairs), raw, table, narrow


def attend_cost(projected, is_local, products):
    rows, columns = projected.shape
    reach = 4 * HALF_WIN if is_local else SEQ_LEN
    pairs = columns // (6 * HEAD_DIM)
    cells = rows * reach * pairs * 2
    return pl.CostEstimate(
        flops=cells * 8 * HEAD_DIM * products,
        bytes_accessed=projected.size * 8,
        transcendentals=cells,
    )


def attend_forward(projected, tables, is_local):
    rows, columns = projected.shape
    wide = 2 * HEAD_DIM
    grid, raw, table, narrow = attend_specs(projected)
    span = SEQ_LEN + 2 * HALF_WIN if is_local else SEQ_LEN
    return pl.pallas_call(
        functools.partial(attend_kernel, is_local, 128),
        out_shape=jax.ShapeDtypeStruct((rows, columns // 3), jnp.bfloat16),
        grid=grid,
        in_specs=[raw, table, table],
        out_specs=narrow,
        scratch_shapes=[
            pltpu.VMEM((span, wide), jnp.bfloat16),
            pltpu.VMEM((wide, span), jnp.bfloat16),
        ],
        compiler_params=pltpu.CompilerParams(vmem_limit_bytes=kernel_vmem),
        cost_estimate=attend_cost(projected, is_local, 2),
    )(projected, *tables)


def attend_backward(projected, tables, d_attended, is_local, part, after=()):
    rows, columns = projected.shape
    wide = 2 * HEAD_DIM
    grid, raw, table, narrow = attend_specs(projected, part, 2)
    span = SEQ_LEN + 2 * HALF_WIN if is_local else SEQ_LEN
    return pl.pallas_call(
        functools.partial(attend_back_kernel, is_local, 128),
        out_shape=jax.ShapeDtypeStruct((rows, columns // 2), jnp.bfloat16),
        grid=grid,
        in_specs=[raw, table, table, narrow] + [pl.BlockSpec(memory_space=pl.ANY)] * len(after),
        out_specs=pl.BlockSpec((SEQ_LEN, 3 * wide), lambda s, j: (s, j)),
        scratch_shapes=[
            pltpu.VMEM((span, wide), jnp.bfloat16),
            pltpu.VMEM((wide, span), jnp.bfloat16),
            pltpu.VMEM((span, wide), jnp.bfloat16),
            pltpu.VMEM((span, wide), jnp.float32),
            pltpu.VMEM((span, wide), jnp.float32),
        ],
        compiler_params=pltpu.CompilerParams(vmem_limit_bytes=kernel_vmem),
        cost_estimate=attend_cost(projected, is_local, 2),
    )(projected, *tables, d_attended, *after)


def weight_grad_kernel(choice, starts, total, left_count, *refs):
    lefts = [ref[...] for ref in refs[:left_count]]
    rights, out_ref = refs[left_count : left_count + len(choice)], refs[-1]
    for right, which, start, stop in zip(rights, choice, starts, list(starts[1:]) + [total]):
        filled = start + right.shape[1]
        if which is None:
            out_ref[:, start:filled] = right[...]
        else:
            out_ref[:, start:filled] = lax.dot_general(
                lefts[which],
                right[...],
                (((0,), (0,)), ((), ())),
                preferred_element_type=jnp.float32,
            ).astype(jnp.bfloat16)
        if filled < stop:
            out_ref[:, filled:stop] = jnp.zeros((out_ref.shape[0], stop - filled), jnp.bfloat16)


def weight_grads(lefts, rights, choice, after=()):
    tokens, features = lefts[0].shape
    block = 256
    starts, total = [], 0
    for right in rights:
        total = padded_width(total)
        starts.append(total)
        total += right.shape[1]
    specs = [pl.BlockSpec((tokens, block), lambda i: (0, i))] * len(lefts)
    for right, which in zip(rights, choice):
        if which is None:
            specs.append(pl.BlockSpec((block, right.shape[1]), lambda i: (i, 0)))
        else:
            specs.append(
                pl.BlockSpec(right.shape, lambda i: (0, 0), pipeline_mode=pl.Buffered(1))
            )
    specs += [pl.BlockSpec(memory_space=pl.ANY)] * len(after)
    return pl.pallas_call(
        functools.partial(weight_grad_kernel, choice, tuple(starts), total, len(lefts)),
        out_shape=jax.ShapeDtypeStruct((features, total), jnp.bfloat16),
        grid=(features // block,),
        in_specs=specs,
        out_specs=pl.BlockSpec((block, total), lambda i: (i, 0)),
        compiler_params=pltpu.CompilerParams(vmem_limit_bytes=kernel_vmem),
        cost_estimate=pl.CostEstimate(
            flops=2 * tokens * features * total,
            bytes_accessed=2 * (len(lefts) * tokens * features + (tokens + features) * total),
            transcendentals=0,
        ),
    )(*lefts, *rights, *after)


def product(left, right, contract):
    return lax.dot_general(
        left, right, ((contract[:1], contract[1:]), ((), ())), preferred_element_type=jnp.float32
    )


def forward_layer(residual, weights, tables, is_local):
    w_qkv, w_out, gain_pair, w_inner, w_gate, w_down = weights
    lowered = layer_norm(residual, gain_pair[0]).astype(jnp.bfloat16)
    projected = product(lowered, w_qkv, (1, 0))
    attended = attend_forward(projected, tables, is_local)
    middle = residual + core_total(product(attended, w_out, (1, 1)))
    lowered_two = layer_norm(middle, gain_pair[1]).astype(jnp.bfloat16)
    inner = product(lowered_two, w_inner, (1, 0))
    gate_part = product(lowered_two, w_gate, (1, 0))
    activated = gelu_gate(inner, gate_part).astype(jnp.bfloat16)
    output = middle + core_total(product(activated, w_down, (1, 1)))
    kept = (residual, middle, lowered, lowered_two, projected, attended, inner, gate_part, activated)
    return (output, kept)


def backward_layer(upstream, weights, tables, kept, is_local, begin, slots):
    w_qkv, w_out, gain_pair, w_inner, w_gate, w_down = weights
    residual, middle, lowered, lowered_two, projected, attended, inner, gate_part, activated = kept
    up_low = upstream.astype(jnp.bfloat16)
    d_activated = product(up_low, w_down, (1, 0))
    unused, pullback = jax.vjp(gelu_gate, inner, gate_part)
    d_inner, d_gate = [v.astype(jnp.bfloat16) for v in pullback(d_activated)]
    hidden_grads = weight_grads(
        (lowered_two, up_low), (d_inner, d_gate, activated), (0, 0, 1), slots[0]()
    )
    d_normed_two = core_total(
        product(d_inner, w_inner, (1, 1)) + product(d_gate, w_gate, (1, 1))
    )
    unused, pullback = jax.vjp(layer_norm, middle, gain_pair[1])
    d_mid_norm, d_gain_two = pullback(d_normed_two)
    d_middle = upstream + d_mid_norm
    d_branch = d_middle.astype(jnp.bfloat16)
    d_attended = product(d_branch, w_out, (1, 0)).astype(jnp.bfloat16)
    d_attended, hidden_grads = lax.optimization_barrier((d_attended, hidden_grads))
    hidden_begun = begin(hidden_grads)
    d_first = attend_backward(projected, tables, d_attended, is_local, 0, slots[1]())
    d_second = attend_backward(
        projected, tables, d_attended, is_local, 1, slots[2]() + next(hidden_begun)
    )
    cut = d_first.shape[1]
    d_normed = core_total(
        product(d_first, w_qkv[:, :cut], (1, 1)) + product(d_second, w_qkv[:, cut:], (1, 1))
    )
    unused, pullback = jax.vjp(layer_norm, residual, gain_pair[0])
    d_in_norm, d_gain_one = pullback(d_normed)
    gains = widen(jnp.stack([d_gain_one, d_gain_two], axis=1)).astype(jnp.bfloat16)
    head_grads = weight_grads(
        (lowered, d_branch),
        (d_first, d_second, attended, gains),
        (0, 0, 1, None),
        slots[3](hidden_begun),
    )
    return (d_middle + d_in_norm, (begin(head_grads), hidden_begun))


def adam_update(weight, moment, square, gradient, step_rate, decay_here):
    moment_new = beta_one * moment + (1.0 - beta_one) * gradient
    square_new = beta_two * square + (1.0 - beta_two) * gradient * gradient
    moment_hat = moment_new / (1.0 - beta_one**STEP)
    square_hat = square_new / (1.0 - beta_two**STEP)
    updated = weight - step_rate * (
        moment_hat / (jnp.sqrt(square_hat) + adam_eps) + decay_here * weight
    )
    return (moment_new, square_new, updated)


def per_device(chips, hidden_in, cotangent, *state):
    masters = state[:5]
    moments = state[5:]
    same = lax.axis_index("core") == lax.axis_index("tensor")

    def chip_sequence(values):
        return jnp.where(same, values, core_swap(values)).astype(jnp.float32)

    def arriving_sequence(values):
        return lax.ppermute(values, every_axis, result_pairs(chips))

    starts = layer_starts(masters)
    hidden = masters[2].shape[3]
    local_tables = rotary_tables(theta_local)
    global_tables = rotary_tables(theta_global)
    packed = [split_packed(pack_shards(masters, layer), starts) for layer in range(2)]
    heads_all, token = gather_quick(role_swap(packed[0][0], chips), chips)
    hidden_both = jnp.concatenate([widen(packed[0][1]), packed[1][1]], axis=1)
    hidden_both = gather_rows(swap_after(hidden_both, token, chips), chips)
    cut = padded_width(packed[0][1].shape[1])
    hidden_first = unpack_hidden(hidden_both[:, :cut], starts, hidden)
    hidden_second = unpack_hidden(hidden_both[:, cut:], starts, hidden)
    inputs = chip_sequence(hidden_in)
    upstream = chip_sequence(cotangent)
    weights = [unpack_heads(heads_all, starts) + hidden_first]
    middle, kept_first = forward_layer(inputs, weights[0], local_tables, True)
    heads_second = swap_after(packed[1][0], kept_first[5], chips)
    heads_second = gather_quick(heads_second, chips)[0]
    weights.append(unpack_heads(heads_second, starts) + hidden_second)
    output, kept_second = forward_layer(middle, weights[1], global_tables, False)
    out_arrived = arriving_sequence(output.astype(jnp.bfloat16))
    results = []

    def begin(gradient):
        results.append([])
        return quick_scatter(gradient, chips, results[-1])

    def none(*unused):
        return ()

    d_middle, (heads_steps, hidden_steps) = backward_layer(
        upstream,
        weights[1],
        global_tables,
        kept_second,
        False,
        begin,
        (none, none, lambda: (corner(out_arrived),), none),
    )
    final_out = jnp.where(same, output.astype(jnp.bfloat16), out_arrived)

    def both():
        return next(hidden_steps) + next(heads_steps)

    d_values, begun_first = backward_layer(
        d_middle,
        weights[0],
        local_tables,
        kept_first,
        True,
        begin,
        (both, both, both, lambda steps: next(heads_steps) + next(steps)),
    )
    for steps in (hidden_steps, heads_steps, begun_first[1], begun_first[0]):
        for unused in steps:
            pass
    hidden_second, heads_second, hidden_first, heads_first = [r[0] for r in results]
    shards_first = role_swap(jnp.concatenate([heads_first, hidden_first], axis=1), chips)
    shards_second = jnp.concatenate([heads_second, hidden_second], axis=1)
    shards_second = role_swap(shards_second, chips)
    grads_first, grads_second = [
        unpack_grads(packed.astype(jnp.float32), starts, hidden)
        for packed in (shards_first, shards_second)
    ]
    d_low = d_values.astype(jnp.bfloat16)
    final_grad = jnp.where(same, d_low, arriving_sequence(d_low)).astype(jnp.float32)
    rates = (rate_qkv, rate_out, rate_inp, rate_down, rate_gain)
    results = [final_out, final_grad]
    for i, rate in enumerate(rates):
        gradient = jnp.stack([grads_first[i], grads_second[i]])
        decay = 0.0 if i == 4 else weight_decay
        results += adam_update(
            masters[i], moments[2 * i], moments[2 * i + 1], gradient, rate, decay
        )
    return tuple(results)


def solution(mesh):
    chips = mesh.shape["dp"] // 2
    fine = Mesh(mesh.devices.reshape(chips, 2, mesh.shape["tensor"]), every_axis)
    dp = ("chip", "core")
    tokens = P(dp, None)
    first = P(None, dp, None, "tensor")
    second = P(None, "tensor", dp)
    gain = P(None, None, dp)
    weights = (first, second, first, second, gain)
    pairs = tuple(s for s in weights for unused in range(2))
    triples = tuple(s for s in weights for unused in range(3))

    def body(*arguments):
        return per_device(chips, *arguments)

    return jax.shard_map(
        body,
        mesh=fine,
        in_specs=(tokens, tokens) + weights + pairs,
        out_specs=(tokens, tokens) + triples,
        check_vma=False,
    )
```

```python
import functools

import jax
import jax.numpy as jnp
from jax import lax
from jax.experimental import pallas as pl
from jax.experimental.pallas import tpu as pltpu
from jax.sharding import Mesh, PartitionSpec as P

HEAD_DIM = 64
HALF_WIN = 64
STEP = 10
SEQ_LEN = 1024


norm_eps = 1e-05
theta_local = 10000.0
theta_global = 160000.0
masked_score = -1e30
beta_one = 0.9
beta_two = 0.98
adam_eps = 1e-06
weight_decay = 1e-05
rate_qkv = 0.03
rate_out = 0.15
rate_inp = 0.03
rate_down = 0.02
rate_gain = 0.5

kernel_vmem = 48 * 1024 * 1024
every_axis = ("chip", "core", "tensor")
chip_axes = ("chip", "tensor")


def swap_pairs(chips):
    pairs = []
    for chip in range(chips):
        for core in range(2):
            for row in range(2):
                pairs.append((chip * 4 + core * 2 + row, chip * 4 + row * 2 + core))
    return pairs


def result_pairs(chips):
    return [(chip * 4 + c * 3, chip * 4 + c * 2 + 1 - c) for chip in range(chips) for c in range(2)]


def role_swap(values, chips):
    return lax.ppermute(values, every_axis, swap_pairs(chips))


def swap_after(values, earlier, chips):
    rows, width = values.shape
    rider = jnp.broadcast_to(earlier[:1, :128], (rows, 128))
    return role_swap(jnp.concatenate([values, rider], axis=1), chips)[:, :width]


def core_swap(values):
    return lax.ppermute(values, "core", [(0, 1), (1, 0)])


def core_total(partial_sum):
    own = partial_sum.astype(jnp.bfloat16)
    return own.astype(jnp.float32) + core_swap(own).astype(jnp.float32)


def layer_norm(values, gain):
    centred = values - jnp.mean(values, axis=-1, keepdims=True)
    spread = jnp.mean(centred * centred, axis=-1, keepdims=True)
    return centred * lax.rsqrt(spread + norm_eps) * gain


def rotary_tables(rotary_base):
    positions = jnp.arange(SEQ_LEN, dtype=jnp.int32)
    inverse = rotary_base ** (-jnp.arange(0, HEAD_DIM, 2, dtype=jnp.float32) / HEAD_DIM)
    angles = positions.astype(jnp.float32)[:, None] * inverse[None, :]
    cosine, sine = jnp.cos(angles), jnp.sin(angles)
    return (
        jnp.concatenate([cosine] * 4, axis=-1),
        jnp.concatenate([-sine, sine, -sine, sine], axis=-1),
    )


def gelu_gate(inner, gate_part):
    return jax.nn.gelu(inner, approximate=False) * gate_part


def group_bits(chips):
    return chips.bit_length() - 1


def bit_swap(values, bit, chips):
    if bit < 0:
        return lax.ppermute(values, "tensor", [(0, 1), (1, 0)])
    return lax.ppermute(values, "chip", [(chip, chip ^ (1 << bit)) for chip in range(chips)])


def own_bit(bit):
    if bit < 0:
        return lax.axis_index("tensor")
    return (lax.axis_index("chip") >> bit) & 1


def gather_bit(values, held, bit, chips):
    place = len([b for b in held if b > bit])
    other = bit_swap(values, bit, chips)
    is_low = own_bit(bit) == 0
    joined = jnp.stack(
        [jnp.where(is_low, values, other), jnp.where(is_low, other, values)], axis=place
    )
    return joined, sorted(held + [bit], reverse=True)


def exchange_bit(values, held, bit, chips):
    place = held.index(bit)
    mine = own_bit(bit)
    kept = lax.dynamic_index_in_dim(values, mine, place, keepdims=False)
    sent = lax.dynamic_index_in_dim(values, 1 - mine, place, keepdims=False)
    return kept, bit_swap(sent, bit, chips), [b for b in held if b != bit]


def add_halves(kept, other):
    return (kept.astype(jnp.float32) + other.astype(jnp.float32)).astype(jnp.bfloat16)


def reduce_bit(values, held, bit, chips):
    kept, other, held = exchange_bit(values, held, bit, chips)
    return add_halves(kept, other), held


def scatter_rows(gradient, chips):
    return lax.psum_scatter(gradient, chip_axes, scatter_dimension=0, tiled=True)


def half_columns(values):
    return values.shape[1] // 256 * 128


def gather_quick(shard, chips):
    values, held = shard, []
    cut = half_columns(shard)
    for bit in range(group_bits(chips) - 1, 0, -1):
        values, held = gather_bit(values, held, bit, chips)
    token = corner(values)
    halves = []
    for order, part in (((0, -1), values[..., :cut]), ((-1, 0), values[..., cut:])):
        part_held = held
        for bit in order:
            part, part_held = gather_bit(part, part_held, bit, chips)
        halves.append(part.reshape(-1, part.shape[-1]))
    return jnp.concatenate(halves, axis=1), token


def corner(values):
    return values[(0,) * (values.ndim - 2)][:16, :128]


def quick_scatter(gradient, chips, results):
    held = list(range(group_bits(chips) - 1, -2, -1))
    cut = half_columns(gradient)
    begun = []
    for bit, part in ((-1, gradient[:, :cut]), (0, gradient[:, cut:])):
        values = part.reshape([2] * len(held) + [-1, part.shape[-1]])
        begun.append(exchange_bit(values, held, bit, chips))
    yield tuple(corner(other) for kept, other, held in begun)
    begun = [
        exchange_bit(add_halves(kept, other), held, bit, chips)
        for bit, (kept, other, held) in zip((0, -1), begun)
    ]
    yield tuple(corner(other) for kept, other, held in begun)
    held = begun[0][2]
    values = jnp.concatenate([add_halves(kept, other) for kept, other, unused in begun], axis=-1)
    for bit in range(1, group_bits(chips)):
        kept, other, held = exchange_bit(values, held, bit, chips)
        yield (corner(other),)
        values = add_halves(kept, other)
    results.append(values)


def gather_rows(shard, chips):
    return lax.all_gather(shard, chip_axes, axis=0, tiled=True)


def padded_width(width):
    return -(-width // 128) * 128


def widen(values):
    width = values.shape[1]
    return jnp.pad(values, ((0, 0), (0, padded_width(width) - width)))


def layer_starts(masters):
    heads = masters[0].shape[3]
    step = padded_width(masters[2].shape[3])
    return (0, 3 * heads, 4 * heads, 4 * heads + 128, 4 * heads + 128 + step, 4 * heads + 128 + 2 * step)


def pair_major(values):
    rows, kinds, width = values.shape
    wide = 2 * HEAD_DIM
    return values.reshape(rows, kinds, width // wide, wide).swapaxes(1, 2).reshape(rows, -1)


def kind_major(values):
    rows, wide = values.shape[0], 2 * HEAD_DIM
    return values.reshape(rows, -1, 3, wide).swapaxes(1, 2).reshape(rows, 3, -1)


def pack_shards(masters, layer):
    qkv, out, inp, down, gains = [m[layer].astype(jnp.bfloat16) for m in masters]
    return jnp.concatenate(
        [pair_major(qkv), out.T, widen(gains.T), widen(inp[:, 0]), widen(inp[:, 1]), down.T], axis=1
    )


def split_packed(packed, starts):
    return packed[:, : starts[3]], packed[:, starts[3] :]


def unpack_hidden(packed, starts, hidden):
    step = starts[4] - starts[3]
    last = 2 * step
    return packed[:, :hidden], packed[:, step : step + hidden], packed[:, last : last + hidden]


def unpack_heads(packed, starts):
    return (
        packed[:, : starts[1]],
        packed[:, starts[1] : starts[2]],
        packed[:, starts[2] : starts[2] + 2].T.astype(jnp.float32),
    )


def unpack_grads(packed, starts, hidden):
    inner = packed[:, starts[3] : starts[3] + hidden]
    gate = packed[:, starts[4] : starts[4] + hidden]
    return (
        kind_major(packed[:, : starts[1]]),
        packed[:, starts[1] : starts[2]].T,
        jnp.stack([inner, gate], axis=1),
        packed[:, starts[5] :].T,
        packed[:, starts[2] : starts[2] + 2].T,
    )


def rolled(values):
    lane = lax.broadcasted_iota(jnp.int32, values.shape, 1) % HEAD_DIM
    half = HEAD_DIM // 2
    width = values.shape[1]
    return jnp.where(
        lane < half, pltpu.roll(values, width - half, 1), pltpu.roll(values, half, 1)
    )


def pair_stack(values):
    lane = lax.broadcasted_iota(jnp.int32, values.shape, 1)
    nothing = jnp.zeros_like(values)
    return jnp.concatenate(
        [jnp.where(lane < HEAD_DIM, values, nothing), jnp.where(lane < HEAD_DIM, nothing, values)],
        axis=0,
    )


def pair_unstack(values):
    rows = values.shape[1] // 2
    return jnp.concatenate(
        [values[:HEAD_DIM, :rows], values[HEAD_DIM:, rows:]], axis=0
    ).T


def probability_block(keys_here, stacked, start, is_local, length):
    scores = lax.dot_general(
        keys_here, stacked, (((1,), (1,)), ((), ())), preferred_element_type=jnp.float32
    )
    if is_local:
        rows = stacked.shape[0] // 2
        key_at = start - HALF_WIN + lax.broadcasted_iota(jnp.int32, scores.shape, 0)
        query_at = start + lax.broadcasted_iota(jnp.int32, scores.shape, 1) % rows
        allowed = (jnp.abs(query_at - key_at) <= HALF_WIN) & (key_at >= 0) & (key_at < length)
        scores = jnp.where(allowed, scores, masked_score)
    exponent = jnp.exp(scores - jnp.max(scores, axis=0, keepdims=True))
    return exponent * (1.0 / jnp.sum(exponent, axis=0, keepdims=True))


def attend_kernel(is_local, block, raw_ref, cos_ref, sin_ref, out_ref, keys, values_t):
    length = raw_ref.shape[0]
    pad = HALF_WIN if is_local else 0
    reach = block + 2 * HALF_WIN if is_local else length
    wide = 2 * HEAD_DIM
    raw_keys = raw_ref[:, wide : 2 * wide]
    rotated = (raw_keys * cos_ref[...] + rolled(raw_keys) * sin_ref[...]).astype(jnp.bfloat16)
    if is_local:
        keys[...] = jnp.zeros_like(keys)
        values_t[...] = jnp.zeros_like(values_t)
    keys[pl.ds(pad, length), :] = rotated
    values_t[:, pl.ds(pad, length)] = raw_ref[:, 2 * wide :].astype(jnp.bfloat16).T

    def step(i):
        start = pl.multiple_of(i * block, block)
        at = start if is_local else 0
        part = raw_ref[pl.ds(start, block), :wide]
        here = pl.ds(start, block)
        query = (part * cos_ref[here, :] + rolled(part) * sin_ref[here, :]).astype(
            jnp.bfloat16
        ) * jnp.bfloat16(0.125)
        probability = probability_block(
            keys[pl.ds(at, reach), :], pair_stack(query), start, is_local, length
        )
        mixed = jnp.dot(
            values_t[:, pl.ds(at, reach)],
            probability.astype(jnp.bfloat16),
            preferred_element_type=jnp.float32,
        )
        out_ref[here, :] = pair_unstack(mixed).astype(jnp.bfloat16)

    pl.loop(0, length // block, unroll=4 if is_local else 2)(step)


def attend_back_kernel(is_local, block, raw_ref, cos_ref, sin_ref, up_ref, *refs):
    out_ref, keys, keys_t, values, d_keys, d_values = refs[-6:]
    length = raw_ref.shape[0]
    pad = HALF_WIN if is_local else 0
    reach = block + 2 * HALF_WIN if is_local else length
    wide = 2 * HEAD_DIM
    raw_keys = raw_ref[:, wide : 2 * wide]
    rotated = (raw_keys * cos_ref[...] + rolled(raw_keys) * sin_ref[...]).astype(jnp.bfloat16)
    if is_local:
        keys[...] = jnp.zeros_like(keys)
        keys_t[...] = jnp.zeros_like(keys_t)
        values[...] = jnp.zeros_like(values)
    keys[pl.ds(pad, length), :] = rotated
    keys_t[:, pl.ds(pad, length)] = (rotated * jnp.bfloat16(0.125)).T
    values[pl.ds(pad, length), :] = raw_ref[:, 2 * wide :].astype(jnp.bfloat16)
    d_keys[...] = jnp.zeros_like(d_keys)
    d_values[...] = jnp.zeros_like(d_values)

    def step(i):
        start = pl.multiple_of(i * block, block)
        at = start if is_local else 0
        here = pl.ds(start, block)
        band = pl.ds(at, reach)
        part = raw_ref[here, :wide]
        query = (part * cos_ref[here, :] + rolled(part) * sin_ref[here, :]).astype(
            jnp.bfloat16
        ) * jnp.bfloat16(0.125)
        stacked = pair_stack(query)
        upstream = pair_stack(up_ref[here, :])
        probability = probability_block(keys[band, :], stacked, start, is_local, length)
        d_values[band, :] += jnp.dot(
            probability.astype(jnp.bfloat16), upstream, preferred_element_type=jnp.float32
        )
        d_probability = lax.dot_general(
            values[band, :], upstream, (((1,), (1,)), ((), ())), preferred_element_type=jnp.float32
        )
        centre = jnp.sum(probability * d_probability, axis=0, keepdims=True)
        d_scores = (probability * (d_probability - centre)).astype(jnp.bfloat16)
        d_keys[band, :] += jnp.dot(d_scores, stacked, preferred_element_type=jnp.float32)
        d_query = pair_unstack(
            jnp.dot(keys_t[:, band], d_scores, preferred_element_type=jnp.float32)
        )
        out_ref[here, :wide] = (
            d_query * cos_ref[here, :] - rolled(d_query) * sin_ref[here, :]
        ).astype(jnp.bfloat16)

    pl.loop(0, length // block, unroll=4 if is_local else 2)(step)
    d_key = d_keys[pl.ds(pad, length), :]
    out_ref[:, wide : 2 * wide] = (d_key * cos_ref[...] - rolled(d_key) * sin_ref[...]).astype(
        jnp.bfloat16
    )
    out_ref[:, 2 * wide :] = d_values[pl.ds(pad, length), :].astype(jnp.bfloat16)


def attend_specs(projected, part=0, parts=1):
    rows, columns = projected.shape
    wide = 2 * HEAD_DIM
    pairs = columns // (3 * wide) // parts
    skipped = part * pairs
    raw = pl.BlockSpec((SEQ_LEN, 3 * wide), lambda s, j: (s, j + skipped))
    table = pl.BlockSpec((SEQ_LEN, wide), lambda s, j: (0, 0))
    narrow = pl.BlockSpec((SEQ_LEN, wide), lambda s, j: (s, j + skipped))
    return (rows // SEQ_LEN, pairs), raw, table, narrow


def attend_cost(projected, is_local, products):
    rows, columns = projected.shape
    reach = 4 * HALF_WIN if is_local else SEQ_LEN
    pairs = columns // (6 * HEAD_DIM)
    cells = rows * reach * pairs * 2
    return pl.CostEstimate(
        flops=cells * 8 * HEAD_DIM * products,
        bytes_accessed=projected.size * 8,
        transcendentals=cells,
    )


def attend_forward(projected, tables, is_local):
    rows, columns = projected.shape
    wide = 2 * HEAD_DIM
    grid, raw, table, narrow = attend_specs(projected)
    span = SEQ_LEN + 2 * HALF_WIN if is_local else SEQ_LEN
    return pl.pallas_call(
        functools.partial(attend_kernel, is_local, 128),
        out_shape=jax.ShapeDtypeStruct((rows, columns // 3), jnp.bfloat16),
        grid=grid,
        in_specs=[raw, table, table],
        out_specs=narrow,
        scratch_shapes=[
            pltpu.VMEM((span, wide), jnp.bfloat16),
            pltpu.VMEM((wide, span), jnp.bfloat16),
        ],
        compiler_params=pltpu.CompilerParams(vmem_limit_bytes=kernel_vmem),
        cost_estimate=attend_cost(projected, is_local, 2),
    )(projected, *tables)


def attend_backward(projected, tables, d_attended, is_local, part, after=()):
    rows, columns = projected.shape
    wide = 2 * HEAD_DIM
    grid, raw, table, narrow = attend_specs(projected, part, 2)
    span = SEQ_LEN + 2 * HALF_WIN if is_local else SEQ_LEN
    return pl.pallas_call(
        functools.partial(attend_back_kernel, is_local, 128),
        out_shape=jax.ShapeDtypeStruct((rows, columns // 2), jnp.bfloat16),
        grid=grid,
        in_specs=[raw, table, table, narrow] + [pl.BlockSpec(memory_space=pl.ANY)] * len(after),
        out_specs=pl.BlockSpec((SEQ_LEN, 3 * wide), lambda s, j: (s, j)),
        scratch_shapes=[
            pltpu.VMEM((span, wide), jnp.bfloat16),
            pltpu.VMEM((wide, span), jnp.bfloat16),
            pltpu.VMEM((span, wide), jnp.bfloat16),
            pltpu.VMEM((span, wide), jnp.float32),
            pltpu.VMEM((span, wide), jnp.float32),
        ],
        compiler_params=pltpu.CompilerParams(vmem_limit_bytes=kernel_vmem),
        cost_estimate=attend_cost(projected, is_local, 2),
    )(projected, *tables, d_attended, *after)


def weight_grad_kernel(choice, starts, total, left_count, *refs):
    lefts = [ref[...] for ref in refs[:left_count]]
    rights, out_ref = refs[left_count : left_count + len(choice)], refs[-1]
    for right, which, start, stop in zip(rights, choice, starts, list(starts[1:]) + [total]):
        filled = start + right.shape[1]
        if which is None:
            out_ref[:, start:filled] = right[...]
        else:
            out_ref[:, start:filled] = lax.dot_general(
                lefts[which],
                right[...],
                (((0,), (0,)), ((), ())),
                preferred_element_type=jnp.float32,
            ).astype(jnp.bfloat16)
        if filled < stop:
            out_ref[:, filled:stop] = jnp.zeros((out_ref.shape[0], stop - filled), jnp.bfloat16)


def weight_grads(lefts, rights, choice, after=()):
    tokens, features = lefts[0].shape
    block = 256
    starts, total = [], 0
    for right in rights:
        total = padded_width(total)
        starts.append(total)
        total += right.shape[1]
    specs = [pl.BlockSpec((tokens, block), lambda i: (0, i))] * len(lefts)
    for right, which in zip(rights, choice):
        if which is None:
            specs.append(pl.BlockSpec((block, right.shape[1]), lambda i: (i, 0)))
        else:
            specs.append(
                pl.BlockSpec(right.shape, lambda i: (0, 0), pipeline_mode=pl.Buffered(1))
            )
    specs += [pl.BlockSpec(memory_space=pl.ANY)] * len(after)
    return pl.pallas_call(
        functools.partial(weight_grad_kernel, choice, tuple(starts), total, len(lefts)),
        out_shape=jax.ShapeDtypeStruct((features, total), jnp.bfloat16),
        grid=(features // block,),
        in_specs=specs,
        out_specs=pl.BlockSpec((block, total), lambda i: (i, 0)),
        compiler_params=pltpu.CompilerParams(vmem_limit_bytes=kernel_vmem),
        cost_estimate=pl.CostEstimate(
            flops=2 * tokens * features * total,
            bytes_accessed=2 * (len(lefts) * tokens * features + (tokens + features) * total),
            transcendentals=0,
        ),
    )(*lefts, *rights, *after)


def product(left, right, contract):
    return lax.dot_general(
        left, right, ((contract[:1], contract[1:]), ((), ())), preferred_element_type=jnp.float32
    )


def forward_layer(residual, weights, tables, is_local):
    w_qkv, w_out, gain_pair, w_inner, w_gate, w_down = weights
    lowered = layer_norm(residual, gain_pair[0]).astype(jnp.bfloat16)
    projected = product(lowered, w_qkv, (1, 0))
    attended = attend_forward(projected, tables, is_local)
    middle = residual + core_total(product(attended, w_out, (1, 1)))
    lowered_two = layer_norm(middle, gain_pair[1]).astype(jnp.bfloat16)
    inner = product(lowered_two, w_inner, (1, 0))
    gate_part = product(lowered_two, w_gate, (1, 0))
    activated = gelu_gate(inner, gate_part).astype(jnp.bfloat16)
    output = middle + core_total(product(activated, w_down, (1, 1)))
    kept = (residual, middle, lowered, lowered_two, projected, attended, inner, gate_part, activated)
    return (output, kept)


def backward_layer(upstream, weights, tables, kept, is_local, begin, slots):
    w_qkv, w_out, gain_pair, w_inner, w_gate, w_down = weights
    residual, middle, lowered, lowered_two, projected, attended, inner, gate_part, activated = kept
    up_low = upstream.astype(jnp.bfloat16)
    d_activated = product(up_low, w_down, (1, 0))
    unused, pullback = jax.vjp(gelu_gate, inner, gate_part)
    d_inner, d_gate = [v.astype(jnp.bfloat16) for v in pullback(d_activated)]
    hidden_grads = weight_grads(
        (lowered_two, up_low), (d_inner, d_gate, activated), (0, 0, 1), slots[0]()
    )
    d_normed_two = core_total(
        product(d_inner, w_inner, (1, 1)) + product(d_gate, w_gate, (1, 1))
    )
    unused, pullback = jax.vjp(layer_norm, middle, gain_pair[1])
    d_mid_norm, d_gain_two = pullback(d_normed_two)
    d_middle = upstream + d_mid_norm
    d_branch = d_middle.astype(jnp.bfloat16)
    d_attended = product(d_branch, w_out, (1, 0)).astype(jnp.bfloat16)
    d_attended, hidden_grads = lax.optimization_barrier((d_attended, hidden_grads))
    hidden_begun = begin(hidden_grads)
    d_first = attend_backward(projected, tables, d_attended, is_local, 0, slots[1]())
    d_second = attend_backward(
        projected, tables, d_attended, is_local, 1, slots[2]()
    )
    cut = d_first.shape[1]
    d_normed = core_total(
        product(d_first, w_qkv[:, :cut], (1, 1)) + product(d_second, w_qkv[:, cut:], (1, 1))
    )
    unused, pullback = jax.vjp(layer_norm, residual, gain_pair[0])
    d_in_norm, d_gain_one = pullback(d_normed)
    gains = widen(jnp.stack([d_gain_one, d_gain_two], axis=1)).astype(jnp.bfloat16)
    head_grads = weight_grads(
        (lowered, d_branch),
        (d_first, d_second, attended, gains),
        (0, 0, 1, None),
        slots[3](hidden_begun),
    )
    return (d_middle + d_in_norm, (begin(head_grads), hidden_begun))


def adam_update(weight, moment, square, gradient, step_rate, decay_here):
    moment_new = beta_one * moment + (1.0 - beta_one) * gradient
    square_new = beta_two * square + (1.0 - beta_two) * gradient * gradient
    moment_hat = moment_new / (1.0 - beta_one**STEP)
    square_hat = square_new / (1.0 - beta_two**STEP)
    updated = weight - step_rate * (
        moment_hat / (jnp.sqrt(square_hat) + adam_eps) + decay_here * weight
    )
    return (moment_new, square_new, updated)


def per_device(chips, hidden_in, cotangent, *state):
    masters = state[:5]
    moments = state[5:]
    same = lax.axis_index("core") == lax.axis_index("tensor")

    def chip_sequence(values):
        return jnp.where(same, values, core_swap(values)).astype(jnp.float32)

    def arriving_sequence(values):
        return lax.ppermute(values, every_axis, result_pairs(chips))

    starts = layer_starts(masters)
    hidden = masters[2].shape[3]
    local_tables = rotary_tables(theta_local)
    global_tables = rotary_tables(theta_global)
    packed = [split_packed(pack_shards(masters, layer), starts) for layer in range(2)]
    heads_all, token = gather_quick(role_swap(packed[0][0], chips), chips)
    hidden_both = jnp.concatenate([widen(packed[0][1]), packed[1][1]], axis=1)
    hidden_both = gather_rows(swap_after(hidden_both, token, chips), chips)
    cut = padded_width(packed[0][1].shape[1])
    hidden_first = unpack_hidden(hidden_both[:, :cut], starts, hidden)
    hidden_second = unpack_hidden(hidden_both[:, cut:], starts, hidden)
    inputs = chip_sequence(hidden_in)
    upstream = chip_sequence(cotangent)
    weights = [unpack_heads(heads_all, starts) + hidden_first]
    middle, kept_first = forward_layer(inputs, weights[0], local_tables, True)
    heads_second = swap_after(packed[1][0], kept_first[5], chips)
    heads_second = gather_quick(heads_second, chips)[0]
    weights.append(unpack_heads(heads_second, starts) + hidden_second)
    output, kept_second = forward_layer(middle, weights[1], global_tables, False)
    out_arrived = arriving_sequence(output.astype(jnp.bfloat16))
    results = []
    by_call = []

    def begin_call(gradient):
        by_call.append((corner(gradient), scatter_rows(gradient, chips)))

    def begin(gradient):
        results.append([])
        return quick_scatter(gradient, chips, results[-1])

    def none(*unused):
        return ()

    d_middle, unused = backward_layer(
        upstream,
        weights[1],
        global_tables,
        kept_second,
        False,
        begin_call,
        (none, none, lambda: (corner(out_arrived),), none),
    )
    final_out = jnp.where(same, output.astype(jnp.bfloat16), out_arrived)
    hidden_second, heads_second = by_call
    d_values, begun_first = backward_layer(
        d_middle,
        weights[0],
        local_tables,
        kept_first,
        True,
        begin,
        (lambda: (heads_second[0],), none, none, next),
    )
    for steps in (begun_first[1], begun_first[0]):
        for unused in steps:
            pass
    hidden_first, heads_first = [r[0] for r in results]
    shards_first = role_swap(jnp.concatenate([heads_first, hidden_first], axis=1), chips)
    hidden_second = swap_after(hidden_second[1], shards_first, chips)
    heads_second = swap_after(heads_second[1], hidden_second, chips)
    shards_second = jnp.concatenate([heads_second, hidden_second], axis=1)
    grads_first, grads_second = [
        unpack_grads(packed.astype(jnp.float32), starts, hidden)
        for packed in (shards_first, shards_second)
    ]
    d_low = d_values.astype(jnp.bfloat16)
    final_grad = jnp.where(same, d_low, arriving_sequence(d_low)).astype(jnp.float32)
    rates = (rate_qkv, rate_out, rate_inp, rate_down, rate_gain)
    results = [final_out, final_grad]
    for i, rate in enumerate(rates):
        gradient = jnp.stack([grads_first[i], grads_second[i]])
        decay = 0.0 if i == 4 else weight_decay
        results += adam_update(
            masters[i], moments[2 * i], moments[2 * i + 1], gradient, rate, decay
        )
    return tuple(results)


def solution(mesh):
    chips = mesh.shape["dp"] // 2
    fine = Mesh(mesh.devices.reshape(chips, 2, mesh.shape["tensor"]), every_axis)
    dp = ("chip", "core")
    tokens = P(dp, None)
    first = P(None, dp, None, "tensor")
    second = P(None, "tensor", dp)
    gain = P(None, None, dp)
    weights = (first, second, first, second, gain)
    pairs = tuple(s for s in weights for unused in range(2))
    triples = tuple(s for s in weights for unused in range(3))

    def body(*arguments):
        return per_device(chips, *arguments)

    return jax.shard_map(
        body,
        mesh=fine,
        in_specs=(tokens, tokens) + weights + pairs,
        out_specs=(tokens, tokens) + triples,
        check_vma=False,
    )
```

```python
import functools

import jax
import jax.numpy as jnp
from jax import lax
from jax.experimental import pallas as pl
from jax.experimental.pallas import tpu as pltpu
from jax.sharding import Mesh, PartitionSpec as P

HEAD_DIM = 64
HALF_WIN = 64
STEP = 10
SEQ_LEN = 1024


norm_eps = 1e-05
theta_local = 10000.0
theta_global = 160000.0
masked_score = -1e30
beta_one = 0.9
beta_two = 0.98
adam_eps = 1e-06
weight_decay = 1e-05
rate_qkv = 0.03
rate_out = 0.15
rate_inp = 0.03
rate_down = 0.02
rate_gain = 0.5

kernel_vmem = 48 * 1024 * 1024
every_axis = ("chip", "core", "tensor")
chip_axes = ("chip", "tensor")


def swap_pairs(chips):
    pairs = []
    for chip in range(chips):
        for core in range(2):
            for row in range(2):
                pairs.append((chip * 4 + core * 2 + row, chip * 4 + row * 2 + core))
    return pairs


def result_pairs(chips):
    return [(chip * 4 + c * 3, chip * 4 + c * 2 + 1 - c) for chip in range(chips) for c in range(2)]


def role_swap(values, chips):
    return lax.ppermute(values, every_axis, swap_pairs(chips))


def swap_after(values, earlier, chips):
    rows, width = values.shape
    rider = jnp.broadcast_to(earlier[:1, :128], (rows, 128))
    return role_swap(jnp.concatenate([values, rider], axis=1), chips)[:, :width]


def core_swap(values):
    return lax.ppermute(values, "core", [(0, 1), (1, 0)])


def core_total(partial_sum):
    own = partial_sum.astype(jnp.bfloat16)
    return own.astype(jnp.float32) + core_swap(own).astype(jnp.float32)


def layer_norm(values, gain):
    centred = values - jnp.mean(values, axis=-1, keepdims=True)
    spread = jnp.mean(centred * centred, axis=-1, keepdims=True)
    return centred * lax.rsqrt(spread + norm_eps) * gain


def rotary_tables(rotary_base):
    positions = jnp.arange(SEQ_LEN, dtype=jnp.int32)
    inverse = rotary_base ** (-jnp.arange(0, HEAD_DIM, 2, dtype=jnp.float32) / HEAD_DIM)
    angles = positions.astype(jnp.float32)[:, None] * inverse[None, :]
    cosine, sine = jnp.cos(angles), jnp.sin(angles)
    return (
        jnp.concatenate([cosine] * 4, axis=-1),
        jnp.concatenate([-sine, sine, -sine, sine], axis=-1),
    )


def gelu_gate(inner, gate_part):
    return jax.nn.gelu(inner, approximate=False) * gate_part


def group_bits(chips):
    return chips.bit_length() - 1


def bit_swap(values, bit, chips):
    if bit < 0:
        return lax.ppermute(values, "tensor", [(0, 1), (1, 0)])
    return lax.ppermute(values, "chip", [(chip, chip ^ (1 << bit)) for chip in range(chips)])


def own_bit(bit):
    if bit < 0:
        return lax.axis_index("tensor")
    return (lax.axis_index("chip") >> bit) & 1


def gather_bit(values, held, bit, chips):
    place = len([b for b in held if b > bit])
    other = bit_swap(values, bit, chips)
    is_low = own_bit(bit) == 0
    joined = jnp.stack(
        [jnp.where(is_low, values, other), jnp.where(is_low, other, values)], axis=place
    )
    return joined, sorted(held + [bit], reverse=True)


def exchange_bit(values, held, bit, chips):
    place = held.index(bit)
    mine = own_bit(bit)
    kept = lax.dynamic_index_in_dim(values, mine, place, keepdims=False)
    sent = lax.dynamic_index_in_dim(values, 1 - mine, place, keepdims=False)
    return kept, bit_swap(sent, bit, chips), [b for b in held if b != bit]


def add_halves(kept, other):
    return (kept.astype(jnp.float32) + other.astype(jnp.float32)).astype(jnp.bfloat16)


def reduce_bit(values, held, bit, chips):
    kept, other, held = exchange_bit(values, held, bit, chips)
    return add_halves(kept, other), held


def scatter_rows(gradient, chips):
    return lax.psum_scatter(gradient, chip_axes, scatter_dimension=0, tiled=True)


def half_columns(values):
    return values.shape[1] * 3 // 7 // 128 * 128


def gather_quick(shard, chips):
    values, held = shard, []
    cut = half_columns(shard)
    for bit in range(group_bits(chips) - 1, 0, -1):
        values, held = gather_bit(values, held, bit, chips)
    token = corner(values)
    halves = []
    for order, part in (((0, -1), values[..., :cut]), ((-1, 0), values[..., cut:])):
        part_held = held
        for bit in order:
            part, part_held = gather_bit(part, part_held, bit, chips)
        halves.append(part.reshape(-1, part.shape[-1]))
    return jnp.concatenate(halves, axis=1), token


def corner(values):
    return values[(0,) * (values.ndim - 2)][:16, :128]


def quick_scatter(gradient, chips, results):
    held = list(range(group_bits(chips) - 1, -2, -1))
    cut = half_columns(gradient)
    begun = []
    for bit, part in ((-1, gradient[:, :cut]), (0, gradient[:, cut:])):
        values = part.reshape([2] * len(held) + [-1, part.shape[-1]])
        begun.append(exchange_bit(values, held, bit, chips))
    yield tuple(corner(other) for kept, other, held in begun)
    begun = [
        exchange_bit(add_halves(kept, other), held, bit, chips)
        for bit, (kept, other, held) in zip((0, -1), begun)
    ]
    yield tuple(corner(other) for kept, other, held in begun)
    held = begun[0][2]
    values = jnp.concatenate([add_halves(kept, other) for kept, other, unused in begun], axis=-1)
    for bit in range(1, group_bits(chips)):
        kept, other, held = exchange_bit(values, held, bit, chips)
        yield (corner(other),)
        values = add_halves(kept, other)
    results.append(values)


def gather_rows(shard, chips):
    return lax.all_gather(shard, chip_axes, axis=0, tiled=True)


def padded_width(width):
    return -(-width // 128) * 128


def widen(values):
    width = values.shape[1]
    return jnp.pad(values, ((0, 0), (0, padded_width(width) - width)))


def layer_starts(masters):
    heads = masters[0].shape[3]
    step = padded_width(masters[2].shape[3])
    return (0, 3 * heads, 4 * heads, 4 * heads + 128, 4 * heads + 128 + step, 4 * heads + 128 + 2 * step)


def pair_major(values):
    rows, kinds, width = values.shape
    wide = 2 * HEAD_DIM
    return values.reshape(rows, kinds, width // wide, wide).swapaxes(1, 2).reshape(rows, -1)


def kind_major(values):
    rows, wide = values.shape[0], 2 * HEAD_DIM
    return values.reshape(rows, -1, 3, wide).swapaxes(1, 2).reshape(rows, 3, -1)


def pack_shards(masters, layer):
    qkv, out, inp, down, gains = [m[layer].astype(jnp.bfloat16) for m in masters]
    return jnp.concatenate(
        [pair_major(qkv), out.T, widen(gains.T), widen(inp[:, 0]), widen(inp[:, 1]), down.T], axis=1
    )


def split_packed(packed, starts):
    return packed[:, : starts[3]], packed[:, starts[3] :]


def unpack_hidden(packed, starts, hidden):
    step = starts[4] - starts[3]
    last = 2 * step
    return packed[:, :hidden], packed[:, step : step + hidden], packed[:, last : last + hidden]


def unpack_heads(packed, starts):
    return (
        packed[:, : starts[1]],
        packed[:, starts[1] : starts[2]],
        packed[:, starts[2] : starts[2] + 2].T.astype(jnp.float32),
    )


def unpack_grads(packed, starts, hidden):
    inner = packed[:, starts[3] : starts[3] + hidden]
    gate = packed[:, starts[4] : starts[4] + hidden]
    return (
        kind_major(packed[:, : starts[1]]),
        packed[:, starts[1] : starts[2]].T,
        jnp.stack([inner, gate], axis=1),
        packed[:, starts[5] :].T,
        packed[:, starts[2] : starts[2] + 2].T,
    )


def rolled(values):
    lane = lax.broadcasted_iota(jnp.int32, values.shape, 1) % HEAD_DIM
    half = HEAD_DIM // 2
    width = values.shape[1]
    return jnp.where(
        lane < half, pltpu.roll(values, width - half, 1), pltpu.roll(values, half, 1)
    )


def pair_stack(values):
    lane = lax.broadcasted_iota(jnp.int32, values.shape, 1)
    nothing = jnp.zeros_like(values)
    return jnp.concatenate(
        [jnp.where(lane < HEAD_DIM, values, nothing), jnp.where(lane < HEAD_DIM, nothing, values)],
        axis=0,
    )


def pair_unstack(values):
    rows = values.shape[1] // 2
    return jnp.concatenate(
        [values[:HEAD_DIM, :rows], values[HEAD_DIM:, rows:]], axis=0
    ).T


def probability_block(keys_here, stacked, start, is_local, length):
    scores = lax.dot_general(
        keys_here, stacked, (((1,), (1,)), ((), ())), preferred_element_type=jnp.float32
    )
    if is_local:
        rows = stacked.shape[0] // 2
        key_at = start - HALF_WIN + lax.broadcasted_iota(jnp.int32, scores.shape, 0)
        query_at = start + lax.broadcasted_iota(jnp.int32, scores.shape, 1) % rows
        allowed = (jnp.abs(query_at - key_at) <= HALF_WIN) & (key_at >= 0) & (key_at < length)
        scores = jnp.where(allowed, scores, masked_score)
    exponent = jnp.exp(scores - jnp.max(scores, axis=0, keepdims=True))
    return exponent * (1.0 / jnp.sum(exponent, axis=0, keepdims=True))


def attend_kernel(is_local, block, raw_ref, cos_ref, sin_ref, out_ref, keys, values_t):
    length = raw_ref.shape[0]
    pad = HALF_WIN if is_local else 0
    reach = block + 2 * HALF_WIN if is_local else length
    wide = 2 * HEAD_DIM
    raw_keys = raw_ref[:, wide : 2 * wide]
    rotated = (raw_keys * cos_ref[...] + rolled(raw_keys) * sin_ref[...]).astype(jnp.bfloat16)
    if is_local:
        keys[...] = jnp.zeros_like(keys)
        values_t[...] = jnp.zeros_like(values_t)
    keys[pl.ds(pad, length), :] = rotated
    values_t[:, pl.ds(pad, length)] = raw_ref[:, 2 * wide :].astype(jnp.bfloat16).T

    def step(i):
        start = pl.multiple_of(i * block, block)
        at = start if is_local else 0
        part = raw_ref[pl.ds(start, block), :wide]
        here = pl.ds(start, block)
        query = (part * cos_ref[here, :] + rolled(part) * sin_ref[here, :]).astype(
            jnp.bfloat16
        ) * jnp.bfloat16(0.125)
        probability = probability_block(
            keys[pl.ds(at, reach), :], pair_stack(query), start, is_local, length
        )
        mixed = jnp.dot(
            values_t[:, pl.ds(at, reach)],
            probability.astype(jnp.bfloat16),
            preferred_element_type=jnp.float32,
        )
        out_ref[here, :] = pair_unstack(mixed).astype(jnp.bfloat16)

    pl.loop(0, length // block, unroll=4 if is_local else 2)(step)


def attend_back_kernel(is_local, block, raw_ref, cos_ref, sin_ref, up_ref, *refs):
    out_ref, keys, keys_t, values, d_keys, d_values = refs[-6:]
    length = raw_ref.shape[0]
    pad = HALF_WIN if is_local else 0
    reach = block + 2 * HALF_WIN if is_local else length
    wide = 2 * HEAD_DIM
    raw_keys = raw_ref[:, wide : 2 * wide]
    rotated = (raw_keys * cos_ref[...] + rolled(raw_keys) * sin_ref[...]).astype(jnp.bfloat16)
    if is_local:
        keys[...] = jnp.zeros_like(keys)
        keys_t[...] = jnp.zeros_like(keys_t)
        values[...] = jnp.zeros_like(values)
    keys[pl.ds(pad, length), :] = rotated
    keys_t[:, pl.ds(pad, length)] = (rotated * jnp.bfloat16(0.125)).T
    values[pl.ds(pad, length), :] = raw_ref[:, 2 * wide :].astype(jnp.bfloat16)
    d_keys[...] = jnp.zeros_like(d_keys)
    d_values[...] = jnp.zeros_like(d_values)

    def step(i):
        start = pl.multiple_of(i * block, block)
        at = start if is_local else 0
        here = pl.ds(start, block)
        band = pl.ds(at, reach)
        part = raw_ref[here, :wide]
        query = (part * cos_ref[here, :] + rolled(part) * sin_ref[here, :]).astype(
            jnp.bfloat16
        ) * jnp.bfloat16(0.125)
        stacked = pair_stack(query)
        upstream = pair_stack(up_ref[here, :])
        probability = probability_block(keys[band, :], stacked, start, is_local, length)
        d_values[band, :] += jnp.dot(
            probability.astype(jnp.bfloat16), upstream, preferred_element_type=jnp.float32
        )
        d_probability = lax.dot_general(
            values[band, :], upstream, (((1,), (1,)), ((), ())), preferred_element_type=jnp.float32
        )
        centre = jnp.sum(probability * d_probability, axis=0, keepdims=True)
        d_scores = (probability * (d_probability - centre)).astype(jnp.bfloat16)
        d_keys[band, :] += jnp.dot(d_scores, stacked, preferred_element_type=jnp.float32)
        d_query = pair_unstack(
            jnp.dot(keys_t[:, band], d_scores, preferred_element_type=jnp.float32)
        )
        out_ref[here, :wide] = (
            d_query * cos_ref[here, :] - rolled(d_query) * sin_ref[here, :]
        ).astype(jnp.bfloat16)

    pl.loop(0, length // block, unroll=4 if is_local else 2)(step)
    d_key = d_keys[pl.ds(pad, length), :]
    out_ref[:, wide : 2 * wide] = (d_key * cos_ref[...] - rolled(d_key) * sin_ref[...]).astype(
        jnp.bfloat16
    )
    out_ref[:, 2 * wide :] = d_values[pl.ds(pad, length), :].astype(jnp.bfloat16)


def attend_specs(projected, part=0, parts=1):
    rows, columns = projected.shape
    wide = 2 * HEAD_DIM
    pairs = columns // (3 * wide) // parts
    skipped = part * pairs
    raw = pl.BlockSpec((SEQ_LEN, 3 * wide), lambda s, j: (s, j + skipped))
    table = pl.BlockSpec((SEQ_LEN, wide), lambda s, j: (0, 0))
    narrow = pl.BlockSpec((SEQ_LEN, wide), lambda s, j: (s, j + skipped))
    return (rows // SEQ_LEN, pairs), raw, table, narrow


def attend_cost(projected, is_local, products):
    rows, columns = projected.shape
    reach = 4 * HALF_WIN if is_local else SEQ_LEN
    pairs = columns // (6 * HEAD_DIM)
    cells = rows * reach * pairs * 2
    return pl.CostEstimate(
        flops=cells * 8 * HEAD_DIM * products,
        bytes_accessed=projected.size * 8,
        transcendentals=cells,
    )


def attend_forward(projected, tables, is_local):
    rows, columns = projected.shape
    wide = 2 * HEAD_DIM
    grid, raw, table, narrow = attend_specs(projected)
    span = SEQ_LEN + 2 * HALF_WIN if is_local else SEQ_LEN
    return pl.pallas_call(
        functools.partial(attend_kernel, is_local, 128),
        out_shape=jax.ShapeDtypeStruct((rows, columns // 3), jnp.bfloat16),
        grid=grid,
        in_specs=[raw, table, table],
        out_specs=narrow,
        scratch_shapes=[
            pltpu.VMEM((span, wide), jnp.bfloat16),
            pltpu.VMEM((wide, span), jnp.bfloat16),
        ],
        compiler_params=pltpu.CompilerParams(vmem_limit_bytes=kernel_vmem),
        cost_estimate=attend_cost(projected, is_local, 2),
    )(projected, *tables)


def attend_backward(projected, tables, d_attended, is_local, part, after=()):
    rows, columns = projected.shape
    wide = 2 * HEAD_DIM
    grid, raw, table, narrow = attend_specs(projected, part, 2)
    span = SEQ_LEN + 2 * HALF_WIN if is_local else SEQ_LEN
    return pl.pallas_call(
        functools.partial(attend_back_kernel, is_local, 128),
        out_shape=jax.ShapeDtypeStruct((rows, columns // 2), jnp.bfloat16),
        grid=grid,
        in_specs=[raw, table, table, narrow] + [pl.BlockSpec(memory_space=pl.ANY)] * len(after),
        out_specs=pl.BlockSpec((SEQ_LEN, 3 * wide), lambda s, j: (s, j)),
        scratch_shapes=[
            pltpu.VMEM((span, wide), jnp.bfloat16),
            pltpu.VMEM((wide, span), jnp.bfloat16),
            pltpu.VMEM((span, wide), jnp.bfloat16),
            pltpu.VMEM((span, wide), jnp.float32),
            pltpu.VMEM((span, wide), jnp.float32),
        ],
        compiler_params=pltpu.CompilerParams(vmem_limit_bytes=kernel_vmem),
        cost_estimate=attend_cost(projected, is_local, 2),
    )(projected, *tables, d_attended, *after)


def weight_grad_kernel(choice, starts, total, left_count, *refs):
    lefts = [ref[...] for ref in refs[:left_count]]
    rights, out_ref = refs[left_count : left_count + len(choice)], refs[-1]
    for right, which, start, stop in zip(rights, choice, starts, list(starts[1:]) + [total]):
        filled = start + right.shape[1]
        if which is None:
            out_ref[:, start:filled] = right[...]
        else:
            out_ref[:, start:filled] = lax.dot_general(
                lefts[which],
                right[...],
                (((0,), (0,)), ((), ())),
                preferred_element_type=jnp.float32,
            ).astype(jnp.bfloat16)
        if filled < stop:
            out_ref[:, filled:stop] = jnp.zeros((out_ref.shape[0], stop - filled), jnp.bfloat16)


def weight_grads(lefts, rights, choice, after=()):
    tokens, features = lefts[0].shape
    block = 256
    starts, total = [], 0
    for right in rights:
        total = padded_width(total)
        starts.append(total)
        total += right.shape[1]
    specs = [pl.BlockSpec((tokens, block), lambda i: (0, i))] * len(lefts)
    for right, which in zip(rights, choice):
        if which is None:
            specs.append(pl.BlockSpec((block, right.shape[1]), lambda i: (i, 0)))
        else:
            specs.append(
                pl.BlockSpec(right.shape, lambda i: (0, 0), pipeline_mode=pl.Buffered(1))
            )
    specs += [pl.BlockSpec(memory_space=pl.ANY)] * len(after)
    return pl.pallas_call(
        functools.partial(weight_grad_kernel, choice, tuple(starts), total, len(lefts)),
        out_shape=jax.ShapeDtypeStruct((features, total), jnp.bfloat16),
        grid=(features // block,),
        in_specs=specs,
        out_specs=pl.BlockSpec((block, total), lambda i: (i, 0)),
        compiler_params=pltpu.CompilerParams(vmem_limit_bytes=kernel_vmem),
        cost_estimate=pl.CostEstimate(
            flops=2 * tokens * features * total,
            bytes_accessed=2 * (len(lefts) * tokens * features + (tokens + features) * total),
            transcendentals=0,
        ),
    )(*lefts, *rights, *after)


def product(left, right, contract):
    return lax.dot_general(
        left, right, ((contract[:1], contract[1:]), ((), ())), preferred_element_type=jnp.float32
    )


def forward_layer(residual, weights, tables, is_local):
    w_qkv, w_out, gain_pair, w_inner, w_gate, w_down = weights
    lowered = layer_norm(residual, gain_pair[0]).astype(jnp.bfloat16)
    projected = product(lowered, w_qkv, (1, 0))
    attended = attend_forward(projected, tables, is_local)
    middle = residual + core_total(product(attended, w_out, (1, 1)))
    lowered_two = layer_norm(middle, gain_pair[1]).astype(jnp.bfloat16)
    inner = product(lowered_two, w_inner, (1, 0))
    gate_part = product(lowered_two, w_gate, (1, 0))
    activated = gelu_gate(inner, gate_part).astype(jnp.bfloat16)
    output = middle + core_total(product(activated, w_down, (1, 1)))
    kept = (residual, middle, lowered, lowered_two, projected, attended, inner, gate_part, activated)
    return (output, kept)


def backward_layer(upstream, weights, tables, kept, is_local, begin, slots, extra=()):
    w_qkv, w_out, gain_pair, w_inner, w_gate, w_down = weights
    residual, middle, lowered, lowered_two, projected, attended, inner, gate_part, activated = kept
    up_low = upstream.astype(jnp.bfloat16)
    d_activated = product(up_low, w_down, (1, 0))
    unused, pullback = jax.vjp(gelu_gate, inner, gate_part)
    d_inner, d_gate = [v.astype(jnp.bfloat16) for v in pullback(d_activated)]
    hidden_grads = weight_grads(
        (lowered_two, up_low), (d_inner, d_gate, activated), (0, 0, 1), slots[0]()
    )
    d_normed_two = core_total(
        product(d_inner, w_inner, (1, 1)) + product(d_gate, w_gate, (1, 1))
    )
    unused, pullback = jax.vjp(layer_norm, middle, gain_pair[1])
    d_mid_norm, d_gain_two = pullback(d_normed_two)
    d_middle = upstream + d_mid_norm
    d_branch = d_middle.astype(jnp.bfloat16)
    d_attended = product(d_branch, w_out, (1, 0)).astype(jnp.bfloat16)
    d_attended, hidden_grads = lax.optimization_barrier((d_attended, hidden_grads))
    hidden_begun = begin(hidden_grads)
    d_first = attend_backward(projected, tables, d_attended, is_local, 0, slots[1]())
    d_second = attend_backward(
        projected, tables, d_attended, is_local, 1, slots[2]()
    )
    cut = d_first.shape[1]
    d_normed = core_total(
        product(d_first, w_qkv[:, :cut], (1, 1)) + product(d_second, w_qkv[:, cut:], (1, 1))
    )
    unused, pullback = jax.vjp(layer_norm, residual, gain_pair[0])
    d_in_norm, d_gain_one = pullback(d_normed)
    gains = widen(jnp.stack([d_gain_one, d_gain_two], axis=1)).astype(jnp.bfloat16)
    head_grads = weight_grads(
        (lowered, d_branch),
        (d_first, d_second, attended, gains) + extra,
        (0, 0, 1, None) + (None,) * len(extra),
        slots[3](),
    )
    return (d_middle + d_in_norm, (begin(head_grads), hidden_begun))


def adam_update(weight, moment, square, gradient, step_rate, decay_here):
    moment_new = beta_one * moment + (1.0 - beta_one) * gradient
    square_new = beta_two * square + (1.0 - beta_two) * gradient * gradient
    moment_hat = moment_new / (1.0 - beta_one**STEP)
    square_hat = square_new / (1.0 - beta_two**STEP)
    updated = weight - step_rate * (
        moment_hat / (jnp.sqrt(square_hat) + adam_eps) + decay_here * weight
    )
    return (moment_new, square_new, updated)


def per_device(chips, hidden_in, cotangent, *state):
    masters = state[:5]
    moments = state[5:]
    same = lax.axis_index("core") == lax.axis_index("tensor")

    def chip_sequence(values):
        return jnp.where(same, values, core_swap(values)).astype(jnp.float32)

    def arriving_sequence(values):
        return lax.ppermute(values, every_axis, result_pairs(chips))

    starts = layer_starts(masters)
    hidden = masters[2].shape[3]
    local_tables = rotary_tables(theta_local)
    global_tables = rotary_tables(theta_global)
    packed = [split_packed(pack_shards(masters, layer), starts) for layer in range(2)]
    heads_all, token = gather_quick(role_swap(packed[0][0], chips), chips)
    hidden_both = jnp.concatenate([widen(packed[0][1]), packed[1][1]], axis=1)
    hidden_both = gather_rows(swap_after(hidden_both, token, chips), chips)
    cut = padded_width(packed[0][1].shape[1])
    hidden_first = unpack_hidden(hidden_both[:, :cut], starts, hidden)
    hidden_second = unpack_hidden(hidden_both[:, cut:], starts, hidden)
    inputs = chip_sequence(hidden_in)
    upstream = chip_sequence(cotangent)
    weights = [unpack_heads(heads_all, starts) + hidden_first]
    middle, kept_first = forward_layer(inputs, weights[0], local_tables, True)
    heads_second = swap_after(packed[1][0], kept_first[5], chips)
    heads_second = gather_quick(heads_second, chips)[0]
    weights.append(unpack_heads(heads_second, starts) + hidden_second)
    output, kept_second = forward_layer(middle, weights[1], global_tables, False)
    out_arrived = arriving_sequence(output.astype(jnp.bfloat16))
    results = []
    seconds = []

    def begin_second(gradient):
        seconds.append(gradient)

    def begin(gradient):
        results.append([])
        return quick_scatter(gradient, chips, results[-1])

    def none(*unused):
        return ()

    d_middle, unused = backward_layer(
        upstream,
        weights[1],
        global_tables,
        kept_second,
        False,
        begin_second,
        (none, none, lambda: (corner(out_arrived),), none),
    )
    final_out = jnp.where(same, output.astype(jnp.bfloat16), out_arrived)
    hidden_second = scatter_rows(seconds[0], chips)
    heads_second = seconds[1]

    def reduced():
        return (corner(hidden_second),)

    d_values, (heads_steps, hidden_steps) = backward_layer(
        d_middle,
        weights[0],
        local_tables,
        kept_first,
        True,
        begin,
        (lambda: (corner(heads_second),), reduced, reduced, none),
        (heads_second,),
    )
    for steps in (hidden_steps, heads_steps):
        for unused in steps:
            pass
    hidden_first, heads_both = [r[0] for r in results]
    shards = role_swap(jnp.concatenate([heads_both, hidden_first], axis=1), chips)
    hidden_second = swap_after(hidden_second, d_values.astype(jnp.bfloat16), chips)
    cut = heads_second.shape[1]
    shards_first = jnp.concatenate([shards[:, :cut], shards[:, 2 * cut :]], axis=1)
    shards_second = jnp.concatenate([shards[:, cut : 2 * cut], hidden_second], axis=1)
    grads_first, grads_second = [
        unpack_grads(packed.astype(jnp.float32), starts, hidden)
        for packed in (shards_first, shards_second)
    ]
    d_low = d_values.astype(jnp.bfloat16)
    final_grad = jnp.where(same, d_low, arriving_sequence(d_low)).astype(jnp.float32)
    rates = (rate_qkv, rate_out, rate_inp, rate_down, rate_gain)
    results = [final_out, final_grad]
    for i, rate in enumerate(rates):
        gradient = jnp.stack([grads_first[i], grads_second[i]])
        decay = 0.0 if i == 4 else weight_decay
        results += adam_update(
            masters[i], moments[2 * i], moments[2 * i + 1], gradient, rate, decay
        )
    return tuple(results)


def solution(mesh):
    chips = mesh.shape["dp"] // 2
    fine = Mesh(mesh.devices.reshape(chips, 2, mesh.shape["tensor"]), every_axis)
    dp = ("chip", "core")
    tokens = P(dp, None)
    first = P(None, dp, None, "tensor")
    second = P(None, "tensor", dp)
    gain = P(None, None, dp)
    weights = (first, second, first, second, gain)
    pairs = tuple(s for s in weights for unused in range(2))
    triples = tuple(s for s in weights for unused in range(3))

    def body(*arguments):
        return per_device(chips, *arguments)

    return jax.shard_map(
        body,
        mesh=fine,
        in_specs=(tokens, tokens) + weights + pairs,
        out_specs=(tokens, tokens) + triples,
        check_vma=False,
    )
```
